512 devices in a mesh: coil: 16 (over z), slab: 2 (over y_hi), row: 16 (over y_lo, x, core).
Axes of the slice: x: 4, y: 4 (y_hi: 2, y_lo: 2; y = y_hi * 2 + y_lo), z: 16, core: 2. Of those that a mesh axis runs over, the one named last changes fastest.
Arguments:
- kspace: float32 [32, 4, 320, 640], P('coil', 'slab', 'row'), may hold values from -6 to 6
- cotangent: float32 [32, 4, 320, 640], P('coil', 'slab', 'row'), may hold values from -6 to 6
- sens: float32 [32, 4, 320, 640], P('coil', 'slab', 'row'), may hold values from -0.75 to 0.75
- mask: int32 [4, 320], P('slab', 'row'), may hold values 0 or 1
- eta: float32 [1], replicated, may hold values from 0.5 to 1.5
- w_first: float32 [18, 2, 3, 3, 3], replicated, may hold values from -0.875 to 0.875
- w_last: float32 [2, 18], replicated, may hold values from -1.5 to 1.5
Outputs:
- grad_kspace: float32 [32, 4, 320, 640], P('coil', 'slab', 'row')
- grad_sens: float32 [32, 4, 320, 640], P('coil', 'slab', 'row')
The draws below stay inside these ranges and needn't reach their ends.
All inputs are finite; a program needn't handle non-finite values. No bound on the sum of `mask` on one device may be relied on, other than what follows from the above.
Results may differ from the reference program's by a relative error of at most 0.00011.
Values sent between devices are 32-bit elements; how exact they have to be, the bound alone decides.
A program may use at most 64 MiB of HBM per device.

```python
import jax
import jax.numpy as jnp
from jax import lax

COILS = 32
ROWS = 320
COLS = 320
HID = 18
PLANES = 4


def set_ends(values, stream_key, least, high):
    place = [jax.random.randint(jax.random.fold_in(stream_key, axis), (), 0, length) for axis, length in enumerate(values.shape)]
    widest = values.shape.index(max(values.shape))
    neighbour = place[:widest] + [(place[widest] + 1) % values.shape[widest]] + place[widest + 1:]
    return values.at[tuple(place)].set(least).at[tuple(neighbour)].set(high)


def level_of(key, dims, cuts, least, largest):
    def one(position, shards_of):
        steps = jax.random.uniform(jax.random.fold_in(jax.random.fold_in(key, 6), position), (shards_of,), jnp.float32, least / len(cuts), largest / len(cuts))
        return jnp.repeat(jnp.exp(steps), dims[position] // shards_of).reshape((-1,) + (1,) * (len(dims) - position - 1))

    loudness = one(*cuts[0])
    for cut in cuts[1:]:
        loudness = loudness * one(*cut)
    return loudness


def gaussian(key, dims, scale, bound, shards=(), dtype=jnp.bfloat16):
    result = jax.random.normal(key, dims, jnp.float32) * scale
    if len(shards) > 0:
        result = level_of(key, dims, shards, -0.22, 0.18) * result
    return jnp.clip(result, min=-bound, max=bound).astype(dtype)


def setup_inputs(seed: int = 0) -> dict:
    arg_keys = jax.random.split(jax.random.key(seed), 8)
    return {
        "kspace": gaussian(arg_keys[0], (COILS, PLANES, ROWS, 2 * COLS), 1.0, 6.0, ((0, 16), (1, 2), (2, 16)), jnp.float32),
        "cotangent": gaussian(arg_keys[1], (COILS, PLANES, ROWS, 2 * COLS), 1.0, 6.0, ((0, 16), (1, 2), (2, 16)), jnp.float32),
        "sens": gaussian(arg_keys[2], (COILS, PLANES, COLS, 2 * ROWS), 0.125, 0.75, ((0, 16), (1, 2), (2, 16)), jnp.float32),
        "mask": set_ends((jax.random.randint(arg_keys[3], (PLANES, ROWS), 0, 3) < 1).astype(jnp.int32), jax.random.fold_in(arg_keys[3], 1), 0, 1),
        "eta": jnp.clip(jax.random.uniform(arg_keys[4], (1,), jnp.float32, 0.5, 1.5), 0.5, 1.5),
        "w_first": gaussian(arg_keys[5], (HID, 2, 3, 3, 3), 54 ** -0.5, 0.875, (), jnp.float32),
        "w_last": gaussian(arg_keys[6], (2, HID), HID ** -0.5, 1.5, (), jnp.float32),
    }


def network(field, w_first, w_last):
    pre_act = lax.conv_general_dilated(field[None], w_first, (1, 1, 1), [(1, 1), (1, 1), (1, 1)], dimension_numbers=('NCDHW', 'OIDHW', 'NCDHW'), precision=lax.Precision.HIGHEST)[0]
    return jnp.einsum('co,opuy->cpuy', w_last, jax.nn.silu(pre_act), precision=lax.Precision.HIGHEST)

def to_complex(array, half):
    return lax.complex(array[..., :half], array[..., half:])

def to_pair(values):
    return jnp.concatenate([jnp.real(values), jnp.imag(values)], axis=-1)

def reference(kspace, cotangent, sens, mask, eta, w_first, w_last):
    k_complex = to_complex(kspace, COLS)
    g_complex = to_complex(cotangent, COLS)
    s_complex = to_complex(sens, ROWS)
    image_input = jnp.swapaxes(jnp.fft.ifft2(k_complex, axes=(2, 3), norm='ortho'), 2, 3)
    image_cot = jnp.swapaxes(jnp.fft.ifft2(g_complex, axes=(2, 3), norm='ortho'), 2, 3)
    image_sum = lax.optimization_barrier(jnp.sum(jnp.conj(s_complex) * image_input, axis=0))
    cot_sum = lax.optimization_barrier(jnp.sum(jnp.conj(s_complex) * image_cot, axis=0))
    field = jnp.stack([jnp.real(image_sum), jnp.imag(image_sum)], axis=0)
    cot_field = jnp.stack([jnp.real(cot_sum), jnp.imag(cot_sum)], axis=0)
    refined, pullback = jax.vjp(lambda values: network(values, w_first, w_last), field)
    back_field = pullback(cot_field)[0]
    refined_c = lax.complex(refined[0], refined[1])
    back_c = lax.complex(back_field[0], back_field[1])
    model_k = jnp.fft.fft2(jnp.swapaxes(s_complex * back_c[None], 2, 3), axes=(2, 3), norm='ortho')
    factor = 1.0 - eta[0] * mask.astype(jnp.float32)[None, :, :, None]
    grad_kspace = to_pair(factor * g_complex - model_k)
    grad_sens = to_pair(-(image_cot * jnp.conj(refined_c) + image_input * jnp.conj(back_c)))
    return (grad_kspace, grad_sens)
```

```python
import math

import jax
import jax.numpy as jnp
import ml_dtypes
import numpy as np
from jax import lax
from jax.experimental import pallas as pl
from jax.experimental.pallas import tpu as pltpu
from jax.sharding import PartitionSpec as P

MESH = pl.DeviceIdType.MESH
LEN = 320
HALF = 384
WIDE = 2 * HALF
CELLS = 20
GROUP = 32
PEERS = 16
COIL_PEERS = 16
SENT = 2 * CELLS
OWNERS = 10
HID = 18


def owner_coil(owner):
    return (8 * owner) // 5


def coil_owner(coil):
    return (5 * coil + 7) // 8


def split_table(table):
    high = table.astype(ml_dtypes.bfloat16)
    low = (table - high.astype(np.float64)).astype(ml_dtypes.bfloat16)
    return high, low


def tables():
    at = np.arange(LEN)
    angle = 2.0 * math.pi * ((at[:, None] * at[None, :]) % LEN) / LEN
    cosine, sine = np.cos(angle) / math.sqrt(LEN), np.sin(angle) / math.sqrt(LEN)
    mix = np.zeros((2, LEN, 2, LEN))
    mix[0, :, 0], mix[0, :, 1], mix[1, :, 0], mix[1, :, 1] = cosine, -sine, sine, cosine
    first = np.zeros((PEERS, 2, CELLS, 2, HALF))
    first[..., :LEN] = mix.reshape(2, PEERS, CELLS, 2, LEN).transpose(1, 0, 2, 3, 4)
    second = np.zeros((2, PEERS, GROUP, 2, HALF))
    second[:, :, :CELLS, :, :LEN] = mix.transpose(2, 3, 0, 1).reshape(2, PEERS, CELLS, 2, LEN)
    return split_table(first.reshape(PEERS * SENT, WIDE)) + split_table(
        second.reshape(2 * PEERS * GROUP, WIDE)
    )


def selectors():
    repeat = np.zeros((HID * 4, HID), np.float32)
    for unit in range(HID):
        repeat[4 * unit : 4 * unit + 4, unit] = 1.0
    pick = np.zeros((3, 54, 144), np.float32)
    place = np.zeros((3, HID * 4, 144), np.float32)
    for column in range(144):
        e3, channel, e1, row = column // 48, column // 24 % 2, column // 8 % 3, column % 8
        for e2 in range(3):
            pick[e2, channel * 27 + e1 * 9 + e2 * 3 + e3, column] = 1.0
            for line in range(HID * 4):
                if row - line % 4 == e2:
                    place[e2, line, column] = 1.0
    repeat_back = np.concatenate([repeat] * 3, axis=0)
    pick_back = np.zeros((9, 16, 54), np.float32)
    place_back = np.zeros((9, 16, 216), np.float32)
    for plane in range(3):
        for e2 in range(3):
            for line in range(12):
                e3, channel, row = line // 4, line // 2 % 2, line % 2
                pick_back[plane * 3 + e2, line, channel * 27 + (2 - plane) * 9 + e2 * 3 + e3] = 1.0
                for column in range(216):
                    if column // 72 == plane and row + 2 - column % 4 == e2:
                        place_back[plane * 3 + e2, line, column] = 1.0
    place_last = np.zeros((8, HID * 4), np.float32)
    pick_last = np.zeros((8, 2), np.float32)
    for line in range(4):
        pick_last[line, line // 2] = 1.0
        for column in range(HID * 4):
            if column % 4 == line % 2 + 1:
                place_last[line, column] = 1.0
    return (
        repeat,
        pick,
        place,
        repeat_back,
        pick_back.reshape(144, 54),
        place_back.reshape(144, 216),
        place_last,
        pick_last,
    )


def split(values):
    high = values.astype(jnp.bfloat16)
    return high, (values - high.astype(jnp.float32)).astype(jnp.bfloat16)


def dot(left, right, dims=((1,), (0,))):
    return lax.dot_general(left, right, (dims, ((), ())), preferred_element_type=jnp.float32)


def dot3(left, right):
    left_high, left_low = split(left)
    right_high, right_low = split(right)
    return dot(left_high, right_high) + dot(left_low, right_high) + dot(left_high, right_low)


def exact_dot(left, right, dims=((1,), (0,))):
    return lax.dot_general(
        left,
        right,
        (dims, ((), ())),
        precision=lax.Precision.HIGHEST,
        preferred_element_type=jnp.float32,
    )


def kernel(
    kspace,
    cotangent,
    sens,
    mask,
    eta,
    w_first,
    w_last,
    first_high_hbm,
    first_low_hbm,
    second_high_hbm,
    second_low_hbm,
    repeat,
    pick,
    place,
    repeat_back,
    pick_back,
    place_back,
    place_last,
    pick_last,
    grad_kspace,
    grad_sens,
    first_high,
    first_low,
    second_high,
    second_low,
    lines,
    spread,
    landed,
    wide,
    images,
    maps,
    parts,
    sums,
    near,
    shifted,
    cot_rows,
    acts,
    hidden,
    pieces,
    fields,
    table_sem,
    swap_send,
    swap_recv,
    sum_send,
    sum_recv,
    near_send,
    near_recv,
    field_send,
    field_recv,
):
    coil, slab, row = lax.axis_index("coil"), lax.axis_index("slab"), lax.axis_index("row")
    owner = coil_owner(coil)
    owns = owner_coil(owner) == coil

    def neighbour(step):
        other = owner + step
        other_row = row + jnp.where(other < 0, -1, 0) + jnp.where(other >= OWNERS, 1, 0)
        there = jnp.logical_and(other_row >= 0, other_row < PEERS)
        return owner_coil((other + OWNERS) % OWNERS), other_row, there

    near_by = [
        (step, across) for step in (-1, 0, 1) for across in (0, 1) if (step, across) != (0, 0)
    ]

    near[...] = jnp.zeros_like(near)

    barrier = pltpu.get_barrier_semaphore()

    @pl.loop(1, PEERS)
    def _(step):
        pl.semaphore_signal(
            barrier, inc=1, device_id={"row": (row + step) % PEERS}, device_id_type=MESH
        )
        pl.semaphore_signal(
            barrier, inc=1, device_id={"coil": (coil + step) % COIL_PEERS}, device_id_type=MESH
        )

    table_copies = [
        pltpu.make_async_copy(source, target, table_sem.at[place_of])
        for place_of, (source, target) in enumerate(
            (
                (first_high_hbm, first_high),
                (first_low_hbm, first_low),
                (second_high_hbm, second_high),
                (second_low_hbm, second_low),
            )
        )
    ]
    for copy in table_copies:
        copy.start()

    for step, across in near_by:
        other_coil, other_row, there = neighbour(step)

        @pl.when(jnp.logical_and(owns, there))
        def _():
            pl.semaphore_signal(
                barrier,
                inc=1,
                device_id={
                    "coil": other_coil,
                    "slab": (slab + across) % 2,
                    "row": other_row,
                },
                device_id_type=MESH,
            )

    def spread_out(which):
        high, low = split(lines[...])
        both = dot(first_high[...], jnp.concatenate([high, low], axis=0), ((1,), (1,)))
        rest = dot(first_low[...], high, ((1,), (1,)))
        spread[which] = both[:, :128] + both[:, 128:] + rest

    def swap(which, step):
        peer = (row + step) % PEERS
        return pltpu.make_async_remote_copy(
            src_ref=spread.at[which, pl.ds(pl.multiple_of(peer * SENT, 8), SENT)],
            dst_ref=landed.at[which, row],
            send_sem=swap_send.at[which, peer],
            recv_sem=swap_recv.at[which, row],
            device_id={"row": peer},
            device_id_type=MESH,
        )

    def swap_start(which):
        @pl.loop(1, PEERS)
        def _(step):
            swap(which, step).start()

        landed[which, row] = spread[which, pl.ds(pl.multiple_of(row * SENT, 8), SENT), :]

    def swap_wait(which):
        @pl.loop(1, PEERS)
        def _(step):
            peer = (row + step) % PEERS
            pltpu.make_async_remote_copy(
                src_ref=spread.at[which, pl.ds(0, SENT)],
                dst_ref=landed.at[which, peer],
                send_sem=swap_send.at[which, peer],
                recv_sem=swap_recv.at[which, peer],
                device_id={"row": peer},
                device_id_type=MESH,
            ).wait_recv()

    lane = lax.broadcasted_iota(jnp.int32, (CELLS, 128), 1)

    def gather_in(which):
        for part in range(2):
            for four in range(PEERS // 4):
                blocks = [
                    landed[which, 4 * four + inner, part * CELLS : (part + 1) * CELLS, :]
                    for inner in range(4)
                ]
                for group in range(4):
                    tile = None
                    for inner in range(4):
                        turn = (inner - group) % 4 * GROUP
                        moved = pltpu.roll(blocks[inner], turn, 1) if turn else blocks[inner]
                        tile = moved if tile is None else jnp.where(lane >= GROUP * inner, moved, tile)
                    start = part * PEERS * GROUP + four * 128
                    wide[24 * group : 24 * group + CELLS, start : start + 128] = tile
        high, low = split(wide[...])
        both = dot(jnp.concatenate([high, low], axis=0), second_high[...])
        return both[:96] + both[96:] + dot(high, second_low[...])

    lines[...] = jnp.zeros_like(lines)
    for group in range(4):
        lines[GROUP * group : GROUP * group + CELLS, :LEN] = kspace[group // 2, group % 2, :, :LEN]
        lines[GROUP * group : GROUP * group + CELLS, HALF : HALF + LEN] = kspace[
            group // 2, group % 2, :, LEN:
        ]
    table_copies[0].wait()
    table_copies[1].wait()
    spread_out(0)

    near_count = jnp.int32(0)
    for step, across in near_by:
        near_count = near_count + jnp.where(jnp.logical_and(owns, neighbour(step)[2]), 1, 0)
    pl.semaphore_wait(barrier, 2 * (PEERS - 1) + near_count)

    swap_start(0)
    for group in range(4):
        lines[GROUP * group : GROUP * group + CELLS, :LEN] = cotangent[
            group // 2, group % 2, :, :LEN
        ]
        lines[GROUP * group : GROUP * group + CELLS, HALF : HALF + LEN] = cotangent[
            group // 2, group % 2, :, LEN:
        ]
    spread_out(1)
    swap_start(1)

    wide[...] = jnp.zeros_like(wide)
    maps[...] = jnp.zeros_like(maps)
    for group in range(4):
        maps[group, :CELLS, :LEN] = sens[group // 2, group % 2, :, :LEN]
        maps[group, :CELLS, HALF : HALF + LEN] = sens[group // 2, group % 2, :, LEN:]
    weights = w_first[...]
    weights_rows = exact_dot(repeat[...], weights)
    forward_matrix = jnp.zeros((HID * 4, 144), jnp.float32)
    for e2 in range(3):
        forward_matrix += place[e2] * exact_dot(weights_rows, pick[e2])
    weights_back = exact_dot(weights, repeat_back[...], ((0,), (1,)))
    backward_matrix = jnp.sum(
        (exact_dot(pick_back[...], weights_back) * place_back[...]).reshape(9, 16, 216), axis=0
    )
    last_columns = exact_dot(repeat[...], w_last[...], ((1,), (1,)))
    last_matrix = place_last[...] * exact_dot(
        pick_last[...], exact_dot(w_last[...], repeat[...], ((1,), (1,)))
    )

    def part_sums(which, total_field):
        for plane in range(2):
            real = imag = None
            for local_coil in range(2):
                group = local_coil * 2 + plane
                map_real, map_imag = maps[group, :, :HALF], maps[group, :, HALF:]
                field = total_field[24 * group : 24 * group + 24]
                field_real, field_imag = field[:, :HALF], field[:, HALF:]
                this_real = map_real * field_real + map_imag * field_imag
                this_imag = map_real * field_imag - map_imag * field_real
                real = this_real if real is None else real + this_real
                imag = this_imag if imag is None else imag + this_imag
            for target in range(OWNERS):
                cut = slice(2 * target, 2 * target + 2)
                parts[which, target, 2 * plane : 2 * plane + 2, :] = real[cut]
                parts[which, target, 4 + 2 * plane : 6 + 2 * plane, :] = imag[cut]

    def part_copy(which, target):
        return pltpu.make_async_remote_copy(
            src_ref=parts.at[which, target],
            dst_ref=sums.at[which, coil],
            send_sem=sum_send.at[which, target],
            recv_sem=sum_recv.at[which, coil],
            device_id={"coil": owner_coil(target)},
            device_id_type=MESH,
        )

    def part_start(which):
        @pl.loop(0, OWNERS)
        def _(step):
            target = (owner + step) % OWNERS

            @pl.when(owner_coil(target) != coil)
            def _():
                part_copy(which, target).start()

    def part_total(which):
        @pl.loop(1, COIL_PEERS)
        def _(step):
            peer = (coil + step) % COIL_PEERS
            pltpu.make_async_remote_copy(
                src_ref=parts.at[which, 0],
                dst_ref=sums.at[which, peer],
                send_sem=sum_send.at[which, 0],
                recv_sem=sum_recv.at[which, peer],
                device_id={"coil": peer},
                device_id_type=MESH,
            ).wait_recv()

        sums[which, coil] = parts[which, owner]
        total = sums[which, 0]
        for peer in range(1, COIL_PEERS):
            total = total + sums[which, peer]
        return total

    def near_copy(which, step, across):
        other_coil, other_row, there = neighbour(step)
        copy = pltpu.make_async_remote_copy(
            src_ref=near.at[which, 1, slab],
            dst_ref=near.at[which, 1 - step, slab],
            send_sem=near_send.at[which, (step + 1) * 2 + across],
            recv_sem=near_recv.at[which, (1 - step) * 2 + across],
            device_id={"coil": other_coil, "slab": (slab + across) % 2, "row": other_row},
            device_id_type=MESH,
        )
        return copy, there

    def near_start(which):
        for step, across in near_by:
            copy, there = near_copy(which, step, across)
            pl.when(there)(copy.start)

    def near_wait(which):
        for step, across in near_by:
            other_coil, other_row, there = neighbour(step)
            copy = pltpu.make_async_remote_copy(
                src_ref=near.at[which, 1, slab],
                dst_ref=near.at[which, 1 + step, (slab + across) % 2],
                send_sem=near_send.at[which, (step + 1) * 2 + across],
                recv_sem=near_recv.at[which, (1 + step) * 2 + across],
                device_id={"coil": other_coil, "slab": (slab + across) % 2, "row": other_row},
                device_id_type=MESH,
            )
            pl.when(there)(copy.wait_recv)

    def field_copy(which, step):
        peer = (coil + step) % COIL_PEERS
        return pltpu.make_async_remote_copy(
            src_ref=pieces.at[which, owner],
            dst_ref=pieces.at[which, owner],
            send_sem=field_send.at[which, peer],
            recv_sem=field_recv.at[which, owner],
            device_id={"coil": peer},
            device_id_type=MESH,
        )

    def field_start(which):
        @pl.loop(1, COIL_PEERS)
        def _(step):
            field_copy(which, step).start()

    def field_wait(which):
        @pl.loop(0, OWNERS)
        def _(target):
            @pl.when(owner_coil(target) != coil)
            def _():
                pltpu.make_async_remote_copy(
                    src_ref=pieces.at[which, target],
                    dst_ref=pieces.at[which, target],
                    send_sem=field_send.at[which, 0],
                    recv_sem=field_recv.at[which, target],
                    device_id={"coil": owner_coil(target)},
                    device_id_type=MESH,
                ).wait_recv()

        for target in range(OWNERS):
            for part in range(2):
                for plane in range(2):
                    line = part * 4 + plane * 2
                    fields[which, part, plane, 2 * target : 2 * target + 2, :] = pieces[
                        which, target, line : line + 2, :
                    ]

    table_copies[2].wait()
    table_copies[3].wait()
    swap_wait(0)
    total_field = gather_in(0)
    images[0] = total_field
    part_sums(0, total_field)
    part_start(0)
    swap_wait(1)
    total_field = gather_in(1)
    images[1] = total_field
    part_sums(1, total_field)
    part_start(1)

    @pl.when(owns)
    def _():
        near[0, 1, slab] = part_total(0)
        near_start(0)
        near[1, 1, slab] = part_total(1)
        near_start(1)
        shifted[...] = jnp.zeros_like(shifted)
        hidden[0] = jnp.zeros((HID * 4, HALF), jnp.float32)
        hidden[4] = jnp.zeros((HID * 4, HALF), jnp.float32)
        near_wait(0)
        for part in range(2):
            for side in range(2):
                for plane in range(2):
                    line = part * 4 + plane * 2
                    for step in range(3):
                        shifted[1, part, 1 + 2 * side + plane, 2 * step : 2 * step + 2, :] = near[
                            0, step, side, line : line + 2, :
                        ]
        middle = shifted[1].reshape(2 * 6 * 8, HALF)
        shifted[0] = pltpu.roll(middle, 1, 1).reshape(2, 6, 8, HALF)
        shifted[2] = pltpu.roll(middle, HALF - 1, 1).reshape(2, 6, 8, HALF)
        for plane in range(3):
            pre = dot3(
                forward_matrix,
                shifted[:, :, pl.ds(slab + plane, 3)].reshape(144, HALF),
            )
            sigmoid = 1.0 / (1.0 + jnp.exp(-pre))
            acts[plane] = pre * sigmoid
            hidden[plane + 1] = sigmoid * (1.0 + pre * (1.0 - sigmoid))
        for plane in range(2):
            refined = dot3(last_matrix, acts[slab + plane])
            pieces[0, owner, 2 * plane : 2 * plane + 2, :] = refined[0:2]
            pieces[0, owner, 4 + 2 * plane : 6 + 2 * plane, :] = refined[2:4]
        field_start(0)
        near_wait(1)
        for part in range(2):
            for side in range(2):
                for plane in range(2):
                    line = part * 4 + plane * 2
                    for again in (0, 4):
                        cot_rows[part, 2 * side + plane, again : again + 1, :] = near[
                            1, 0, side, line + 1 : line + 2, :
                        ]
                        cot_rows[part, 2 * side + plane, again + 1 : again + 3, :] = near[
                            1, 1, side, line : line + 2, :
                        ]
                        cot_rows[part, 2 * side + plane, again + 3 : again + 4, :] = near[
                            1, 2, side, line : line + 1, :
                        ]
        for plane in range(3):
            real = jnp.broadcast_to(cot_rows[0, slab + plane][None], (9, 8, HALF))
            imag = jnp.broadcast_to(cot_rows[1, slab + plane][None], (9, 8, HALF))
            spread_cot = last_columns[:, 0:1] * real.reshape(HID * 4, HALF) + last_columns[
                :, 1:2
            ] * imag.reshape(HID * 4, HALF)
            hidden[plane + 1] = hidden[plane + 1] * spread_cot
        for plane in range(2):
            back = dot3(
                backward_matrix, hidden[pl.ds(slab + plane, 3)].reshape(3 * HID * 4, HALF)
            )
            back = (
                pltpu.roll(back[0:4], HALF - 1, 1) + back[4:8] + pltpu.roll(back[8:12], 1, 1)
            )
            pieces[1, owner, 2 * plane : 2 * plane + 2, :] = back[0:2]
            pieces[1, owner, 4 + 2 * plane : 6 + 2 * plane, :] = back[2:4]
        field_start(1)

    field_wait(0)
    for group in range(4):
        plane = group % 2
        other_real, other_imag = fields[0, 0, plane, :CELLS], fields[0, 1, plane, :CELLS]
        field = images[1, 24 * group : 24 * group + CELLS, :]
        real, imag = field[:, :HALF], field[:, HALF:]
        out_real = -(real * other_real + imag * other_imag)
        out_imag = real * other_imag - imag * other_real
        grad_sens[group // 2, plane, :, :LEN] = out_real[:, :LEN]
        grad_sens[group // 2, plane, :, LEN:] = out_imag[:, :LEN]
    field_wait(1)
    for group in range(4):
        plane = group % 2
        other_real, other_imag = fields[1, 0, plane, :CELLS], fields[1, 1, plane, :CELLS]
        real, imag = maps[group, :CELLS, :HALF], maps[group, :CELLS, HALF:]
        lines[GROUP * group : GROUP * group + CELLS, :HALF] = real * other_real - imag * other_imag
        lines[GROUP * group : GROUP * group + CELLS, HALF:] = -(
            real * other_imag + imag * other_real
        )
    spread_out(2)
    swap_start(2)
    for group in range(4):
        plane = group % 2
        other_real, other_imag = fields[1, 0, plane, :CELLS], fields[1, 1, plane, :CELLS]
        field = images[0, 24 * group : 24 * group + CELLS, :]
        real, imag = field[:, :HALF], field[:, HALF:]
        out_real = -(real * other_real + imag * other_imag)
        out_imag = real * other_imag - imag * other_real
        grad_sens[group // 2, plane, :, :LEN] += out_real[:, :LEN]
        grad_sens[group // 2, plane, :, LEN:] += out_imag[:, :LEN]
    square_row = lax.broadcasted_iota(jnp.int32, (CELLS, CELLS), 0)
    square_column = lax.broadcasted_iota(jnp.int32, (CELLS, CELLS), 1)
    factors = []
    for plane in range(2):
        sampled = jnp.broadcast_to(mask[plane : plane + 1, :].astype(jnp.float32), (CELLS, CELLS))
        column = jnp.sum(
            jnp.where(square_row == square_column, sampled, 0.0), axis=1, keepdims=True
        )
        factors.append(1.0 - eta[0] * column)
    swap_wait(2)
    model = gather_in(2)
    for group in range(4):
        plane = group % 2
        mine = model[24 * group : 24 * group + CELLS]
        real, imag = mine[:, :LEN], mine[:, HALF : HALF + LEN]
        grad_kspace[group // 2, plane, :, :LEN] = (
            factors[plane] * cotangent[group // 2, plane, :, :LEN] - real
        )
        grad_kspace[group // 2, plane, :, LEN:] = (
            factors[plane] * cotangent[group // 2, plane, :, LEN:] + imag
        )

    for which in range(3):

        @pl.loop(1, PEERS)
        def _(step):
            swap(which, step).wait_send()

    for which in range(2):

        @pl.loop(0, OWNERS)
        def _(target):
            @pl.when(owner_coil(target) != coil)
            def _():
                part_copy(which, target).wait_send()

        @pl.when(owns)
        def _():
            for step, across in near_by:
                copy, there = near_copy(which, step, across)
                pl.when(there)(copy.wait_send)

            @pl.loop(1, COIL_PEERS)
            def _(step):
                field_copy(which, step).wait_send()


def local(kspace, cotangent, sens, mask, eta, w_first, w_last):
    table_arrays = tables()
    constant_arrays = selectors()
    vmem = pl.BlockSpec(memory_space=pltpu.VMEM)
    smem = pl.BlockSpec(memory_space=pltpu.SMEM)
    anywhere = pl.BlockSpec(memory_space=pl.ANY)
    f32, b16 = jnp.float32, jnp.bfloat16
    return pl.pallas_call(
        kernel,
        out_shape=(
            jax.ShapeDtypeStruct(kspace.shape, f32),
            jax.ShapeDtypeStruct(sens.shape, f32),
        ),
        in_specs=[vmem] * 4 + [smem] + [vmem] * 2 + [anywhere] * 4 + [vmem] * len(constant_arrays),
        out_specs=(vmem, vmem),
        scratch_shapes=[
            pltpu.VMEM((PEERS * SENT, WIDE), b16),
            pltpu.VMEM((PEERS * SENT, WIDE), b16),
            pltpu.VMEM((2 * PEERS * GROUP, WIDE), b16),
            pltpu.VMEM((2 * PEERS * GROUP, WIDE), b16),
            pltpu.VMEM((4 * GROUP, WIDE), f32),
            pltpu.VMEM((3, PEERS * SENT, 128), f32),
            pltpu.VMEM((3, PEERS, SENT, 128), f32),
            pltpu.VMEM((96, 2 * PEERS * GROUP), f32),
            pltpu.VMEM((2, 96, WIDE), f32),
            pltpu.VMEM((4, 24, WIDE), f32),
            pltpu.VMEM((2, OWNERS, 8, HALF), f32),
            pltpu.VMEM((2, COIL_PEERS, 8, HALF), f32),
            pltpu.VMEM((2, 3, 2, 8, HALF), f32),
            pltpu.VMEM((3, 2, 6, 8, HALF), f32),
            pltpu.VMEM((2, 4, 8, HALF), f32),
            pltpu.VMEM((3, HID * 4, HALF), f32),
            pltpu.VMEM((5, HID * 4, HALF), f32),
            pltpu.VMEM((2, OWNERS, 8, HALF), f32),
            pltpu.VMEM((2, 2, 2, 24, HALF), f32),
            pltpu.SemaphoreType.DMA((4,)),
            pltpu.SemaphoreType.DMA((3, PEERS)),
            pltpu.SemaphoreType.DMA((3, PEERS)),
            pltpu.SemaphoreType.DMA((2, OWNERS)),
            pltpu.SemaphoreType.DMA((2, COIL_PEERS)),
            pltpu.SemaphoreType.DMA((2, 6)),
            pltpu.SemaphoreType.DMA((2, 6)),
            pltpu.SemaphoreType.DMA((2, COIL_PEERS)),
            pltpu.SemaphoreType.DMA((2, OWNERS)),
        ],
        compiler_params=pltpu.CompilerParams(
            collective_id=0, has_side_effects=True, vmem_limit_bytes=48 * 1024 * 1024
        ),
    )(
        kspace,
        cotangent,
        sens,
        mask,
        eta,
        w_first.reshape(HID, 54),
        w_last,
        *[jnp.asarray(table) for table in table_arrays],
        *[jnp.asarray(array) for array in constant_arrays],
    )


def solution(mesh):
    part = P("coil", "slab", "row", None)
    return jax.shard_map(
        local,
        mesh=mesh,
        in_specs=(part, part, part, P("slab", "row"), P(), P(), P()),
        out_specs=(part, part),
        check_vma=False,
    )
```

```python
import math

import jax
import jax.numpy as jnp
import ml_dtypes
import numpy as np
from jax import lax
from jax.experimental import pallas as pl
from jax.experimental.pallas import tpu as pltpu
from jax.sharding import PartitionSpec as P

MESH = pl.DeviceIdType.MESH
LEN = 320
HALF = 384
WIDE = 2 * HALF
CELLS = 20
GROUP = 32
PEERS = 16
COIL_PEERS = 16
SENT = 2 * CELLS
OWNERS = 10
HID = 18


def turned(owner, row):
    return owner + (row % 2) * (OWNERS - 1 - 2 * owner)


def owner_coil(owner, row):
    return (8 * turned(owner, row)) // 5


def coil_owner(coil, row):
    return turned((5 * coil + 7) // 8, row)


def split_table(table):
    high = table.astype(ml_dtypes.bfloat16)
    low = (table - high.astype(np.float64)).astype(ml_dtypes.bfloat16)
    return high, low


def tables():
    at = np.arange(LEN)
    angle = 2.0 * math.pi * ((at[:, None] * at[None, :]) % LEN) / LEN
    cosine, sine = np.cos(angle) / math.sqrt(LEN), np.sin(angle) / math.sqrt(LEN)
    mix = np.zeros((2, LEN, 2, LEN))
    mix[0, :, 0], mix[0, :, 1], mix[1, :, 0], mix[1, :, 1] = cosine, -sine, sine, cosine
    first = np.zeros((PEERS, 2, CELLS, 2, HALF))
    first[..., :LEN] = mix.reshape(2, PEERS, CELLS, 2, LEN).transpose(1, 0, 2, 3, 4)
    second = np.zeros((2, PEERS, GROUP, 2, HALF))
    second[:, :, :CELLS, :, :LEN] = mix.transpose(2, 3, 0, 1).reshape(2, PEERS, CELLS, 2, LEN)
    return split_table(first.reshape(PEERS * SENT, WIDE)) + split_table(
        second.reshape(2 * PEERS * GROUP, WIDE)
    )


def selectors():
    repeat = np.zeros((HID * 4, HID), np.float32)
    for unit in range(HID):
        repeat[4 * unit : 4 * unit + 4, unit] = 1.0
    pick = np.zeros((3, 54, 144), np.float32)
    place = np.zeros((3, HID * 4, 144), np.float32)
    for column in range(144):
        e3, channel, e1, row = column // 48, column // 24 % 2, column // 8 % 3, column % 8
        for e2 in range(3):
            pick[e2, 2 * (e1 * 9 + e2 * 3 + e3) + channel, column] = 1.0
            for line in range(HID * 4):
                if row - line % 4 == e2:
                    place[e2, line, column] = 1.0
    repeat_back = np.concatenate([repeat] * 3, axis=0)
    pick_back = np.zeros((9, 16, 54), np.float32)
    place_back = np.zeros((9, 16, 216), np.float32)
    for plane in range(3):
        for e2 in range(3):
            for line in range(12):
                e3, channel, row = line // 4, line // 2 % 2, line % 2
                pick_back[plane * 3 + e2, line, 2 * ((2 - plane) * 9 + e2 * 3 + e3) + channel] = 1.0
                for column in range(216):
                    if column // 72 == plane and row + 2 - column % 4 == e2:
                        place_back[plane * 3 + e2, line, column] = 1.0
    place_last = np.zeros((8, HID * 4), np.float32)
    pick_last = np.zeros((8, 2), np.float32)
    for line in range(4):
        pick_last[line, line // 2] = 1.0
        for column in range(HID * 4):
            if column % 4 == line % 2 + 1:
                place_last[line, column] = 1.0
    return (
        repeat,
        pick,
        place,
        repeat_back,
        pick_back.reshape(144, 54),
        place_back.reshape(144, 216),
        place_last,
        pick_last,
    )


def split(values):
    high = values.astype(jnp.bfloat16)
    return high, (values - high.astype(jnp.float32)).astype(jnp.bfloat16)


def dot(left, right, dims=((1,), (0,))):
    return lax.dot_general(left, right, (dims, ((), ())), preferred_element_type=jnp.float32)


def dot3(left, right):
    left_high, left_low = split(left)
    right_high, right_low = split(right)
    return dot(left_high, right_high) + dot(left_low, right_high) + dot(left_high, right_low)


def exact_dot(left, right, dims=((1,), (0,))):
    return lax.dot_general(
        left,
        right,
        (dims, ((), ())),
        precision=lax.Precision.HIGHEST,
        preferred_element_type=jnp.float32,
    )


def kernel(*refs):
    (
        kspace_hbm,
        cotangent_hbm,
        sens_hbm,
        mask_hbm,
        eta,
        w_first_hbm,
        w_last_hbm,
        *constants_hbm,
    ) = refs[:19]
    grad_kspace_hbm, grad_sens_hbm = refs[19:21]
    (
        kspace,
        cotangent,
        sens,
        mask,
        w_first,
        w_last,
        first_high,
        first_low,
        second_high,
        second_low,
        repeat,
        pick,
        place,
        repeat_back,
        pick_back,
        place_back,
        place_last,
        pick_last,
        grad_kspace,
        grad_sens,
        lines,
        spread,
        landed,
        wide,
        images,
        maps,
        parts,
        sums,
        near,
        shifted,
        cot_rows,
        acts,
        hidden,
        pieces,
        fields,
        half_done,
        load_sem,
        store_sem,
        swap_send,
        swap_recv,
        sum_send,
        sum_recv,
        near_send,
        near_recv,
        field_send,
        field_recv,
    ) = refs[21:]
    coil, slab, row = lax.axis_index("coil"), lax.axis_index("slab"), lax.axis_index("row")
    owner = coil_owner(coil, row)
    owns = owner_coil(owner, row) == coil

    def neighbour(step):
        other = owner + step
        other_row = row + jnp.where(other < 0, -1, 0) + jnp.where(other >= OWNERS, 1, 0)
        there = jnp.logical_and(other_row >= 0, other_row < PEERS)
        return owner_coil((other + OWNERS) % OWNERS, other_row), other_row, there

    near_by = [
        (step, across) for step in (-1, 0, 1) for across in (0, 1) if (step, across) != (0, 0)
    ]

    sources = [kspace_hbm, *constants_hbm[:2], cotangent_hbm, sens_hbm, *constants_hbm[2:4]]
    targets = [kspace, first_high, first_low, cotangent, sens, second_high, second_low]
    sources += [w_first_hbm, w_last_hbm, mask_hbm, *constants_hbm[4:]]
    targets += [w_first, w_last, mask, repeat, pick, place, repeat_back, pick_back, place_back]
    targets += [place_last, pick_last]
    loads = [
        pltpu.make_async_copy(source, target, load_sem.at[number])
        for number, (source, target) in enumerate(zip(sources, targets))
    ]
    for load in loads[:4]:
        load.start()

    near[...] = jnp.zeros_like(near)

    barrier = pltpu.get_barrier_semaphore()

    @pl.loop(1, PEERS)
    def _(step):
        pl.semaphore_signal(
            barrier, inc=1, device_id={"row": (row + step) % PEERS}, device_id_type=MESH
        )
        pl.semaphore_signal(
            barrier, inc=1, device_id={"coil": (coil + step) % COIL_PEERS}, device_id_type=MESH
        )

    for step, across in near_by:
        other_coil, other_row, there = neighbour(step)

        @pl.when(jnp.logical_and(owns, there))
        def _():
            pl.semaphore_signal(
                barrier,
                inc=1,
                device_id={
                    "coil": other_coil,
                    "slab": (slab + across) % 2,
                    "row": other_row,
                },
                device_id_type=MESH,
            )

    def spread_out(which):
        high, low = split(lines[...])
        both = dot(first_high[...], jnp.concatenate([high, low], axis=0), ((1,), (1,)))
        rest = dot(first_low[...], high, ((1,), (1,)))
        spread[which] = both[:, :128] + both[:, 128:] + rest

    def swap(which, step):
        peer = (row + step) % PEERS
        return pltpu.make_async_remote_copy(
            src_ref=spread.at[which, pl.ds(pl.multiple_of(peer * SENT, 8), SENT)],
            dst_ref=landed.at[which, row],
            send_sem=swap_send.at[which, peer],
            recv_sem=swap_recv.at[which, row],
            device_id={"row": peer},
            device_id_type=MESH,
        )

    def swap_start(which):
        @pl.loop(1, PEERS)
        def _(step):
            swap(which, step).start()

        landed[which, row] = spread[which, pl.ds(pl.multiple_of(row * SENT, 8), SENT), :]

    def swap_wait(which):
        @pl.loop(1, PEERS)
        def _(step):
            peer = (row + step) % PEERS
            pltpu.make_async_remote_copy(
                src_ref=spread.at[which, pl.ds(0, SENT)],
                dst_ref=landed.at[which, peer],
                send_sem=swap_send.at[which, peer],
                recv_sem=swap_recv.at[which, peer],
                device_id={"row": peer},
                device_id_type=MESH,
            ).wait_recv()

    lane = lax.broadcasted_iota(jnp.int32, (CELLS, 128), 1)

    def gather_in(which):
        for part in range(2):
            for four in range(PEERS // 4):
                blocks = [
                    landed[which, 4 * four + inner, part * CELLS : (part + 1) * CELLS, :]
                    for inner in range(4)
                ]
                for group in range(4):
                    tile = None
                    for inner in range(4):
                        turn = (inner - group) % 4 * GROUP
                        moved = pltpu.roll(blocks[inner], turn, 1) if turn else blocks[inner]
                        tile = moved if tile is None else jnp.where(lane >= GROUP * inner, moved, tile)
                    start = part * PEERS * GROUP + four * 128
                    wide[24 * group : 24 * group + CELLS, start : start + 128] = tile
        high, low = split(wide[...])
        both = dot(jnp.concatenate([high, low], axis=0), second_high[...])
        return both[:96] + both[96:] + dot(high, second_low[...])

    def halves(ref, group):
        lines_now = ref[group // 2, :, group % 2, :]
        tiles = [lines_now[:, 128 * tile : 128 * tile + 128] for tile in range(5)]
        low = lane < 64
        turned = [pltpu.roll(tile, 64, 1) for tile in tiles[2:]]
        zero = jnp.zeros_like(tiles[0])
        return (
            tiles[:2] + [jnp.where(low, tiles[2], zero)],
            [
                jnp.where(low, turned[0], turned[1]),
                jnp.where(low, turned[1], turned[2]),
                jnp.where(low, turned[2], zero),
            ],
        )

    def whole_lines(real, imag):
        low = lane < 64
        turned = [pltpu.roll(imag[:, 128 * tile : 128 * tile + 128], 64, 1) for tile in range(3)]
        tiles = [
            real[:, :128],
            real[:, 128:256],
            jnp.where(low, real[:, 256:], turned[0]),
            jnp.where(low, turned[0], turned[1]),
            jnp.where(low, turned[1], turned[2]),
        ]
        return jnp.concatenate(tiles, axis=1)

    def put_lines(ref):
        for group in range(4):
            for half, tiles in enumerate(halves(ref, group)):
                for number, tile in enumerate(tiles):
                    start = half * HALF + 128 * number
                    lines[GROUP * group : GROUP * group + CELLS, start : start + 128] = tile

    lines[...] = jnp.zeros_like(lines)
    loads[0].wait()
    put_lines(kspace)
    loads[1].wait()
    loads[2].wait()
    for load in loads[4:]:
        load.start()
    spread_out(0)

    near_count = jnp.int32(0)
    for step, across in near_by:
        near_count = near_count + jnp.where(jnp.logical_and(owns, neighbour(step)[2]), 1, 0)
    pl.semaphore_wait(barrier, 2 * (PEERS - 1) + near_count)

    swap_start(0)
    loads[3].wait()
    put_lines(cotangent)
    spread_out(1)
    swap_start(1)

    wide[...] = jnp.zeros_like(wide)
    maps[...] = jnp.zeros_like(maps)
    loads[4].wait()
    for group in range(4):
        for half, tiles in enumerate(halves(sens, group)):
            for number, tile in enumerate(tiles):
                start = half * HALF + 128 * number
                maps[group, :CELLS, start : start + 128] = tile
    for load in loads[5:]:
        load.wait()
    weights = w_first[...].reshape(54, HID)
    weights_rows = exact_dot(repeat[...], weights, ((1,), (1,)))
    forward_matrix = jnp.zeros((HID * 4, 144), jnp.float32)
    for e2 in range(3):
        forward_matrix += place[e2] * exact_dot(weights_rows, pick[e2])
    weights_back = exact_dot(weights, repeat_back[...], ((1,), (1,)))
    backward_matrix = jnp.sum(
        (exact_dot(pick_back[...], weights_back) * place_back[...]).reshape(9, 16, 216), axis=0
    )
    last_columns = exact_dot(repeat[...], w_last[...], ((1,), (1,)))
    last_matrix = place_last[...] * exact_dot(
        pick_last[...], exact_dot(w_last[...], repeat[...], ((1,), (1,)))
    )

    def part_sums(which, total_field):
        for plane in range(2):
            real = imag = None
            for local_coil in range(2):
                group = local_coil * 2 + plane
                map_real, map_imag = maps[group, :, :HALF], maps[group, :, HALF:]
                field = total_field[24 * group : 24 * group + 24]
                field_real, field_imag = field[:, :HALF], field[:, HALF:]
                this_real = map_real * field_real + map_imag * field_imag
                this_imag = map_real * field_imag - map_imag * field_real
                real = this_real if real is None else real + this_real
                imag = this_imag if imag is None else imag + this_imag
            for target in range(OWNERS):
                cut = slice(2 * target, 2 * target + 2)
                parts[which, target, 2 * plane : 2 * plane + 2, :] = real[cut]
                parts[which, target, 4 + 2 * plane : 6 + 2 * plane, :] = imag[cut]

    def part_copy(which, target):
        return pltpu.make_async_remote_copy(
            src_ref=parts.at[which, target],
            dst_ref=sums.at[which, coil],
            send_sem=sum_send.at[which, target],
            recv_sem=sum_recv.at[which, coil],
            device_id={"coil": owner_coil(target, row)},
            device_id_type=MESH,
        )

    def part_start(which):
        @pl.loop(0, OWNERS)
        def _(step):
            target = (owner + step) % OWNERS

            @pl.when(owner_coil(target, row) != coil)
            def _():
                part_copy(which, target).start()

    def part_total(which):
        @pl.loop(1, COIL_PEERS)
        def _(step):
            peer = (coil + step) % COIL_PEERS
            pltpu.make_async_remote_copy(
                src_ref=parts.at[which, 0],
                dst_ref=sums.at[which, peer],
                send_sem=sum_send.at[which, 0],
                recv_sem=sum_recv.at[which, peer],
                device_id={"coil": peer},
                device_id_type=MESH,
            ).wait_recv()

        sums[which, coil] = parts[which, owner]
        total = sums[which, 0]
        for peer in range(1, COIL_PEERS):
            total = total + sums[which, peer]
        return total

    def near_copy(which, step, across):
        other_coil, other_row, there = neighbour(step)
        copy = pltpu.make_async_remote_copy(
            src_ref=near.at[which, 1, slab],
            dst_ref=near.at[which, 1 - step, slab],
            send_sem=near_send.at[which, (step + 1) * 2 + across],
            recv_sem=near_recv.at[which, (1 - step) * 2 + across],
            device_id={"coil": other_coil, "slab": (slab + across) % 2, "row": other_row},
            device_id_type=MESH,
        )
        return copy, there

    def near_start(which):
        for step, across in near_by:
            copy, there = near_copy(which, step, across)
            pl.when(there)(copy.start)

    def near_wait(which):
        for step, across in near_by:
            other_coil, other_row, there = neighbour(step)
            copy = pltpu.make_async_remote_copy(
                src_ref=near.at[which, 1, slab],
                dst_ref=near.at[which, 1 + step, (slab + across) % 2],
                send_sem=near_send.at[which, (step + 1) * 2 + across],
                recv_sem=near_recv.at[which, (1 + step) * 2 + across],
                device_id={"coil": other_coil, "slab": (slab + across) % 2, "row": other_row},
                device_id_type=MESH,
            )
            pl.when(there)(copy.wait_recv)

    def field_copy(which, step):
        peer = (coil + step) % COIL_PEERS
        return pltpu.make_async_remote_copy(
            src_ref=pieces.at[which, owner],
            dst_ref=pieces.at[which, owner],
            send_sem=field_send.at[which, peer],
            recv_sem=field_recv.at[which, owner],
            device_id={"coil": peer},
            device_id_type=MESH,
        )

    def field_start(which):
        @pl.loop(1, COIL_PEERS)
        def _(step):
            field_copy(which, step).start()

    def field_wait(which):
        @pl.loop(0, OWNERS)
        def _(target):
            @pl.when(owner_coil(target, row) != coil)
            def _():
                pltpu.make_async_remote_copy(
                    src_ref=pieces.at[which, target],
                    dst_ref=pieces.at[which, target],
                    send_sem=field_send.at[which, 0],
                    recv_sem=field_recv.at[which, target],
                    device_id={"coil": owner_coil(target, row)},
                    device_id_type=MESH,
                ).wait_recv()

        for target in range(OWNERS):
            for part in range(2):
                for plane in range(2):
                    line = part * 4 + plane * 2
                    fields[which, part, plane, 2 * target : 2 * target + 2, :] = pieces[
                        which, target, line : line + 2, :
                    ]

    swap_wait(0)
    total_field = gather_in(0)
    images[0] = total_field
    part_sums(0, total_field)
    part_start(0)
    swap_wait(1)
    total_field = gather_in(1)
    images[1] = total_field
    part_sums(1, total_field)
    part_start(1)

    @pl.when(owns)
    def _():
        near[0, 1, slab] = part_total(0)
        near_start(0)
        near[1, 1, slab] = part_total(1)
        near_start(1)
        shifted[...] = jnp.zeros_like(shifted)
        hidden[0] = jnp.zeros((HID * 4, HALF), jnp.float32)
        hidden[4] = jnp.zeros((HID * 4, HALF), jnp.float32)
        near_wait(0)
        for part in range(2):
            for side in range(2):
                for plane in range(2):
                    line = part * 4 + plane * 2
                    for step in range(3):
                        shifted[1, part, 1 + 2 * side + plane, 2 * step : 2 * step + 2, :] = near[
                            0, step, side, line : line + 2, :
                        ]
        middle = shifted[1].reshape(2 * 6 * 8, HALF)
        shifted[0] = pltpu.roll(middle, 1, 1).reshape(2, 6, 8, HALF)
        shifted[2] = pltpu.roll(middle, HALF - 1, 1).reshape(2, 6, 8, HALF)
        for plane in range(3):
            pre = dot3(
                forward_matrix,
                shifted[:, :, pl.ds(slab + plane, 3)].reshape(144, HALF),
            )
            sigmoid = 1.0 / (1.0 + jnp.exp(-pre))
            acts[plane] = pre * sigmoid
            hidden[plane + 1] = sigmoid * (1.0 + pre * (1.0 - sigmoid))
        for plane in range(2):
            refined = dot3(last_matrix, acts[slab + plane])
            pieces[0, owner, 2 * plane : 2 * plane + 2, :] = refined[0:2]
            pieces[0, owner, 4 + 2 * plane : 6 + 2 * plane, :] = refined[2:4]
        field_start(0)
        near_wait(1)
        for part in range(2):
            for side in range(2):
                for plane in range(2):
                    line = part * 4 + plane * 2
                    for again in (0, 4):
                        cot_rows[part, 2 * side + plane, again : again + 1, :] = near[
                            1, 0, side, line + 1 : line + 2, :
                        ]
                        cot_rows[part, 2 * side + plane, again + 1 : again + 3, :] = near[
                            1, 1, side, line : line + 2, :
                        ]
                        cot_rows[part, 2 * side + plane, again + 3 : again + 4, :] = near[
                            1, 2, side, line : line + 1, :
                        ]
        for plane in range(3):
            real = jnp.broadcast_to(cot_rows[0, slab + plane][None], (9, 8, HALF))
            imag = jnp.broadcast_to(cot_rows[1, slab + plane][None], (9, 8, HALF))
            spread_cot = last_columns[:, 0:1] * real.reshape(HID * 4, HALF) + last_columns[
                :, 1:2
            ] * imag.reshape(HID * 4, HALF)
            hidden[plane + 1] = hidden[plane + 1] * spread_cot
        for plane in range(2):
            back = dot3(
                backward_matrix, hidden[pl.ds(slab + plane, 3)].reshape(3 * HID * 4, HALF)
            )
            back = (
                pltpu.roll(back[0:4], HALF - 1, 1) + back[4:8] + pltpu.roll(back[8:12], 1, 1)
            )
            pieces[1, owner, 2 * plane : 2 * plane + 2, :] = back[0:2]
            pieces[1, owner, 4 + 2 * plane : 6 + 2 * plane, :] = back[2:4]
        field_start(1)

    field_wait(0)
    for group in range(4):
        plane = group % 2
        other_real, other_imag = fields[0, 0, plane, :CELLS], fields[0, 1, plane, :CELLS]
        field = images[1, 24 * group : 24 * group + CELLS, :]
        real, imag = field[:, :HALF], field[:, HALF:]
        out_real = -(real * other_real + imag * other_imag)
        out_imag = real * other_imag - imag * other_real
        half_done[group, :CELLS, :HALF] = out_real
        half_done[group, :CELLS, HALF:] = out_imag
    field_wait(1)
    for group in range(4):
        plane = group % 2
        other_real, other_imag = fields[1, 0, plane, :CELLS], fields[1, 1, plane, :CELLS]
        real, imag = maps[group, :CELLS, :HALF], maps[group, :CELLS, HALF:]
        lines[GROUP * group : GROUP * group + CELLS, :HALF] = real * other_real - imag * other_imag
        lines[GROUP * group : GROUP * group + CELLS, HALF:] = -(
            real * other_imag + imag * other_real
        )
    spread_out(2)
    swap_start(2)
    for group in range(4):
        plane = group % 2
        other_real, other_imag = fields[1, 0, plane, :CELLS], fields[1, 1, plane, :CELLS]
        field = images[0, 24 * group : 24 * group + CELLS, :]
        real, imag = field[:, :HALF], field[:, HALF:]
        out_real = -(real * other_real + imag * other_imag)
        out_imag = real * other_imag - imag * other_real
        out_real = out_real + half_done[group, :CELLS, :HALF]
        out_imag = out_imag + half_done[group, :CELLS, HALF:]
        grad_sens[group // 2, plane, :, :] = whole_lines(out_real, out_imag)
    stores = [
        pltpu.make_async_copy(grad_sens, grad_sens_hbm, store_sem.at[0]),
        pltpu.make_async_copy(grad_kspace, grad_kspace_hbm, store_sem.at[1]),
    ]
    stores[0].start()
    square_row = lax.broadcasted_iota(jnp.int32, (CELLS, CELLS), 0)
    square_column = lax.broadcasted_iota(jnp.int32, (CELLS, CELLS), 1)
    factors = []
    for plane in range(2):
        sampled = jnp.broadcast_to(mask[plane : plane + 1, :].astype(jnp.float32), (CELLS, CELLS))
        column = jnp.sum(
            jnp.where(square_row == square_column, sampled, 0.0), axis=1, keepdims=True
        )
        factors.append(1.0 - eta[0] * column)
    swap_wait(2)
    model = gather_in(2)
    for group in range(4):
        plane = group % 2
        mine = model[24 * group : 24 * group + CELLS]
        grad_kspace[group // 2, plane, :, :] = factors[plane] * cotangent[
            group // 2, :, plane, :
        ] - whole_lines(mine[:, :HALF], -mine[:, HALF:])
    stores[1].start()

    for which in range(3):

        @pl.loop(1, PEERS)
        def _(step):
            swap(which, step).wait_send()

    for which in range(2):

        @pl.loop(0, OWNERS)
        def _(target):
            @pl.when(owner_coil(target, row) != coil)
            def _():
                part_copy(which, target).wait_send()

        @pl.when(owns)
        def _():
            for step, across in near_by:
                copy, there = near_copy(which, step, across)
                pl.when(there)(copy.wait_send)

            @pl.loop(1, COIL_PEERS)
            def _(step):
                field_copy(which, step).wait_send()
    stores[0].wait()
    stores[1].wait()


def local(kspace, cotangent, sens, mask, eta, w_first, w_last):
    constants = [jnp.asarray(array) for array in tables() + selectors()]
    smem = pl.BlockSpec(memory_space=pltpu.SMEM)
    anywhere = pl.BlockSpec(memory_space=pl.ANY)
    f32, b16 = jnp.float32, jnp.bfloat16
    rows = jax.ShapeDtypeStruct((2, CELLS, 2, 2 * LEN), f32)
    result = jax.ShapeDtypeStruct(kspace.shape, f32)
    return pl.pallas_call(
        kernel,
        out_shape=(result, result),
        in_specs=[anywhere] * 4 + [smem] + [anywhere] * 14,
        out_specs=(anywhere, anywhere),
        scratch_shapes=[
            pltpu.VMEM(rows.shape, f32),
            pltpu.VMEM(rows.shape, f32),
            pltpu.VMEM(rows.shape, f32),
            pltpu.VMEM(mask.shape, jnp.int32),
            pltpu.VMEM((27, 2, HID), f32),
            pltpu.VMEM(w_last.shape, f32),
            *[pltpu.VMEM(array.shape, array.dtype) for array in constants],
            pltpu.VMEM(result.shape, f32),
            pltpu.VMEM(result.shape, f32),
            pltpu.VMEM((4 * GROUP, WIDE), f32),
            pltpu.VMEM((3, PEERS * SENT, 128), f32),
            pltpu.VMEM((3, PEERS, SENT, 128), f32),
            pltpu.VMEM((96, 2 * PEERS * GROUP), f32),
            pltpu.VMEM((2, 96, WIDE), f32),
            pltpu.VMEM((4, 24, WIDE), f32),
            pltpu.VMEM((2, OWNERS, 8, HALF), f32),
            pltpu.VMEM((2, COIL_PEERS, 8, HALF), f32),
            pltpu.VMEM((2, 3, 2, 8, HALF), f32),
            pltpu.VMEM((3, 2, 6, 8, HALF), f32),
            pltpu.VMEM((2, 4, 8, HALF), f32),
            pltpu.VMEM((3, HID * 4, HALF), f32),
            pltpu.VMEM((5, HID * 4, HALF), f32),
            pltpu.VMEM((2, OWNERS, 8, HALF), f32),
            pltpu.VMEM((2, 2, 2, 24, HALF), f32),
            pltpu.VMEM((4, 24, WIDE), f32),
            pltpu.SemaphoreType.DMA((18,)),
            pltpu.SemaphoreType.DMA((2,)),
            pltpu.SemaphoreType.DMA((3, PEERS)),
            pltpu.SemaphoreType.DMA((3, PEERS)),
            pltpu.SemaphoreType.DMA((2, OWNERS)),
            pltpu.SemaphoreType.DMA((2, COIL_PEERS)),
            pltpu.SemaphoreType.DMA((2, 6)),
            pltpu.SemaphoreType.DMA((2, 6)),
            pltpu.SemaphoreType.DMA((2, COIL_PEERS)),
            pltpu.SemaphoreType.DMA((2, OWNERS)),
        ],
        compiler_params=pltpu.CompilerParams(
            collective_id=0, has_side_effects=True, vmem_limit_bytes=62 * 1024 * 1024
        ),
    )(
        kspace.transpose(0, 2, 1, 3),
        cotangent.transpose(0, 2, 1, 3),
        sens.transpose(0, 2, 1, 3),
        mask,
        eta,
        w_first.transpose(2, 3, 4, 1, 0).reshape(27, 2, HID),
        w_last,
        *constants,
    )


def solution(mesh):
    part = P("coil", "slab", "row", None)
    return jax.shard_map(
        local,
        mesh=mesh,
        in_specs=(part, part, part, P("slab", "row"), P(), P(), P()),
        out_specs=(part, part),
        check_vma=False,
    )
```

```python
import math

import jax
import jax.numpy as jnp
import ml_dtypes
import numpy as np
from jax import lax
from jax.experimental import pallas as pl
from jax.experimental.pallas import tpu as pltpu
from jax.sharding import PartitionSpec as P

MESH = pl.DeviceIdType.MESH
LEN = 320
HALF = 384
WIDE = 2 * HALF
CELLS = 20
GROUP = 32
PEERS = 16
COIL_PEERS = 16
SENT = 2 * CELLS
REACH = 4
OWNERS = 10
HID = 18


def turned(owner, row):
    return owner + (row % 2) * (OWNERS - 1 - 2 * owner)


def owner_coil(owner, row):
    return (8 * turned(owner, row)) // 5


def coil_owner(coil, row):
    return turned((5 * coil + 7) // 8, row)


def split_table(table):
    high = table.astype(ml_dtypes.bfloat16)
    low = (table - high.astype(np.float64)).astype(ml_dtypes.bfloat16)
    return high, low


def tables():
    at = np.arange(LEN)
    angle = 2.0 * math.pi * ((at[:, None] * at[None, :]) % LEN) / LEN
    cosine, sine = np.cos(angle) / math.sqrt(LEN), np.sin(angle) / math.sqrt(LEN)
    mix = np.zeros((2, LEN, 2, LEN))
    mix[0, :, 0], mix[0, :, 1], mix[1, :, 0], mix[1, :, 1] = cosine, -sine, sine, cosine
    first = np.zeros((PEERS, 2, CELLS, 2, HALF))
    first[..., :LEN] = mix.reshape(2, PEERS, CELLS, 2, LEN).transpose(1, 0, 2, 3, 4)
    second = np.zeros((2, PEERS, GROUP, 2, HALF))
    second[:, :, :CELLS, :, :LEN] = mix.transpose(2, 3, 0, 1).reshape(2, PEERS, CELLS, 2, LEN)
    return split_table(first.reshape(PEERS * SENT, WIDE)) + split_table(
        second.reshape(2 * PEERS * GROUP, WIDE)
    )


def selectors():
    repeat = np.zeros((HID * 4, HID), np.float32)
    for unit in range(HID):
        repeat[4 * unit : 4 * unit + 4, unit] = 1.0
    pick = np.zeros((3, 54, 144), np.float32)
    place = np.zeros((3, HID * 4, 144), np.float32)
    for column in range(144):
        e3, channel, e1, row = column // 48, column // 24 % 2, column // 8 % 3, column % 8
        for e2 in range(3):
            pick[e2, 2 * (e1 * 9 + e2 * 3 + e3) + channel, column] = 1.0
            for line in range(HID * 4):
                if row - line % 4 == e2:
                    place[e2, line, column] = 1.0
    repeat_back = np.concatenate([repeat] * 3, axis=0)
    pick_back = np.zeros((9, 16, 54), np.float32)
    place_back = np.zeros((9, 16, 216), np.float32)
    for plane in range(3):
        for e2 in range(3):
            for line in range(12):
                e3, channel, row = line // 4, line // 2 % 2, line % 2
                pick_back[plane * 3 + e2, line, 2 * ((2 - plane) * 9 + e2 * 3 + e3) + channel] = 1.0
                for column in range(216):
                    if column // 72 == plane and row + 2 - column % 4 == e2:
                        place_back[plane * 3 + e2, line, column] = 1.0
    place_last = np.zeros((8, HID * 4), np.float32)
    pick_last = np.zeros((8, 2), np.float32)
    for line in range(4):
        pick_last[line, line // 2] = 1.0
        for column in range(HID * 4):
            if column % 4 == line % 2 + 1:
                place_last[line, column] = 1.0
    return (
        repeat,
        pick,
        place,
        repeat_back,
        pick_back.reshape(144, 54),
        place_back.reshape(144, 216),
        place_last,
        pick_last,
    )


def unpack(packed):
    low = lax.broadcasted_iota(jnp.int32, (4, 128), 1) < LEN - 256
    last = packed[16:20]
    upper = jnp.where(low, last, 0.0)
    lower = jnp.where(low, pltpu.roll(last, 64, 1), 0.0)
    return jnp.concatenate(
        [packed[0:8], packed[8:16], jnp.concatenate([upper, lower], axis=0)], axis=1
    )


def split(values):
    high = values.astype(jnp.bfloat16)
    return high, (values - high.astype(jnp.float32)).astype(jnp.bfloat16)


def dot(left, right, dims=((1,), (0,))):
    return lax.dot_general(left, right, (dims, ((), ())), preferred_element_type=jnp.float32)


def dot3(left, right):
    left_high, left_low = split(left)
    right_high, right_low = split(right)
    return dot(left_high, right_high) + dot(left_low, right_high) + dot(left_high, right_low)


def exact_dot(left, right, dims=((1,), (0,))):
    return lax.dot_general(
        left,
        right,
        (dims, ((), ())),
        precision=lax.Precision.HIGHEST,
        preferred_element_type=jnp.float32,
    )


def kernel(*refs):
    (
        kspace_hbm,
        cotangent_hbm,
        sens_hbm,
        mask_hbm,
        eta,
        w_first_hbm,
        w_last_hbm,
        *constants_hbm,
    ) = refs[:19]
    grad_kspace_hbm, grad_sens_hbm = refs[19:21]
    (
        kspace,
        cotangent,
        sens,
        mask,
        w_first,
        w_last,
        first_high,
        first_low,
        second_high,
        second_low,
        repeat,
        pick,
        place,
        repeat_back,
        pick_back,
        place_back,
        place_last,
        pick_last,
        grad_kspace,
        grad_sens,
        lines,
        spread,
        landed,
        wide,
        images,
        maps,
        parts,
        sums,
        near,
        shifted,
        cot_rows,
        acts,
        hidden,
        pieces,
        fields,
        half_done,
        load_sem,
        store_sem,
        swap_send,
        swap_recv,
        sum_send,
        sum_recv,
        near_send,
        near_recv,
        field_send,
        field_recv,
        greet_far,
    ) = refs[21:]
    coil, slab, row = lax.axis_index("coil"), lax.axis_index("slab"), lax.axis_index("row")
    owner = coil_owner(coil, row)
    owns = owner_coil(owner, row) == coil

    def neighbour(step):
        other = owner + step
        other_row = row + jnp.where(other < 0, -1, 0) + jnp.where(other >= OWNERS, 1, 0)
        there = jnp.logical_and(other_row >= 0, other_row < PEERS)
        return owner_coil((other + OWNERS) % OWNERS, other_row), other_row, there

    near_by = [
        (step, across) for step in (-1, 0, 1) for across in (0, 1) if (step, across) != (0, 0)
    ]

    sources = [kspace_hbm, *constants_hbm[:2], cotangent_hbm, sens_hbm, *constants_hbm[2:4]]
    targets = [kspace, first_high, first_low, cotangent, sens, second_high, second_low]
    sources += [w_first_hbm, w_last_hbm, mask_hbm, *constants_hbm[4:]]
    targets += [w_first, w_last, mask, repeat, pick, place, repeat_back, pick_back, place_back]
    targets += [place_last, pick_last]
    loads = [
        pltpu.make_async_copy(source, target, load_sem.at[number])
        for number, (source, target) in enumerate(zip(sources, targets))
    ]
    for load in loads[:4]:
        load.start()

    near[...] = jnp.zeros_like(near)

    barrier = pltpu.get_barrier_semaphore()

    @pl.loop(1, PEERS)
    def _(step):
        pl.semaphore_signal(
            barrier, inc=1, device_id={"row": (row + step) % PEERS}, device_id_type=MESH
        )

    @pl.loop(1, REACH + 1)
    def _(step):
        for sign in (1, -1):
            pl.semaphore_signal(
                barrier,
                inc=1,
                device_id={"coil": (coil + sign * step) % COIL_PEERS},
                device_id_type=MESH,
            )

    for step, across in near_by:
        other_coil, other_row, there = neighbour(step)

        @pl.when(jnp.logical_and(owns, there))
        def _():
            pl.semaphore_signal(
                barrier,
                inc=1,
                device_id={
                    "coil": other_coil,
                    "slab": (slab + across) % 2,
                    "row": other_row,
                },
                device_id_type=MESH,
            )

    def spread_out(which):
        high, low = split(lines[...])
        both = dot(first_high[...], jnp.concatenate([high, low], axis=0), ((1,), (1,)))
        rest = dot(first_low[...], high, ((1,), (1,)))
        spread[which] = both[:, :128] + both[:, 128:] + rest

    def swap(which, step):
        peer = (row + step) % PEERS
        return pltpu.make_async_remote_copy(
            src_ref=spread.at[which, pl.ds(pl.multiple_of(peer * SENT, 8), SENT)],
            dst_ref=landed.at[which, row],
            send_sem=swap_send.at[which, peer],
            recv_sem=swap_recv.at[which, row],
            device_id={"row": peer},
            device_id_type=MESH,
        )

    def swap_start(which):
        @pl.loop(1, PEERS)
        def _(step):
            swap(which, step).start()

        landed[which, row] = spread[which, pl.ds(pl.multiple_of(row * SENT, 8), SENT), :]

    def swap_wait(which):
        @pl.loop(1, PEERS)
        def _(step):
            peer = (row + step) % PEERS
            pltpu.make_async_remote_copy(
                src_ref=spread.at[which, pl.ds(0, SENT)],
                dst_ref=landed.at[which, peer],
                send_sem=swap_send.at[which, peer],
                recv_sem=swap_recv.at[which, peer],
                device_id={"row": peer},
                device_id_type=MESH,
            ).wait_recv()

    lane = lax.broadcasted_iota(jnp.int32, (CELLS, 128), 1)

    def gather_in(which):
        for part in range(2):
            for four in range(PEERS // 4):
                blocks = [
                    landed[which, 4 * four + inner, part * CELLS : (part + 1) * CELLS, :]
                    for inner in range(4)
                ]
                for group in range(4):
                    tile = None
                    for inner in range(4):
                        turn = (inner - group) % 4 * GROUP
                        moved = pltpu.roll(blocks[inner], turn, 1) if turn else blocks[inner]
                        tile = moved if tile is None else jnp.where(lane >= GROUP * inner, moved, tile)
                    start = part * PEERS * GROUP + four * 128
                    wide[24 * group : 24 * group + CELLS, start : start + 128] = tile
        high, low = split(wide[...])
        both = dot(jnp.concatenate([high, low], axis=0), second_high[...])
        return both[:96] + both[96:] + dot(high, second_low[...])

    def halves(ref, group):
        lines_now = ref[group // 2, :, group % 2, :]
        tiles = [lines_now[:, 128 * tile : 128 * tile + 128] for tile in range(5)]
        low = lane < 64
        turned = [pltpu.roll(tile, 64, 1) for tile in tiles[2:]]
        zero = jnp.zeros_like(tiles[0])
        return (
            tiles[:2] + [jnp.where(low, tiles[2], zero)],
            [
                jnp.where(low, turned[0], turned[1]),
                jnp.where(low, turned[1], turned[2]),
                jnp.where(low, turned[2], zero),
            ],
        )

    def whole_lines(real, imag):
        low = lane < 64
        turned = [pltpu.roll(imag[:, 128 * tile : 128 * tile + 128], 64, 1) for tile in range(3)]
        tiles = [
            real[:, :128],
            real[:, 128:256],
            jnp.where(low, real[:, 256:], turned[0]),
            jnp.where(low, turned[0], turned[1]),
            jnp.where(low, turned[1], turned[2]),
        ]
        return jnp.concatenate(tiles, axis=1)

    def put_lines(ref):
        for group in range(4):
            for half, tiles in enumerate(halves(ref, group)):
                for number, tile in enumerate(tiles):
                    start = half * HALF + 128 * number
                    lines[GROUP * group : GROUP * group + CELLS, start : start + 128] = tile

    lines[...] = jnp.zeros_like(lines)
    loads[0].wait()
    put_lines(kspace)
    loads[1].wait()
    loads[2].wait()
    for load in loads[4:]:
        load.start()
    spread_out(0)

    near_count = jnp.int32(0)
    for step, across in near_by:
        near_count = near_count + jnp.where(jnp.logical_and(owns, neighbour(step)[2]), 1, 0)
    pl.semaphore_wait(barrier, PEERS - 1 + 2 * REACH + near_count)

    @pl.loop(1, REACH + 1)
    def _(step):
        for sign in (1, -1):
            pl.semaphore_signal(
                greet_far,
                inc=1,
                device_id={"coil": (coil + sign * step) % COIL_PEERS},
                device_id_type=MESH,
            )


    swap_start(0)
    loads[3].wait()
    put_lines(cotangent)
    spread_out(1)
    swap_start(1)

    wide[...] = jnp.zeros_like(wide)
    maps[...] = jnp.zeros_like(maps)
    loads[4].wait()
    for group in range(4):
        for half, tiles in enumerate(halves(sens, group)):
            for number, tile in enumerate(tiles):
                start = half * HALF + 128 * number
                maps[group, :CELLS, start : start + 128] = tile
    for load in loads[5:]:
        load.wait()
    weights = w_first[...].reshape(54, HID)
    weights_rows = exact_dot(repeat[...], weights, ((1,), (1,)))
    forward_matrix = jnp.zeros((HID * 4, 144), jnp.float32)
    for e2 in range(3):
        forward_matrix += place[e2] * exact_dot(weights_rows, pick[e2])
    weights_back = exact_dot(weights, repeat_back[...], ((1,), (1,)))
    backward_matrix = jnp.sum(
        (exact_dot(pick_back[...], weights_back) * place_back[...]).reshape(9, 16, 216), axis=0
    )
    last_columns = exact_dot(repeat[...], w_last[...], ((1,), (1,)))
    last_matrix = place_last[...] * exact_dot(
        pick_last[...], exact_dot(w_last[...], repeat[...], ((1,), (1,)))
    )

    def part_sums(which, total_field):
        for plane in range(2):
            real = imag = None
            for local_coil in range(2):
                group = local_coil * 2 + plane
                map_real, map_imag = maps[group, :, :HALF], maps[group, :, HALF:]
                field = total_field[24 * group : 24 * group + 24]
                field_real, field_imag = field[:, :HALF], field[:, HALF:]
                this_real = map_real * field_real + map_imag * field_imag
                this_imag = map_real * field_imag - map_imag * field_real
                real = this_real if real is None else real + this_real
                imag = this_imag if imag is None else imag + this_imag
            last = real[:, 256:] + pltpu.roll(imag[:, 256:], 64, 1)
            for target in range(OWNERS):
                cut = slice(2 * target, 2 * target + 2)
                for half in range(2):
                    lanes = slice(128 * half, 128 * half + 128)
                    at = 8 * half + 2 * plane
                    parts[which, target, at : at + 2, :] = real[cut, lanes]
                    parts[which, target, at + 4 : at + 6, :] = imag[cut, lanes]
                parts[which, target, 16 + 2 * plane : 18 + 2 * plane, :] = last[cut]

    def part_copy(which, target):
        return pltpu.make_async_remote_copy(
            src_ref=parts.at[which, target],
            dst_ref=sums.at[which, coil],
            send_sem=sum_send.at[which, target],
            recv_sem=sum_recv.at[which, coil],
            device_id={"coil": owner_coil(target, row)},
            device_id_type=MESH,
        )

    def part_start(which):
        @pl.loop(0, OWNERS)
        def _(step):
            target = (owner + step) % OWNERS

            @pl.when(owner_coil(target, row) != coil)
            def _():
                part_copy(which, target).start()

    def part_total(which):
        @pl.loop(1, COIL_PEERS)
        def _(step):
            peer = (coil + step) % COIL_PEERS
            pltpu.make_async_remote_copy(
                src_ref=parts.at[which, 0],
                dst_ref=sums.at[which, peer],
                send_sem=sum_send.at[which, 0],
                recv_sem=sum_recv.at[which, peer],
                device_id={"coil": peer},
                device_id_type=MESH,
            ).wait_recv()

        sums[which, coil] = parts[which, owner]
        total = sums[which, 0]
        for peer in range(1, COIL_PEERS):
            total = total + sums[which, peer]
        return unpack(total)

    def near_copy(which, step, across):
        other_coil, other_row, there = neighbour(step)
        copy = pltpu.make_async_remote_copy(
            src_ref=near.at[which, 1, slab],
            dst_ref=near.at[which, 1 - step, slab],
            send_sem=near_send.at[which, (step + 1) * 2 + across],
            recv_sem=near_recv.at[which, (1 - step) * 2 + across],
            device_id={"coil": other_coil, "slab": (slab + across) % 2, "row": other_row},
            device_id_type=MESH,
        )
        return copy, there

    def near_start(which):
        for step, across in near_by:
            copy, there = near_copy(which, step, across)
            pl.when(there)(copy.start)

    def near_wait(which):
        for step, across in near_by:
            other_coil, other_row, there = neighbour(step)
            copy = pltpu.make_async_remote_copy(
                src_ref=near.at[which, 1, slab],
                dst_ref=near.at[which, 1 + step, (slab + across) % 2],
                send_sem=near_send.at[which, (step + 1) * 2 + across],
                recv_sem=near_recv.at[which, (1 + step) * 2 + across],
                device_id={"coil": other_coil, "slab": (slab + across) % 2, "row": other_row},
                device_id_type=MESH,
            )
            pl.when(there)(copy.wait_recv)

    def put_piece(which, plane, values):
        for half in range(2):
            lanes = slice(128 * half, 128 * half + 128)
            at = 8 * half + 2 * plane
            pieces[which, owner, at : at + 2, :] = values[0:2, lanes]
            pieces[which, owner, at + 4 : at + 6, :] = values[2:4, lanes]
        low = lax.broadcasted_iota(jnp.int32, (2, 128), 1) < LEN - 256
        pieces[which, owner, 16 + 2 * plane : 18 + 2 * plane, :] = jnp.where(
            low, values[0:2, 256:], pltpu.roll(values[2:4, 256:], 64, 1)
        )

    def field_copy(which, step):
        peer = (coil + step) % COIL_PEERS
        return pltpu.make_async_remote_copy(
            src_ref=pieces.at[which, owner],
            dst_ref=pieces.at[which, owner],
            send_sem=field_send.at[which, peer],
            recv_sem=field_recv.at[which, owner],
            device_id={"coil": peer},
            device_id_type=MESH,
        )

    def field_start(which):
        @pl.loop(1, COIL_PEERS)
        def _(step):
            field_copy(which, step).start()

    def field_wait(which):
        @pl.loop(0, OWNERS)
        def _(target):
            @pl.when(owner_coil(target, row) != coil)
            def _():
                pltpu.make_async_remote_copy(
                    src_ref=pieces.at[which, target],
                    dst_ref=pieces.at[which, target],
                    send_sem=field_send.at[which, 0],
                    recv_sem=field_recv.at[which, target],
                    device_id={"coil": owner_coil(target, row)},
                    device_id_type=MESH,
                ).wait_recv()

        for target in range(OWNERS):
            cut = slice(2 * target, 2 * target + 2)
            for plane in range(2):
                for part in range(2):
                    for half in range(2):
                        at = 8 * half + 4 * part + 2 * plane
                        fields[which, part, plane, cut, 128 * half : 128 * half + 128] = pieces[
                            which, target, at : at + 2, :
                        ]
                last = pieces[which, target, 16 + 2 * plane : 18 + 2 * plane, :]
                fields[which, 0, plane, cut, 256:] = last
                fields[which, 1, plane, cut, 256:] = pltpu.roll(last, 64, 1)

    swap_wait(0)
    total_field = gather_in(0)
    images[0] = total_field
    part_sums(0, total_field)
    pl.semaphore_wait(greet_far, 2 * REACH)
    part_start(0)
    swap_wait(1)
    total_field = gather_in(1)
    images[1] = total_field
    part_sums(1, total_field)
    part_start(1)

    @pl.when(owns)
    def _():
        near[0, 1, slab] = part_total(0)
        near_start(0)
        shifted[...] = jnp.zeros_like(shifted)
        hidden[0] = jnp.zeros((HID * 4, HALF), jnp.float32)
        hidden[4] = jnp.zeros((HID * 4, HALF), jnp.float32)
        near_wait(0)
        for part in range(2):
            for side in range(2):
                for plane in range(2):
                    line = part * 4 + plane * 2
                    for step in range(3):
                        shifted[1, part, 1 + 2 * side + plane, 2 * step : 2 * step + 2, :] = near[
                            0, step, side, line : line + 2, :
                        ]
        middle = shifted[1].reshape(2 * 6 * 8, HALF)
        shifted[0] = pltpu.roll(middle, 1, 1).reshape(2, 6, 8, HALF)
        shifted[2] = pltpu.roll(middle, HALF - 1, 1).reshape(2, 6, 8, HALF)
        for plane in range(3):
            pre = dot3(
                forward_matrix,
                shifted[:, :, pl.ds(slab + plane, 3)].reshape(144, HALF),
            )
            sigmoid = 1.0 / (1.0 + jnp.exp(-pre))
            acts[plane] = pre * sigmoid
            hidden[plane + 1] = sigmoid * (1.0 + pre * (1.0 - sigmoid))
        for plane in range(2):
            put_piece(0, plane, dot3(last_matrix, acts[slab + plane]))
        field_start(0)
        near[1, 1, slab] = part_total(1)
        near_start(1)
        near_wait(1)
        for part in range(2):
            for side in range(2):
                for plane in range(2):
                    line = part * 4 + plane * 2
                    for again in (0, 4):
                        cot_rows[part, 2 * side + plane, again : again + 1, :] = near[
                            1, 0, side, line + 1 : line + 2, :
                        ]
                        cot_rows[part, 2 * side + plane, again + 1 : again + 3, :] = near[
                            1, 1, side, line : line + 2, :
                        ]
                        cot_rows[part, 2 * side + plane, again + 3 : again + 4, :] = near[
                            1, 2, side, line : line + 1, :
                        ]
        for plane in range(3):
            real = jnp.broadcast_to(cot_rows[0, slab + plane][None], (9, 8, HALF))
            imag = jnp.broadcast_to(cot_rows[1, slab + plane][None], (9, 8, HALF))
            spread_cot = last_columns[:, 0:1] * real.reshape(HID * 4, HALF) + last_columns[
                :, 1:2
            ] * imag.reshape(HID * 4, HALF)
            hidden[plane + 1] = hidden[plane + 1] * spread_cot
        for plane in range(2):
            back = dot3(
                backward_matrix, hidden[pl.ds(slab + plane, 3)].reshape(3 * HID * 4, HALF)
            )
            back = (
                pltpu.roll(back[0:4], HALF - 1, 1) + back[4:8] + pltpu.roll(back[8:12], 1, 1)
            )
            put_piece(1, plane, back)
        field_start(1)

    field_wait(0)
    for group in range(4):
        plane = group % 2
        other_real, other_imag = fields[0, 0, plane, :CELLS], fields[0, 1, plane, :CELLS]
        field = images[1, 24 * group : 24 * group + CELLS, :]
        real, imag = field[:, :HALF], field[:, HALF:]
        out_real = -(real * other_real + imag * other_imag)
        out_imag = real * other_imag - imag * other_real
        half_done[group, :CELLS, :HALF] = out_real
        half_done[group, :CELLS, HALF:] = out_imag
    field_wait(1)
    for group in range(4):
        plane = group % 2
        other_real, other_imag = fields[1, 0, plane, :CELLS], fields[1, 1, plane, :CELLS]
        real, imag = maps[group, :CELLS, :HALF], maps[group, :CELLS, HALF:]
        lines[GROUP * group : GROUP * group + CELLS, :HALF] = real * other_real - imag * other_imag
        lines[GROUP * group : GROUP * group + CELLS, HALF:] = -(
            real * other_imag + imag * other_real
        )
    spread_out(2)
    swap_start(2)
    for group in range(4):
        plane = group % 2
        other_real, other_imag = fields[1, 0, plane, :CELLS], fields[1, 1, plane, :CELLS]
        field = images[0, 24 * group : 24 * group + CELLS, :]
        real, imag = field[:, :HALF], field[:, HALF:]
        out_real = -(real * other_real + imag * other_imag)
        out_imag = real * other_imag - imag * other_real
        out_real = out_real + half_done[group, :CELLS, :HALF]
        out_imag = out_imag + half_done[group, :CELLS, HALF:]
        grad_sens[group // 2, :, plane, :] = whole_lines(out_real, out_imag)
    stores = [
        pltpu.make_async_copy(grad_sens, grad_sens_hbm, store_sem.at[0]),
        pltpu.make_async_copy(grad_kspace, grad_kspace_hbm, store_sem.at[1]),
    ]
    stores[0].start()
    square_row = lax.broadcasted_iota(jnp.int32, (CELLS, CELLS), 0)
    square_column = lax.broadcasted_iota(jnp.int32, (CELLS, CELLS), 1)
    factors = []
    for plane in range(2):
        sampled = jnp.broadcast_to(mask[plane : plane + 1, :].astype(jnp.float32), (CELLS, CELLS))
        column = jnp.sum(
            jnp.where(square_row == square_column, sampled, 0.0), axis=1, keepdims=True
        )
        factors.append(1.0 - eta[0] * column)
    swap_wait(2)
    model = gather_in(2)
    for group in range(4):
        plane = group % 2
        mine = model[24 * group : 24 * group + CELLS]
        grad_kspace[group // 2, :, plane, :] = factors[plane] * cotangent[
            group // 2, :, plane, :
        ] - whole_lines(mine[:, :HALF], -mine[:, HALF:])
    stores[1].start()

    for which in range(3):

        @pl.loop(1, PEERS)
        def _(step):
            swap(which, step).wait_send()

    for which in range(2):

        @pl.loop(0, OWNERS)
        def _(target):
            @pl.when(owner_coil(target, row) != coil)
            def _():
                part_copy(which, target).wait_send()

        @pl.when(owns)
        def _():
            for step, across in near_by:
                copy, there = near_copy(which, step, across)
                pl.when(there)(copy.wait_send)

            @pl.loop(1, COIL_PEERS)
            def _(step):
                field_copy(which, step).wait_send()
    stores[0].wait()
    stores[1].wait()


def hand_on(first, second, first_out, second_out, sems):
    copies = [
        pltpu.make_async_copy(first, first_out, sems.at[0]),
        pltpu.make_async_copy(second, second_out, sems.at[1]),
    ]
    for copy in copies:
        copy.start()
    for copy in copies:
        copy.wait()


def local(kspace, cotangent, sens, mask, eta, w_first, w_last):
    constants = [jnp.asarray(array) for array in tables() + selectors()]
    smem = pl.BlockSpec(memory_space=pltpu.SMEM)
    anywhere = pl.BlockSpec(memory_space=pl.ANY)
    f32, b16 = jnp.float32, jnp.bfloat16
    rows = jax.ShapeDtypeStruct((2, CELLS, 2, 2 * LEN), f32)
    results = pl.pallas_call(
        kernel,
        out_shape=(rows, rows),
        in_specs=[anywhere] * 4 + [smem] + [anywhere] * 14,
        out_specs=(anywhere, anywhere),
        scratch_shapes=[
            pltpu.VMEM(rows.shape, f32),
            pltpu.VMEM(rows.shape, f32),
            pltpu.VMEM(rows.shape, f32),
            pltpu.VMEM(mask.shape, jnp.int32),
            pltpu.VMEM((27, 2, HID), f32),
            pltpu.VMEM(w_last.shape, f32),
            *[pltpu.VMEM(array.shape, array.dtype) for array in constants],
            pltpu.VMEM(rows.shape, f32),
            pltpu.VMEM(rows.shape, f32),
            pltpu.VMEM((4 * GROUP, WIDE), f32),
            pltpu.VMEM((3, PEERS * SENT, 128), f32),
            pltpu.VMEM((3, PEERS, SENT, 128), f32),
            pltpu.VMEM((96, 2 * PEERS * GROUP), f32),
            pltpu.VMEM((2, 96, WIDE), f32),
            pltpu.VMEM((4, 24, WIDE), f32),
            pltpu.VMEM((2, OWNERS, 20, 128), f32),
            pltpu.VMEM((2, COIL_PEERS, 20, 128), f32),
            pltpu.VMEM((2, 3, 2, 8, HALF), f32),
            pltpu.VMEM((3, 2, 6, 8, HALF), f32),
            pltpu.VMEM((2, 4, 8, HALF), f32),
            pltpu.VMEM((3, HID * 4, HALF), f32),
            pltpu.VMEM((5, HID * 4, HALF), f32),
            pltpu.VMEM((2, OWNERS, 20, 128), f32),
            pltpu.VMEM((2, 2, 2, 24, HALF), f32),
            pltpu.VMEM((4, 24, WIDE), f32),
            pltpu.SemaphoreType.DMA((18,)),
            pltpu.SemaphoreType.DMA((2,)),
            pltpu.SemaphoreType.DMA((3, PEERS)),
            pltpu.SemaphoreType.DMA((3, PEERS)),
            pltpu.SemaphoreType.DMA((2, OWNERS)),
            pltpu.SemaphoreType.DMA((2, COIL_PEERS)),
            pltpu.SemaphoreType.DMA((2, 6)),
            pltpu.SemaphoreType.DMA((2, 6)),
            pltpu.SemaphoreType.DMA((2, COIL_PEERS)),
            pltpu.SemaphoreType.DMA((2, OWNERS)),
            pltpu.SemaphoreType.REGULAR,
        ],
        compiler_params=pltpu.CompilerParams(
            collective_id=0, has_side_effects=True, vmem_limit_bytes=62 * 1024 * 1024
        ),
    )(
        kspace.transpose(0, 2, 1, 3),
        cotangent.transpose(0, 2, 1, 3),
        sens.transpose(0, 2, 1, 3),
        mask,
        eta,
        w_first.transpose(2, 3, 4, 1, 0).reshape(27, 2, HID),
        w_last,
        *constants,
    )
    results = pl.pallas_call(
        hand_on,
        out_shape=(rows, rows),
        in_specs=[anywhere] * 2,
        out_specs=(anywhere, anywhere),
        scratch_shapes=[pltpu.SemaphoreType.DMA((2,))],
        compiler_params=pltpu.CompilerParams(vmem_limit_bytes=62 * 1024 * 1024),
    )(*results)
    return tuple(result.transpose(0, 2, 1, 3) for result in results)


def solution(mesh):
    part = P("coil", "slab", "row", None)
    return jax.shard_map(
        local,
        mesh=mesh,
        in_specs=(part, part, part, P("slab", "row"), P(), P(), P()),
        out_specs=(part, part),
        check_vma=False,
    )
```

```python
import math

import jax
import jax.numpy as jnp
import ml_dtypes
import numpy as np
from jax import lax
from jax.experimental import pallas as pl
from jax.experimental.pallas import tpu as pltpu
from jax.sharding import PartitionSpec as P

MESH = pl.DeviceIdType.MESH
LEN = 320
HALF = 384
WIDE = 2 * HALF
CELLS = 20
GROUP = 32
PEERS = 16
COIL_PEERS = 16
SENT = 2 * CELLS
REACH = 4
OWNERS = 10
HID = 18


def turned(owner, row):
    return owner + (row % 2) * (OWNERS - 1 - 2 * owner)


def owner_coil(owner, row):
    return (8 * turned(owner, row)) // 5


def coil_owner(coil, row):
    return turned((5 * coil + 7) // 8, row)


def split_table(table):
    high = table.astype(ml_dtypes.bfloat16)
    low = (table - high.astype(np.float64)).astype(ml_dtypes.bfloat16)
    return high, low


def tables():
    at = np.arange(LEN)
    angle = 2.0 * math.pi * ((at[:, None] * at[None, :]) % LEN) / LEN
    cosine, sine = np.cos(angle) / math.sqrt(LEN), np.sin(angle) / math.sqrt(LEN)
    mix = np.zeros((2, LEN, 2, LEN))
    mix[0, :, 0], mix[0, :, 1], mix[1, :, 0], mix[1, :, 1] = cosine, -sine, sine, cosine
    first = np.zeros((PEERS, 2, CELLS, 2, HALF))
    first[..., :LEN] = mix.reshape(2, PEERS, CELLS, 2, LEN).transpose(1, 0, 2, 3, 4)
    second = np.zeros((2, PEERS, GROUP, 2, HALF))
    second[:, :, :CELLS, :, :LEN] = mix.transpose(2, 3, 0, 1).reshape(2, PEERS, CELLS, 2, LEN)
    return split_table(first.reshape(PEERS * SENT, WIDE)) + split_table(
        second.reshape(2 * PEERS * GROUP, WIDE)
    )


def selectors():
    repeat = np.zeros((HID * 4, HID), np.float32)
    for unit in range(HID):
        repeat[4 * unit : 4 * unit + 4, unit] = 1.0
    pick = np.zeros((3, 54, 144), np.float32)
    place = np.zeros((3, HID * 4, 144), np.float32)
    for column in range(144):
        e3, channel, e1, row = column // 48, column // 24 % 2, column // 8 % 3, column % 8
        for e2 in range(3):
            pick[e2, 2 * (e1 * 9 + e2 * 3 + e3) + channel, column] = 1.0
            for line in range(HID * 4):
                if row - line % 4 == e2:
                    place[e2, line, column] = 1.0
    repeat_back = np.concatenate([repeat] * 3, axis=0)
    pick_back = np.zeros((9, 16, 54), np.float32)
    place_back = np.zeros((9, 16, 216), np.float32)
    for plane in range(3):
        for e2 in range(3):
            for line in range(12):
                e3, channel, row = line // 4, line // 2 % 2, line % 2
                pick_back[plane * 3 + e2, line, 2 * ((2 - plane) * 9 + e2 * 3 + e3) + channel] = 1.0
                for column in range(216):
                    if column // 72 == plane and row + 2 - column % 4 == e2:
                        place_back[plane * 3 + e2, line, column] = 1.0
    place_last = np.zeros((8, HID * 4), np.float32)
    pick_last = np.zeros((8, 2), np.float32)
    for line in range(4):
        pick_last[line, line // 2] = 1.0
        for column in range(HID * 4):
            if column % 4 == line % 2 + 1:
                place_last[line, column] = 1.0
    return (
        repeat,
        pick,
        place,
        repeat_back,
        pick_back.reshape(144, 54),
        place_back.reshape(144, 216),
        place_last,
        pick_last,
    )


def unpack(packed):
    low = lax.broadcasted_iota(jnp.int32, (4, 128), 1) < LEN - 256
    last = packed[16:20]
    upper = jnp.where(low, last, 0.0)
    lower = jnp.where(low, pltpu.roll(last, 64, 1), 0.0)
    return jnp.concatenate(
        [packed[0:8], packed[8:16], jnp.concatenate([upper, lower], axis=0)], axis=1
    )


def split(values):
    high = values.astype(jnp.bfloat16)
    return high, (values - high.astype(jnp.float32)).astype(jnp.bfloat16)


def dot(left, right, dims=((1,), (0,))):
    return lax.dot_general(left, right, (dims, ((), ())), preferred_element_type=jnp.float32)


def dot3(left, right):
    left_high, left_low = split(left)
    right_high, right_low = split(right)
    return dot(left_high, right_high) + dot(left_low, right_high) + dot(left_high, right_low)


def exact_dot(left, right, dims=((1,), (0,))):
    return lax.dot_general(
        left,
        right,
        (dims, ((), ())),
        precision=lax.Precision.HIGHEST,
        preferred_element_type=jnp.float32,
    )


def kernel(*refs):
    (
        kspace_hbm,
        cotangent_hbm,
        sens_hbm,
        mask_hbm,
        eta,
        w_first_hbm,
        w_last_hbm,
        *constants_hbm,
    ) = refs[:19]
    grad_kspace_hbm, grad_sens_hbm = refs[19:21]
    (
        kspace,
        cotangent,
        sens,
        mask,
        w_first,
        w_last,
        first_high,
        first_low,
        second_high,
        second_low,
        repeat,
        pick,
        place,
        repeat_back,
        pick_back,
        place_back,
        place_last,
        pick_last,
        grad_kspace,
        grad_sens,
        lines,
        spread,
        landed,
        wide,
        images,
        maps,
        parts,
        sums,
        near,
        shifted,
        cot_rows,
        acts,
        hidden,
        pieces,
        fields,
        load_sem,
        store_sem,
        swap_send,
        swap_recv,
        sum_send,
        sum_recv,
        near_send,
        near_recv,
        field_send,
        field_recv,
        greet_far,
    ) = refs[21:]
    coil, slab, row = lax.axis_index("coil"), lax.axis_index("slab"), lax.axis_index("row")
    owner = coil_owner(coil, row)
    owns = owner_coil(owner, row) == coil

    def neighbour(step):
        other = owner + step
        other_row = row + jnp.where(other < 0, -1, 0) + jnp.where(other >= OWNERS, 1, 0)
        there = jnp.logical_and(other_row >= 0, other_row < PEERS)
        return owner_coil((other + OWNERS) % OWNERS, other_row), other_row, there

    near_by = [
        (step, across) for step in (-1, 0, 1) for across in (0, 1) if (step, across) != (0, 0)
    ]

    sources = [kspace_hbm, *constants_hbm[:2], cotangent_hbm, sens_hbm, *constants_hbm[2:4]]
    targets = [kspace, first_high, first_low, cotangent, sens, second_high, second_low]
    sources += [w_first_hbm, w_last_hbm, mask_hbm, *constants_hbm[4:]]
    targets += [w_first, w_last, mask, repeat, pick, place, repeat_back, pick_back, place_back]
    targets += [place_last, pick_last]
    loads = [
        pltpu.make_async_copy(source, target, load_sem.at[number])
        for number, (source, target) in enumerate(zip(sources, targets))
    ]
    for load in loads[:4]:
        load.start()

    near[...] = jnp.zeros_like(near)

    barrier = pltpu.get_barrier_semaphore()

    @pl.loop(1, PEERS)
    def _(step):
        pl.semaphore_signal(
            barrier, inc=1, device_id={"row": (row + step) % PEERS}, device_id_type=MESH
        )

    @pl.loop(1, REACH + 1)
    def _(step):
        for sign in (1, -1):
            pl.semaphore_signal(
                barrier,
                inc=1,
                device_id={"coil": (coil + sign * step) % COIL_PEERS},
                device_id_type=MESH,
            )

    for step, across in near_by:
        other_coil, other_row, there = neighbour(step)

        @pl.when(jnp.logical_and(owns, there))
        def _():
            pl.semaphore_signal(
                barrier,
                inc=1,
                device_id={
                    "coil": other_coil,
                    "slab": (slab + across) % 2,
                    "row": other_row,
                },
                device_id_type=MESH,
            )

    def spread_out(which):
        high, low = split(lines[...])
        both = dot(first_high[...], jnp.concatenate([high, low], axis=0), ((1,), (1,)))
        rest = dot(first_low[...], high, ((1,), (1,)))
        spread[which] = both[:, :128] + both[:, 128:] + rest

    def swap(which, step):
        peer = (row + step) % PEERS
        return pltpu.make_async_remote_copy(
            src_ref=spread.at[which, pl.ds(pl.multiple_of(peer * SENT, 8), SENT)],
            dst_ref=landed.at[which, row],
            send_sem=swap_send.at[which, peer],
            recv_sem=swap_recv.at[which, row],
            device_id={"row": peer},
            device_id_type=MESH,
        )

    def swap_start(which):
        @pl.loop(1, PEERS)
        def _(step):
            swap(which, step).start()

        landed[which, row] = spread[which, pl.ds(pl.multiple_of(row * SENT, 8), SENT), :]

    def swap_wait(which):
        @pl.loop(1, PEERS)
        def _(step):
            peer = (row + step) % PEERS
            pltpu.make_async_remote_copy(
                src_ref=spread.at[which, pl.ds(0, SENT)],
                dst_ref=landed.at[which, peer],
                send_sem=swap_send.at[which, peer],
                recv_sem=swap_recv.at[which, peer],
                device_id={"row": peer},
                device_id_type=MESH,
            ).wait_recv()

    lane = lax.broadcasted_iota(jnp.int32, (CELLS, 128), 1)

    def gather_in(which):
        for part in range(2):
            for four in range(PEERS // 4):
                blocks = [
                    landed[which, 4 * four + inner, part * CELLS : (part + 1) * CELLS, :]
                    for inner in range(4)
                ]
                for group in range(4):
                    tile = None
                    for inner in range(4):
                        turn = (inner - group) % 4 * GROUP
                        moved = pltpu.roll(blocks[inner], turn, 1) if turn else blocks[inner]
                        tile = moved if tile is None else jnp.where(lane >= GROUP * inner, moved, tile)
                    start = part * PEERS * GROUP + four * 128
                    wide[24 * group : 24 * group + CELLS, start : start + 128] = tile
        high, low = split(wide[...])
        both = dot(jnp.concatenate([high, low], axis=0), second_high[...])
        return both[:96] + both[96:] + dot(high, second_low[...])

    def halves(ref, group):
        lines_now = ref[group // 2, :, group % 2, :]
        tiles = [lines_now[:, 128 * tile : 128 * tile + 128] for tile in range(5)]
        low = lane < 64
        turned = [pltpu.roll(tile, 64, 1) for tile in tiles[2:]]
        zero = jnp.zeros_like(tiles[0])
        return (
            tiles[:2] + [jnp.where(low, tiles[2], zero)],
            [
                jnp.where(low, turned[0], turned[1]),
                jnp.where(low, turned[1], turned[2]),
                jnp.where(low, turned[2], zero),
            ],
        )

    def whole_lines(real, imag):
        low = lane < 64
        turned = [pltpu.roll(imag[:, 128 * tile : 128 * tile + 128], 64, 1) for tile in range(3)]
        tiles = [
            real[:, :128],
            real[:, 128:256],
            jnp.where(low, real[:, 256:], turned[0]),
            jnp.where(low, turned[0], turned[1]),
            jnp.where(low, turned[1], turned[2]),
        ]
        return jnp.concatenate(tiles, axis=1)

    def put_lines(ref):
        for group in range(4):
            for half, tiles in enumerate(halves(ref, group)):
                for number, tile in enumerate(tiles):
                    start = half * HALF + 128 * number
                    lines[GROUP * group : GROUP * group + CELLS, start : start + 128] = tile

    lines[...] = jnp.zeros_like(lines)
    loads[0].wait()
    put_lines(kspace)
    loads[1].wait()
    loads[2].wait()
    for load in loads[4:]:
        load.start()
    spread_out(0)

    near_count = jnp.int32(0)
    for step, across in near_by:
        near_count = near_count + jnp.where(jnp.logical_and(owns, neighbour(step)[2]), 1, 0)
    pl.semaphore_wait(barrier, PEERS - 1 + 2 * REACH + near_count)

    @pl.loop(1, REACH + 1)
    def _(step):
        for sign in (1, -1):
            pl.semaphore_signal(
                greet_far,
                inc=1,
                device_id={"coil": (coil + sign * step) % COIL_PEERS},
                device_id_type=MESH,
            )


    swap_start(0)
    loads[3].wait()
    put_lines(cotangent)
    spread_out(1)
    swap_start(1)

    wide[...] = jnp.zeros_like(wide)
    maps[...] = jnp.zeros_like(maps)
    loads[4].wait()
    for group in range(4):
        for half, tiles in enumerate(halves(sens, group)):
            for number, tile in enumerate(tiles):
                start = half * HALF + 128 * number
                maps[group, :CELLS, start : start + 128] = tile
    for load in loads[5:]:
        load.wait()
    weights = w_first[...].reshape(54, HID)
    weights_rows = exact_dot(repeat[...], weights, ((1,), (1,)))
    forward_matrix = jnp.zeros((HID * 4, 144), jnp.float32)
    for e2 in range(3):
        forward_matrix += place[e2] * exact_dot(weights_rows, pick[e2])
    weights_back = exact_dot(weights, repeat_back[...], ((1,), (1,)))
    backward_matrix = jnp.sum(
        (exact_dot(pick_back[...], weights_back) * place_back[...]).reshape(9, 16, 216), axis=0
    )
    last_columns = exact_dot(repeat[...], w_last[...], ((1,), (1,)))
    last_matrix = place_last[...] * exact_dot(
        pick_last[...], exact_dot(w_last[...], repeat[...], ((1,), (1,)))
    )

    def part_sums(which, total_field):
        for plane in range(2):
            real = imag = None
            for local_coil in range(2):
                group = local_coil * 2 + plane
                map_real, map_imag = maps[group, :, :HALF], maps[group, :, HALF:]
                field = total_field[24 * group : 24 * group + 24]
                field_real, field_imag = field[:, :HALF], field[:, HALF:]
                this_real = map_real * field_real + map_imag * field_imag
                this_imag = map_real * field_imag - map_imag * field_real
                real = this_real if real is None else real + this_real
                imag = this_imag if imag is None else imag + this_imag
            last = real[:, 256:] + pltpu.roll(imag[:, 256:], 64, 1)
            for target in range(OWNERS):
                cut = slice(2 * target, 2 * target + 2)
                for half in range(2):
                    lanes = slice(128 * half, 128 * half + 128)
                    at = 8 * half + 2 * plane
                    parts[which, target, at : at + 2, :] = real[cut, lanes]
                    parts[which, target, at + 4 : at + 6, :] = imag[cut, lanes]
                parts[which, target, 16 + 2 * plane : 18 + 2 * plane, :] = last[cut]

    def part_copy(which, target):
        return pltpu.make_async_remote_copy(
            src_ref=parts.at[which, target],
            dst_ref=sums.at[which, coil],
            send_sem=sum_send.at[which, target],
            recv_sem=sum_recv.at[which, coil],
            device_id={"coil": owner_coil(target, row)},
            device_id_type=MESH,
        )

    def part_start(which):
        @pl.loop(0, OWNERS)
        def _(step):
            target = (owner + step) % OWNERS

            @pl.when(owner_coil(target, row) != coil)
            def _():
                part_copy(which, target).start()

    def part_total(which):
        @pl.loop(1, COIL_PEERS)
        def _(step):
            peer = (coil + step) % COIL_PEERS
            pltpu.make_async_remote_copy(
                src_ref=parts.at[which, 0],
                dst_ref=sums.at[which, peer],
                send_sem=sum_send.at[which, 0],
                recv_sem=sum_recv.at[which, peer],
                device_id={"coil": peer},
                device_id_type=MESH,
            ).wait_recv()

        sums[which, coil] = parts[which, owner]
        total = sums[which, 0]
        for peer in range(1, COIL_PEERS):
            total = total + sums[which, peer]
        return unpack(total)

    def near_copy(which, step, across):
        other_coil, other_row, there = neighbour(step)
        copy = pltpu.make_async_remote_copy(
            src_ref=near.at[which, 1, slab],
            dst_ref=near.at[which, 1 - step, slab],
            send_sem=near_send.at[which, (step + 1) * 2 + across],
            recv_sem=near_recv.at[which, (1 - step) * 2 + across],
            device_id={"coil": other_coil, "slab": (slab + across) % 2, "row": other_row},
            device_id_type=MESH,
        )
        return copy, there

    def near_start(which):
        for step, across in near_by:
            copy, there = near_copy(which, step, across)
            pl.when(there)(copy.start)

    def near_wait(which):
        for step, across in near_by:
            other_coil, other_row, there = neighbour(step)
            copy = pltpu.make_async_remote_copy(
                src_ref=near.at[which, 1, slab],
                dst_ref=near.at[which, 1 + step, (slab + across) % 2],
                send_sem=near_send.at[which, (step + 1) * 2 + across],
                recv_sem=near_recv.at[which, (1 + step) * 2 + across],
                device_id={"coil": other_coil, "slab": (slab + across) % 2, "row": other_row},
                device_id_type=MESH,
            )
            pl.when(there)(copy.wait_recv)

    def put_piece(which, plane, values):
        for half in range(2):
            lanes = slice(128 * half, 128 * half + 128)
            at = 8 * half + 2 * plane
            pieces[which, owner, at : at + 2, :] = values[0:2, lanes]
            pieces[which, owner, at + 4 : at + 6, :] = values[2:4, lanes]
        low = lax.broadcasted_iota(jnp.int32, (2, 128), 1) < LEN - 256
        pieces[which, owner, 16 + 2 * plane : 18 + 2 * plane, :] = jnp.where(
            low, values[0:2, 256:], pltpu.roll(values[2:4, 256:], 64, 1)
        )

    def field_copy(which, step):
        peer = (coil + step) % COIL_PEERS
        return pltpu.make_async_remote_copy(
            src_ref=pieces.at[which, owner],
            dst_ref=pieces.at[which, owner],
            send_sem=field_send.at[which, peer],
            recv_sem=field_recv.at[which, owner],
            device_id={"coil": peer},
            device_id_type=MESH,
        )

    def field_start(which):
        @pl.loop(1, COIL_PEERS)
        def _(step):
            field_copy(which, step).start()

    def field_wait(which):
        @pl.loop(0, OWNERS)
        def _(target):
            @pl.when(owner_coil(target, row) != coil)
            def _():
                pltpu.make_async_remote_copy(
                    src_ref=pieces.at[which, target],
                    dst_ref=pieces.at[which, target],
                    send_sem=field_send.at[which, 0],
                    recv_sem=field_recv.at[which, target],
                    device_id={"coil": owner_coil(target, row)},
                    device_id_type=MESH,
                ).wait_recv()

        for target in range(OWNERS):
            cut = slice(2 * target, 2 * target + 2)
            for plane in range(2):
                for part in range(2):
                    for half in range(2):
                        at = 8 * half + 4 * part + 2 * plane
                        fields[which, part, plane, cut, 128 * half : 128 * half + 128] = pieces[
                            which, target, at : at + 2, :
                        ]
                last = pieces[which, target, 16 + 2 * plane : 18 + 2 * plane, :]
                fields[which, 0, plane, cut, 256:] = last
                fields[which, 1, plane, cut, 256:] = pltpu.roll(last, 64, 1)

    swap_wait(0)
    total_field = gather_in(0)
    images[0] = total_field
    part_sums(0, total_field)
    pl.semaphore_wait(greet_far, 2 * REACH)
    part_start(0)
    swap_wait(1)
    total_field = gather_in(1)
    images[1] = total_field
    part_sums(1, total_field)
    part_start(1)

    @pl.when(owns)
    def _():
        near[0, 1, slab] = part_total(0)
        near_start(0)
        shifted[...] = jnp.zeros_like(shifted)
        hidden[0] = jnp.zeros((HID * 4, HALF), jnp.float32)
        hidden[4] = jnp.zeros((HID * 4, HALF), jnp.float32)
        near_wait(0)
        for part in range(2):
            for side in range(2):
                for plane in range(2):
                    line = part * 4 + plane * 2
                    for step in range(3):
                        shifted[1, part, 1 + 2 * side + plane, 2 * step : 2 * step + 2, :] = near[
                            0, step, side, line : line + 2, :
                        ]
        middle = shifted[1].reshape(2 * 6 * 8, HALF)
        shifted[0] = pltpu.roll(middle, 1, 1).reshape(2, 6, 8, HALF)
        shifted[2] = pltpu.roll(middle, HALF - 1, 1).reshape(2, 6, 8, HALF)
        for plane in range(3):
            pre = dot3(
                forward_matrix,
                shifted[:, :, pl.ds(slab + plane, 3)].reshape(144, HALF),
            )
            sigmoid = 1.0 / (1.0 + jnp.exp(-pre))
            acts[plane] = pre * sigmoid
            hidden[plane + 1] = sigmoid * (1.0 + pre * (1.0 - sigmoid))
        near[1, 1, slab] = part_total(1)
        near_start(1)
        for plane in range(2):
            put_piece(0, plane, dot3(last_matrix, acts[slab + plane]))
        near_wait(1)
        for part in range(2):
            for side in range(2):
                for plane in range(2):
                    line = part * 4 + plane * 2
                    for again in (0, 4):
                        cot_rows[part, 2 * side + plane, again : again + 1, :] = near[
                            1, 0, side, line + 1 : line + 2, :
                        ]
                        cot_rows[part, 2 * side + plane, again + 1 : again + 3, :] = near[
                            1, 1, side, line : line + 2, :
                        ]
                        cot_rows[part, 2 * side + plane, again + 3 : again + 4, :] = near[
                            1, 2, side, line : line + 1, :
                        ]
        for plane in range(3):
            real = jnp.broadcast_to(cot_rows[0, slab + plane][None], (9, 8, HALF))
            imag = jnp.broadcast_to(cot_rows[1, slab + plane][None], (9, 8, HALF))
            spread_cot = last_columns[:, 0:1] * real.reshape(HID * 4, HALF) + last_columns[
                :, 1:2
            ] * imag.reshape(HID * 4, HALF)
            hidden[plane + 1] = hidden[plane + 1] * spread_cot
        for plane in range(2):
            back = dot3(
                backward_matrix, hidden[pl.ds(slab + plane, 3)].reshape(3 * HID * 4, HALF)
            )
            back = (
                pltpu.roll(back[0:4], HALF - 1, 1) + back[4:8] + pltpu.roll(back[8:12], 1, 1)
            )
            put_piece(1, plane, back)
        field_start(1)
        field_start(0)

    field_wait(1)
    for group in range(4):
        plane = group % 2
        other_real, other_imag = fields[1, 0, plane, :CELLS], fields[1, 1, plane, :CELLS]
        real, imag = maps[group, :CELLS, :HALF], maps[group, :CELLS, HALF:]
        lines[GROUP * group : GROUP * group + CELLS, :HALF] = real * other_real - imag * other_imag
        lines[GROUP * group : GROUP * group + CELLS, HALF:] = -(
            real * other_imag + imag * other_real
        )
    spread_out(2)
    swap_start(2)
    field_wait(0)
    for group in range(4):
        plane = group % 2
        at = slice(24 * group, 24 * group + CELLS)
        out_real = out_imag = None
        for which in range(2):
            other_real, other_imag = fields[which, 0, plane, :CELLS], fields[which, 1, plane, :CELLS]
            real, imag = images[1 - which, at, :HALF], images[1 - which, at, HALF:]
            this_real = -(real * other_real + imag * other_imag)
            this_imag = real * other_imag - imag * other_real
            out_real = this_real if out_real is None else out_real + this_real
            out_imag = this_imag if out_imag is None else out_imag + this_imag
        grad_sens[group // 2, :, plane, :] = whole_lines(out_real, out_imag)
    stores = [
        pltpu.make_async_copy(grad_sens, grad_sens_hbm, store_sem.at[0]),
        pltpu.make_async_copy(grad_kspace, grad_kspace_hbm, store_sem.at[1]),
    ]
    stores[0].start()
    square_row = lax.broadcasted_iota(jnp.int32, (CELLS, CELLS), 0)
    square_column = lax.broadcasted_iota(jnp.int32, (CELLS, CELLS), 1)
    factors = []
    for plane in range(2):
        sampled = jnp.broadcast_to(mask[plane : plane + 1, :].astype(jnp.float32), (CELLS, CELLS))
        column = jnp.sum(
            jnp.where(square_row == square_column, sampled, 0.0), axis=1, keepdims=True
        )
        factors.append(1.0 - eta[0] * column)
    swap_wait(2)
    model = gather_in(2)
    for group in range(4):
        plane = group % 2
        mine = model[24 * group : 24 * group + CELLS]
        grad_kspace[group // 2, :, plane, :] = factors[plane] * cotangent[
            group // 2, :, plane, :
        ] - whole_lines(mine[:, :HALF], -mine[:, HALF:])
    stores[1].start()

    for which in range(3):

        @pl.loop(1, PEERS)
        def _(step):
            swap(which, step).wait_send()

    for which in range(2):

        @pl.loop(0, OWNERS)
        def _(target):
            @pl.when(owner_coil(target, row) != coil)
            def _():
                part_copy(which, target).wait_send()

        @pl.when(owns)
        def _():
            for step, across in near_by:
                copy, there = near_copy(which, step, across)
                pl.when(there)(copy.wait_send)

            @pl.loop(1, COIL_PEERS)
            def _(step):
                field_copy(which, step).wait_send()
    stores[0].wait()
    stores[1].wait()


def hand_on(first, second, first_out, second_out, first_held, second_held, sems):
    loads = [
        pltpu.make_async_copy(first, first_held, sems.at[0]),
        pltpu.make_async_copy(second, second_held, sems.at[1]),
    ]
    stores = [
        pltpu.make_async_copy(first_held, first_out, sems.at[2]),
        pltpu.make_async_copy(second_held, second_out, sems.at[3]),
    ]
    for load in loads:
        load.start()
    for load, store in zip(loads, stores):
        load.wait()
        store.start()
    for store in stores:
        store.wait()


def local(kspace, cotangent, sens, mask, eta, w_first, w_last):
    constants = [jnp.asarray(array) for array in tables() + selectors()]
    smem = pl.BlockSpec(memory_space=pltpu.SMEM)
    anywhere = pl.BlockSpec(memory_space=pl.ANY)
    f32, b16 = jnp.float32, jnp.bfloat16
    rows = jax.ShapeDtypeStruct((2, CELLS, 2, 2 * LEN), f32)
    results = pl.pallas_call(
        kernel,
        out_shape=(rows, rows),
        in_specs=[anywhere] * 4 + [smem] + [anywhere] * 14,
        out_specs=(anywhere, anywhere),
        scratch_shapes=[
            pltpu.VMEM(rows.shape, f32),
            pltpu.VMEM(rows.shape, f32),
            pltpu.VMEM(rows.shape, f32),
            pltpu.VMEM(mask.shape, jnp.int32),
            pltpu.VMEM((27, 2, HID), f32),
            pltpu.VMEM(w_last.shape, f32),
            *[pltpu.VMEM(array.shape, array.dtype) for array in constants],
            pltpu.VMEM(rows.shape, f32),
            pltpu.VMEM(rows.shape, f32),
            pltpu.VMEM((4 * GROUP, WIDE), f32),
            pltpu.VMEM((3, PEERS * SENT, 128), f32),
            pltpu.VMEM((3, PEERS, SENT, 128), f32),
            pltpu.VMEM((96, 2 * PEERS * GROUP), f32),
            pltpu.VMEM((2, 96, WIDE), f32),
            pltpu.VMEM((4, 24, WIDE), f32),
            pltpu.VMEM((2, OWNERS, 20, 128), f32),
            pltpu.VMEM((2, COIL_PEERS, 20, 128), f32),
            pltpu.VMEM((2, 3, 2, 8, HALF), f32),
            pltpu.VMEM((3, 2, 6, 8, HALF), f32),
            pltpu.VMEM((2, 4, 8, HALF), f32),
            pltpu.VMEM((3, HID * 4, HALF), f32),
            pltpu.VMEM((5, HID * 4, HALF), f32),
            pltpu.VMEM((2, OWNERS, 20, 128), f32),
            pltpu.VMEM((2, 2, 2, 24, HALF), f32),
            pltpu.SemaphoreType.DMA((18,)),
            pltpu.SemaphoreType.DMA((2,)),
            pltpu.SemaphoreType.DMA((3, PEERS)),
            pltpu.SemaphoreType.DMA((3, PEERS)),
            pltpu.SemaphoreType.DMA((2, OWNERS)),
            pltpu.SemaphoreType.DMA((2, COIL_PEERS)),
            pltpu.SemaphoreType.DMA((2, 6)),
            pltpu.SemaphoreType.DMA((2, 6)),
            pltpu.SemaphoreType.DMA((2, COIL_PEERS)),
            pltpu.SemaphoreType.DMA((2, OWNERS)),
            pltpu.SemaphoreType.REGULAR,
        ],
        compiler_params=pltpu.CompilerParams(
            collective_id=0, has_side_effects=True, vmem_limit_bytes=62 * 1024 * 1024
        ),
    )(
        kspace.transpose(0, 2, 1, 3),
        cotangent.transpose(0, 2, 1, 3),
        sens.transpose(0, 2, 1, 3),
        mask,
        eta,
        w_first.transpose(2, 3, 4, 1, 0).reshape(27, 2, HID),
        w_last,
        *constants,
    )
    results = pl.pallas_call(
        hand_on,
        out_shape=(rows, rows),
        in_specs=[anywhere] * 2,
        out_specs=(anywhere, anywhere),
        scratch_shapes=[pltpu.VMEM(rows.shape, f32)] * 2 + [pltpu.SemaphoreType.DMA((4,))],
        compiler_params=pltpu.CompilerParams(vmem_limit_bytes=62 * 1024 * 1024),
    )(*results)
    return tuple(result.transpose(0, 2, 1, 3) for result in results)


def solution(mesh):
    part = P("coil", "slab", "row", None)
    return jax.shard_map(
        local,
        mesh=mesh,
        in_specs=(part, part, part, P("slab", "row"), P(), P(), P()),
        out_specs=(part, part),
        check_vma=False,
    )
```

```python
import math

import jax
import jax.numpy as jnp
import ml_dtypes
import numpy as np
from jax import lax
from jax.experimental import pallas as pl
from jax.experimental.pallas import tpu as pltpu
from jax.sharding import PartitionSpec as P

MESH = pl.DeviceIdType.MESH
LEN = 320
HALF = 384
WIDE = 2 * HALF
CELLS = 20
LONG = 16
PEERS = 16
COIL_PEERS = 16
SENT = 8 + CELLS
REACH = 4
OWNERS = 10
HID = 18


def turned(owner, row):
    return owner + (row % 2) * (OWNERS - 1 - 2 * owner)


def owner_coil(owner, row):
    return (8 * turned(owner, row)) // 5


def coil_owner(coil, row):
    return turned((5 * coil + 7) // 8, row)


def split_table(table):
    high = table.astype(ml_dtypes.bfloat16)
    low = (table - high.astype(np.float64)).astype(ml_dtypes.bfloat16)
    return high, low


def tables():
    at = np.arange(LEN)
    angle = 2.0 * math.pi * ((at[:, None] * at[None, :]) % LEN) / LEN
    cosine, sine = np.cos(angle) / math.sqrt(LEN), np.sin(angle) / math.sqrt(LEN)
    first = np.zeros((PEERS, 24, 2, HALF))
    first[:, :CELLS, 0, :LEN] = cosine.reshape(PEERS, CELLS, LEN)
    first[:, :CELLS, 1, :LEN] = sine.reshape(PEERS, CELLS, LEN)
    line = np.arange(LEN).reshape(PEERS, CELLS)
    long, short = line[:, :LONG].reshape(-1), line[:, LONG:].reshape(-1)
    second = np.zeros((2 * LEN, 2, HALF))
    for part, rows in enumerate(((cosine, sine), (-sine, cosine))):
        for half in range(2):
            second[256 * part : 256 * part + 256, half, :LEN] = rows[half][long]
            second[512 + 64 * part : 576 + 64 * part, half, :LEN] = rows[half][short]
    return split_table(first.reshape(PEERS * 24, WIDE)) + split_table(
        second.reshape(2 * LEN, WIDE)
    )


def selectors():
    repeat = np.zeros((HID * 4, HID), np.float32)
    for unit in range(HID):
        repeat[4 * unit : 4 * unit + 4, unit] = 1.0
    pick = np.zeros((3, 54, 144), np.float32)
    place = np.zeros((3, HID * 4, 144), np.float32)
    for column in range(144):
        e3, channel, e1, row = column // 48, column // 24 % 2, column // 8 % 3, column % 8
        for e2 in range(3):
            pick[e2, 2 * (e1 * 9 + e2 * 3 + e3) + channel, column] = 1.0
            for line in range(HID * 4):
                if row - line % 4 == e2:
                    place[e2, line, column] = 1.0
    pick_back = np.zeros((3, 3, 16, 54), np.float32)
    place_back = np.zeros((3, 3, 16, HID * 4), np.float32)
    for e2 in range(3):
        for plane in range(3):
            for line in range(12):
                e3, channel, row = line // 4, line // 2 % 2, line % 2
                pick_back[e2, plane, line, 2 * ((2 - plane) * 9 + e2 * 3 + e3) + channel] = 1.0
                for column in range(HID * 4):
                    if row + 2 - column % 4 == e2:
                        place_back[e2, plane, line, column] = 1.0
    place_last = np.zeros((8, HID * 4), np.float32)
    pick_last = np.zeros((8, 2), np.float32)
    for line in range(4):
        pick_last[line, line // 2] = 1.0
        for column in range(HID * 4):
            if column % 4 == line % 2 + 1:
                place_last[line, column] = 1.0
    return (
        repeat,
        pick,
        place,
        pick_back.reshape(144, 54),
        place_back.reshape(144, HID * 4),
        place_last,
        pick_last,
    )


def unpack(packed):
    low = lax.broadcasted_iota(jnp.int32, (4, 128), 1) < LEN - 256
    last = packed[16:20]
    upper = jnp.where(low, last, 0.0)
    lower = jnp.where(low, pltpu.roll(last, 64, 1), 0.0)
    return jnp.concatenate(
        [packed[0:8], packed[8:16], jnp.concatenate([upper, lower], axis=0)], axis=1
    )


def split(values):
    high = values.astype(jnp.bfloat16)
    return high, (values - high.astype(jnp.float32)).astype(jnp.bfloat16)


def dot(left, right, dims=((1,), (0,))):
    return lax.dot_general(left, right, (dims, ((), ())), preferred_element_type=jnp.float32)


def pair(left):
    high = left.astype(jnp.bfloat16).astype(jnp.float32)
    both = jnp.concatenate([high, left - high], axis=0)
    return both.astype(jnp.bfloat16), high.astype(jnp.bfloat16)


def dot3(left_pair, right):
    both_left, left_high = left_pair
    rows = left_high.shape[0]
    right_high, right_low = split(right)
    both = dot(both_left, right_high)
    return both[:rows] + both[rows:] + dot(left_high, right_low)


def exchange(blocks, width, lane):
    blocks = list(blocks)
    step = 1
    while step < len(blocks):
        shift = width * step
        low = (lane & shift) == 0
        for first in range(len(blocks)):
            if first & step:
                continue
            upper, lower = blocks[first], blocks[first + step]
            blocks[first] = jnp.where(low, upper, pltpu.roll(lower, shift, 1))
            blocks[first + step] = jnp.where(low, pltpu.roll(upper, 128 - shift, 1), lower)
        step *= 2
    return blocks


def exact_dot(left, right, dims=((1,), (0,))):
    return lax.dot_general(
        left,
        right,
        (dims, ((), ())),
        precision=lax.Precision.HIGHEST,
        preferred_element_type=jnp.float32,
    )


def kernel(*refs):
    (
        kspace_hbm,
        cotangent_hbm,
        sens_hbm,
        mask_hbm,
        eta,
        w_first_hbm,
        w_last_hbm,
        *constants_hbm,
    ) = refs[:18]
    grad_kspace_hbm, grad_sens_hbm = refs[18:20]
    (
        kspace,
        cotangent,
        sens,
        mask,
        w_first,
        w_last,
        first_high,
        first_low,
        second_high,
        second_low,
        repeat,
        pick,
        place,
        pick_back,
        place_back,
        place_last,
        pick_last,
        grad_kspace,
        grad_sens,
        lines,
        spread,
        landed,
        wide,
        images,
        maps,
        parts,
        sums,
        near,
        shifted,
        cot_rows,
        acts,
        slopes,
        backs,
        pieces,
        fields,
        load_sem,
        store_sem,
        swap_send,
        swap_recv,
        sum_send,
        sum_recv,
        near_send,
        near_recv,
        field_send,
        field_recv,
        greet_far,
    ) = refs[20:]
    coil, slab, row = lax.axis_index("coil"), lax.axis_index("slab"), lax.axis_index("row")
    owner = coil_owner(coil, row)
    owns = owner_coil(owner, row) == coil

    def neighbour(step):
        other = owner + step
        other_row = row + jnp.where(other < 0, -1, 0) + jnp.where(other >= OWNERS, 1, 0)
        there = jnp.logical_and(other_row >= 0, other_row < PEERS)
        return owner_coil((other + OWNERS) % OWNERS, other_row), other_row, there

    near_by = [
        (step, across) for step in (-1, 0, 1) for across in (0, 1) if (step, across) != (0, 0)
    ]

    sources = [kspace_hbm, *constants_hbm[:2], cotangent_hbm, sens_hbm, *constants_hbm[2:4]]
    targets = [kspace, first_high, first_low, cotangent, sens, second_high, second_low]
    sources += [w_first_hbm, w_last_hbm, mask_hbm, *constants_hbm[4:]]
    targets += [w_first, w_last, mask, repeat, pick, place, pick_back, place_back]
    targets += [place_last, pick_last]
    loads = [
        pltpu.make_async_copy(source, target, load_sem.at[number])
        for number, (source, target) in enumerate(zip(sources, targets))
    ]
    for load in loads[:4]:
        load.start()

    near[...] = jnp.zeros_like(near)

    barrier = pltpu.get_barrier_semaphore()

    @pl.loop(1, PEERS)
    def _(step):
        pl.semaphore_signal(
            barrier, inc=1, device_id={"row": (row + step) % PEERS}, device_id_type=MESH
        )

    @pl.loop(1, REACH + 1)
    def _(step):
        for sign in (1, -1):
            pl.semaphore_signal(
                barrier,
                inc=1,
                device_id={"coil": (coil + sign * step) % COIL_PEERS},
                device_id_type=MESH,
            )

    for step, across in near_by:
        other_coil, other_row, there = neighbour(step)

        @pl.when(jnp.logical_and(owns, there))
        def _():
            pl.semaphore_signal(
                barrier,
                inc=1,
                device_id={
                    "coil": other_coil,
                    "slab": (slab + across) % 2,
                    "row": other_row,
                },
                device_id_type=MESH,
            )

    lane = lax.broadcasted_iota(jnp.int32, (CELLS, 128), 1)

    def put_rows(group, real, imag):
        for part, (first, second) in enumerate(((real, -imag), (imag, real))):
            at = 64 * part + LONG * group
            lines[at : at + LONG, :HALF] = first[:LONG]
            lines[at : at + LONG, HALF:] = second[:LONG]
            at = 128 + 16 * part + 4 * group
            lines[at : at + 4, :HALF] = first[LONG:]
            lines[at : at + 4, HALF:] = second[LONG:]

    def spread_out(which):
        high, low = split(lines[...])
        right = jnp.concatenate([high[:128], low[:128], high[128:192], low[128:192]], axis=0)
        both = dot(first_high[...], right, ((1,), (1,)))
        rest = dot(first_low[...], high, ((1,), (1,)))
        long = both[:, :128] + both[:, 128:256] + rest[:, :128]
        short = both[:, 256:] + pltpu.roll(both[:, 256:], 64, 1) + rest[:, 128:]
        folds = short.reshape(PEERS, 3, 8, 128)
        second = pltpu.roll(folds[:, 1].reshape(PEERS * 8, 128), 32, 1)
        third = pltpu.roll(folds[:, 2].reshape(PEERS * 8, 128), 64, 1)
        at = lax.broadcasted_iota(jnp.int32, (PEERS * 8, 128), 1)
        fold = jnp.where(
            at < 32,
            folds[:, 0].reshape(PEERS * 8, 128),
            jnp.where(at < 64, second, jnp.where(at < 96, third, 0.0)),
        )
        spread[which, :, 0:8, :] = fold.reshape(PEERS, 8, 128)
        spread[which, :, 8:SENT, :] = long.reshape(PEERS, 24, 128)[:, :CELLS]

    def swap(which, step):
        peer = (row + step) % PEERS
        return pltpu.make_async_remote_copy(
            src_ref=spread.at[which, peer],
            dst_ref=landed.at[which, row],
            send_sem=swap_send.at[which, peer],
            recv_sem=swap_recv.at[which, row],
            device_id={"row": peer},
            device_id_type=MESH,
        )

    def swap_start(which):
        @pl.loop(1, PEERS)
        def _(step):
            swap(which, step).start()

        landed[which, row] = spread[which, row]

    def swap_wait(which):
        @pl.loop(1, PEERS)
        def _(step):
            peer = (row + step) % PEERS
            pltpu.make_async_remote_copy(
                src_ref=spread.at[which, peer],
                dst_ref=landed.at[which, peer],
                send_sem=swap_send.at[which, peer],
                recv_sem=swap_recv.at[which, peer],
                device_id={"row": peer},
                device_id_type=MESH,
            ).wait_recv()

    def gather_in(which):
        for half in range(2):
            blocks = [landed[which, 8 * half + peer, 8:SENT, :] for peer in range(8)]
            for unit, block in enumerate(exchange(blocks, LONG, lane)):
                part, group = unit // 4, unit % 4
                start = 256 * part + 128 * half
                wide[24 * group : 24 * group + CELLS, start : start + 128] = block
        blocks = exchange([landed[which, peer, 0:8, :] for peer in range(PEERS)], 4, lane[:8])
        low = lane[:8] < 64
        for group in range(4):
            folds = (
                jnp.where(low, blocks[group], pltpu.roll(blocks[4 + group], 64, 1)),
                jnp.where(low, blocks[8 + group], pltpu.roll(blocks[12 + group], 64, 1)),
                jnp.where(low, pltpu.roll(blocks[group], 64, 1), blocks[4 + group]),
            )
            for number, fold in enumerate(folds):
                at = 24 * group + 8 * number
                wide[at : at + 8, 512:] = fold
        high, low = split(wide[...])
        both = dot(jnp.concatenate([high, low], axis=0), second_high[...])
        return both[:96] + both[96:] + dot(high, second_low[...])

    def halves(ref, group):
        lines_now = ref[group // 2, :, group % 2, :]
        tiles = [lines_now[:, 128 * tile : 128 * tile + 128] for tile in range(5)]
        low = lane < 64
        turned = [pltpu.roll(tile, 64, 1) for tile in tiles[2:]]
        zero = jnp.zeros_like(tiles[0])
        return (
            tiles[:2] + [jnp.where(low, tiles[2], zero)],
            [
                jnp.where(low, turned[0], turned[1]),
                jnp.where(low, turned[1], turned[2]),
                jnp.where(low, turned[2], zero),
            ],
        )

    def whole_lines(real, imag):
        low = lane < 64
        turned = [pltpu.roll(imag[:, 128 * tile : 128 * tile + 128], 64, 1) for tile in range(3)]
        tiles = [
            real[:, :128],
            real[:, 128:256],
            jnp.where(low, real[:, 256:], turned[0]),
            jnp.where(low, turned[0], turned[1]),
            jnp.where(low, turned[1], turned[2]),
        ]
        return jnp.concatenate(tiles, axis=1)

    def put_lines(ref):
        for group in range(4):
            real, imag = halves(ref, group)
            put_rows(group, jnp.concatenate(real, axis=1), jnp.concatenate(imag, axis=1))

    lines[...] = jnp.zeros_like(lines)
    loads[0].wait()
    put_lines(kspace)
    loads[1].wait()
    loads[2].wait()
    for load in loads[4:]:
        load.start()
    spread_out(0)

    near_count = jnp.int32(0)
    for step, across in near_by:
        near_count = near_count + jnp.where(jnp.logical_and(owns, neighbour(step)[2]), 1, 0)
    pl.semaphore_wait(barrier, PEERS - 1 + 2 * REACH + near_count)

    @pl.loop(1, REACH + 1)
    def _(step):
        for sign in (1, -1):
            pl.semaphore_signal(
                greet_far,
                inc=1,
                device_id={"coil": (coil + sign * step) % COIL_PEERS},
                device_id_type=MESH,
            )


    swap_start(0)
    loads[3].wait()
    put_lines(cotangent)
    spread_out(1)
    swap_start(1)

    wide[...] = jnp.zeros_like(wide)
    maps[...] = jnp.zeros_like(maps)
    loads[4].wait()
    for group in range(4):
        for half, tiles in enumerate(halves(sens, group)):
            for number, tile in enumerate(tiles):
                start = half * HALF + 128 * number
                maps[group, :CELLS, start : start + 128] = tile
    for load in loads[5:]:
        load.wait()
    weights = w_first[...].reshape(54, HID)
    weights_rows = exact_dot(repeat[...], weights, ((1,), (1,)))
    forward_matrix = jnp.zeros((HID * 4, 144), jnp.float32)
    for e2 in range(3):
        forward_matrix += place[e2] * exact_dot(weights_rows, pick[e2])
    weights_back = exact_dot(weights, repeat[...], ((1,), (1,)))
    backward_matrix = jnp.sum(
        (exact_dot(pick_back[...], weights_back) * place_back[...]).reshape(3, 48, HID * 4), axis=0
    )
    last_columns = exact_dot(repeat[...], w_last[...], ((1,), (1,)))
    last_matrix = place_last[...] * exact_dot(
        pick_last[...], exact_dot(w_last[...], repeat[...], ((1,), (1,)))
    )
    forward_pair, backward_pair, last_pair = map(
        pair, (forward_matrix, backward_matrix, last_matrix)
    )

    def part_sums(which, total_field):
        for plane in range(2):
            real = imag = None
            for local_coil in range(2):
                group = local_coil * 2 + plane
                map_real, map_imag = maps[group, :, :HALF], maps[group, :, HALF:]
                field = total_field[24 * group : 24 * group + 24]
                field_real, field_imag = field[:, :HALF], field[:, HALF:]
                this_real = map_real * field_real + map_imag * field_imag
                this_imag = map_real * field_imag - map_imag * field_real
                real = this_real if real is None else real + this_real
                imag = this_imag if imag is None else imag + this_imag
            last = real[:, 256:] + pltpu.roll(imag[:, 256:], 64, 1)
            for target in range(OWNERS):
                cut = slice(2 * target, 2 * target + 2)
                for half in range(2):
                    lanes = slice(128 * half, 128 * half + 128)
                    at = 8 * half + 2 * plane
                    parts[which, target, at : at + 2, :] = real[cut, lanes]
                    parts[which, target, at + 4 : at + 6, :] = imag[cut, lanes]
                parts[which, target, 16 + 2 * plane : 18 + 2 * plane, :] = last[cut]

    def part_copy(which, target):
        return pltpu.make_async_remote_copy(
            src_ref=parts.at[which, target],
            dst_ref=sums.at[which, coil],
            send_sem=sum_send.at[which, target],
            recv_sem=sum_recv.at[which, coil],
            device_id={"coil": owner_coil(target, row)},
            device_id_type=MESH,
        )

    def part_start(which):
        @pl.loop(0, OWNERS)
        def _(step):
            target = (owner + step) % OWNERS

            @pl.when(owner_coil(target, row) != coil)
            def _():
                part_copy(which, target).start()

    def part_total(which):
        @pl.loop(1, COIL_PEERS)
        def _(step):
            peer = (coil + step) % COIL_PEERS
            pltpu.make_async_remote_copy(
                src_ref=parts.at[which, 0],
                dst_ref=sums.at[which, peer],
                send_sem=sum_send.at[which, 0],
                recv_sem=sum_recv.at[which, peer],
                device_id={"coil": peer},
                device_id_type=MESH,
            ).wait_recv()

        sums[which, coil] = parts[which, owner]
        total = sums[which, 0]
        for peer in range(1, COIL_PEERS):
            total = total + sums[which, peer]
        return unpack(total)

    def near_copy(which, step, across):
        other_coil, other_row, there = neighbour(step)
        copy = pltpu.make_async_remote_copy(
            src_ref=near.at[which, 1, slab],
            dst_ref=near.at[which, 1 - step, slab],
            send_sem=near_send.at[which, (step + 1) * 2 + across],
            recv_sem=near_recv.at[which, (1 - step) * 2 + across],
            device_id={"coil": other_coil, "slab": (slab + across) % 2, "row": other_row},
            device_id_type=MESH,
        )
        return copy, there

    def near_start(which):
        for step, across in near_by:
            copy, there = near_copy(which, step, across)
            pl.when(there)(copy.start)

    def near_wait(which):
        for step, across in near_by:
            other_coil, other_row, there = neighbour(step)
            copy = pltpu.make_async_remote_copy(
                src_ref=near.at[which, 1, slab],
                dst_ref=near.at[which, 1 + step, (slab + across) % 2],
                send_sem=near_send.at[which, (step + 1) * 2 + across],
                recv_sem=near_recv.at[which, (1 + step) * 2 + across],
                device_id={"coil": other_coil, "slab": (slab + across) % 2, "row": other_row},
                device_id_type=MESH,
            )
            pl.when(there)(copy.wait_recv)

    def put_piece(which, plane, values):
        for half in range(2):
            lanes = slice(128 * half, 128 * half + 128)
            at = 8 * half + 2 * plane
            pieces[which, owner, at : at + 2, :] = values[0:2, lanes]
            pieces[which, owner, at + 4 : at + 6, :] = values[2:4, lanes]
        low = lax.broadcasted_iota(jnp.int32, (2, 128), 1) < LEN - 256
        pieces[which, owner, 16 + 2 * plane : 18 + 2 * plane, :] = jnp.where(
            low, values[0:2, 256:], pltpu.roll(values[2:4, 256:], 64, 1)
        )

    def field_copy(which, step):
        peer = (coil + step) % COIL_PEERS
        return pltpu.make_async_remote_copy(
            src_ref=pieces.at[which, owner],
            dst_ref=pieces.at[which, owner],
            send_sem=field_send.at[which, peer],
            recv_sem=field_recv.at[which, owner],
            device_id={"coil": peer},
            device_id_type=MESH,
        )

    def field_start(which):
        @pl.loop(1, COIL_PEERS)
        def _(step):
            field_copy(which, step).start()

    def field_wait(which):
        @pl.loop(0, OWNERS)
        def _(target):
            @pl.when(owner_coil(target, row) != coil)
            def _():
                pltpu.make_async_remote_copy(
                    src_ref=pieces.at[which, target],
                    dst_ref=pieces.at[which, target],
                    send_sem=field_send.at[which, 0],
                    recv_sem=field_recv.at[which, target],
                    device_id={"coil": owner_coil(target, row)},
                    device_id_type=MESH,
                ).wait_recv()

        for target in range(OWNERS):
            cut = slice(2 * target, 2 * target + 2)
            for plane in range(2):
                for part in range(2):
                    for half in range(2):
                        at = 8 * half + 4 * part + 2 * plane
                        fields[which, part, plane, cut, 128 * half : 128 * half + 128] = pieces[
                            which, target, at : at + 2, :
                        ]
                last = pieces[which, target, 16 + 2 * plane : 18 + 2 * plane, :]
                fields[which, 0, plane, cut, 256:] = last
                fields[which, 1, plane, cut, 256:] = pltpu.roll(last, 64, 1)

    swap_wait(0)
    total_field = gather_in(0)
    images[0] = total_field
    part_sums(0, total_field)
    pl.semaphore_wait(greet_far, 2 * REACH)
    part_start(0)
    swap_wait(1)
    total_field = gather_in(1)
    images[1] = total_field
    part_sums(1, total_field)
    part_start(1)

    @pl.when(owns)
    def _():
        near[0, 1, slab] = part_total(0)
        near_start(0)
        shifted[...] = jnp.zeros_like(shifted)
        backs[0] = jnp.zeros((48, HALF), jnp.float32)
        backs[4] = jnp.zeros((48, HALF), jnp.float32)
        near_wait(0)
        for part in range(2):
            for side in range(2):
                for plane in range(2):
                    line = part * 4 + plane * 2
                    for step in range(3):
                        shifted[1, part, 1 + 2 * side + plane, 2 * step : 2 * step + 2, :] = near[
                            0, step, side, line : line + 2, :
                        ]
        middle = shifted[1].reshape(2 * 6 * 8, HALF)
        shifted[0] = pltpu.roll(middle, 1, 1).reshape(2, 6, 8, HALF)
        shifted[2] = pltpu.roll(middle, HALF - 1, 1).reshape(2, 6, 8, HALF)
        for plane in range(3):
            pre = dot3(
                forward_pair,
                shifted[:, :, pl.ds(slab + plane, 3)].reshape(144, HALF),
            )
            sigmoid = 1.0 / (1.0 + jnp.exp(-pre))
            acts[plane] = pre * sigmoid
            slopes[plane] = sigmoid * (1.0 + pre * (1.0 - sigmoid))
        near[1, 1, slab] = part_total(1)
        near_start(1)
        for plane in range(2):
            put_piece(0, plane, dot3(last_pair, acts[slab + plane]))
        near_wait(1)
        for part in range(2):
            for side in range(2):
                for plane in range(2):
                    line = part * 4 + plane * 2
                    for again in (0, 4):
                        cot_rows[part, 2 * side + plane, again : again + 1, :] = near[
                            1, 0, side, line + 1 : line + 2, :
                        ]
                        cot_rows[part, 2 * side + plane, again + 1 : again + 3, :] = near[
                            1, 1, side, line : line + 2, :
                        ]
                        cot_rows[part, 2 * side + plane, again + 3 : again + 4, :] = near[
                            1, 2, side, line : line + 1, :
                        ]
        for plane in range(3):
            real = jnp.broadcast_to(cot_rows[0, slab + plane][None], (9, 8, HALF))
            imag = jnp.broadcast_to(cot_rows[1, slab + plane][None], (9, 8, HALF))
            spread_cot = last_columns[:, 0:1] * real.reshape(HID * 4, HALF) + last_columns[
                :, 1:2
            ] * imag.reshape(HID * 4, HALF)
            backs[plane + 1] = dot3(backward_pair, slopes[plane] * spread_cot)
        for plane in range(2):
            back = (
                backs[slab + plane, 0:16]
                + backs[slab + plane + 1, 16:32]
                + backs[slab + plane + 2, 32:48]
            )
            back = (
                pltpu.roll(back[0:4], HALF - 1, 1) + back[4:8] + pltpu.roll(back[8:12], 1, 1)
            )
            put_piece(1, plane, back)
        field_start(1)
        field_start(0)

    field_wait(1)
    for group in range(4):
        plane = group % 2
        other_real, other_imag = fields[1, 0, plane, :CELLS], fields[1, 1, plane, :CELLS]
        real, imag = maps[group, :CELLS, :HALF], maps[group, :CELLS, HALF:]
        put_rows(
            group,
            real * other_real - imag * other_imag,
            -(real * other_imag + imag * other_real),
        )
    spread_out(2)
    swap_start(2)
    stores = [
        pltpu.make_async_copy(grad_sens, grad_sens_hbm, store_sem.at[0]),
        pltpu.make_async_copy(grad_kspace, grad_kspace_hbm, store_sem.at[1]),
    ]
    field_wait(0)
    for group in range(4):
        plane = group % 2
        at = slice(24 * group, 24 * group + CELLS)
        out_real = out_imag = None
        for which in range(2):
            other_real, other_imag = fields[which, 0, plane, :CELLS], fields[which, 1, plane, :CELLS]
            real, imag = images[1 - which, at, :HALF], images[1 - which, at, HALF:]
            this_real = -(real * other_real + imag * other_imag)
            this_imag = real * other_imag - imag * other_real
            out_real = this_real if out_real is None else out_real + this_real
            out_imag = this_imag if out_imag is None else out_imag + this_imag
        grad_sens[group // 2, :, plane, :] = whole_lines(out_real, out_imag)
    stores[0].start()
    square_row = lax.broadcasted_iota(jnp.int32, (CELLS, CELLS), 0)
    square_column = lax.broadcasted_iota(jnp.int32, (CELLS, CELLS), 1)
    factors = []
    for plane in range(2):
        sampled = jnp.broadcast_to(mask[plane : plane + 1, :].astype(jnp.float32), (CELLS, CELLS))
        column = jnp.sum(
            jnp.where(square_row == square_column, sampled, 0.0), axis=1, keepdims=True
        )
        factors.append(1.0 - eta[0] * column)
    swap_wait(2)
    model = gather_in(2)
    for group in range(4):
        plane = group % 2
        mine = model[24 * group : 24 * group + CELLS]
        grad_kspace[group // 2, :, plane, :] = factors[plane] * cotangent[
            group // 2, :, plane, :
        ] - whole_lines(mine[:, :HALF], -mine[:, HALF:])
    stores[1].start()

    for which in range(3):

        @pl.loop(1, PEERS)
        def _(step):
            swap(which, step).wait_send()

    for which in range(2):

        @pl.loop(0, OWNERS)
        def _(target):
            @pl.when(owner_coil(target, row) != coil)
            def _():
                part_copy(which, target).wait_send()

        @pl.when(owns)
        def _():
            for step, across in near_by:
                copy, there = near_copy(which, step, across)
                pl.when(there)(copy.wait_send)

            @pl.loop(1, COIL_PEERS)
            def _(step):
                field_copy(which, step).wait_send()
    stores[0].wait()
    stores[1].wait()


def hand_on(first, second, first_out, second_out, first_held, second_held, sems):
    loads = [
        pltpu.make_async_copy(first, first_held, sems.at[0]),
        pltpu.make_async_copy(second, second_held, sems.at[1]),
    ]
    stores = [
        pltpu.make_async_copy(first_held, first_out, sems.at[2]),
        pltpu.make_async_copy(second_held, second_out, sems.at[3]),
    ]
    for load in loads:
        load.start()
    for load, store in zip(loads, stores):
        load.wait()
        store.start()
    for store in stores:
        store.wait()


def local(kspace, cotangent, sens, mask, eta, w_first, w_last):
    constants = [jnp.asarray(array) for array in tables() + selectors()]
    smem = pl.BlockSpec(memory_space=pltpu.SMEM)
    anywhere = pl.BlockSpec(memory_space=pl.ANY)
    f32, b16 = jnp.float32, jnp.bfloat16
    rows = jax.ShapeDtypeStruct((2, CELLS, 2, 2 * LEN), f32)
    results = pl.pallas_call(
        kernel,
        out_shape=(rows, rows),
        in_specs=[anywhere] * 4 + [smem] + [anywhere] * 13,
        out_specs=(anywhere, anywhere),
        scratch_shapes=[
            pltpu.VMEM(rows.shape, f32),
            pltpu.VMEM(rows.shape, f32),
            pltpu.VMEM(rows.shape, f32),
            pltpu.VMEM(mask.shape, jnp.int32),
            pltpu.VMEM((27, 2, HID), f32),
            pltpu.VMEM(w_last.shape, f32),
            *[pltpu.VMEM(array.shape, array.dtype) for array in constants],
            pltpu.VMEM(rows.shape, f32),
            pltpu.VMEM(rows.shape, f32),
            pltpu.VMEM((256, WIDE), f32),
            pltpu.VMEM((3, PEERS, SENT, 128), f32),
            pltpu.VMEM((3, PEERS, SENT, 128), f32),
            pltpu.VMEM((96, 2 * LEN), f32),
            pltpu.VMEM((2, 96, WIDE), f32),
            pltpu.VMEM((4, 24, WIDE), f32),
            pltpu.VMEM((2, OWNERS, 20, 128), f32),
            pltpu.VMEM((2, COIL_PEERS, 20, 128), f32),
            pltpu.VMEM((2, 3, 2, 8, HALF), f32),
            pltpu.VMEM((3, 2, 6, 8, HALF), f32),
            pltpu.VMEM((2, 4, 8, HALF), f32),
            pltpu.VMEM((3, HID * 4, HALF), f32),
            pltpu.VMEM((3, HID * 4, HALF), f32),
            pltpu.VMEM((5, 48, HALF), f32),
            pltpu.VMEM((2, OWNERS, 20, 128), f32),
            pltpu.VMEM((2, 2, 2, 24, HALF), f32),
            pltpu.SemaphoreType.DMA((17,)),
            pltpu.SemaphoreType.DMA((2,)),
            pltpu.SemaphoreType.DMA((3, PEERS)),
            pltpu.SemaphoreType.DMA((3, PEERS)),
            pltpu.SemaphoreType.DMA((2, OWNERS)),
            pltpu.SemaphoreType.DMA((2, COIL_PEERS)),
            pltpu.SemaphoreType.DMA((2, 6)),
            pltpu.SemaphoreType.DMA((2, 6)),
            pltpu.SemaphoreType.DMA((2, COIL_PEERS)),
            pltpu.SemaphoreType.DMA((2, OWNERS)),
            pltpu.SemaphoreType.REGULAR,
        ],
        compiler_params=pltpu.CompilerParams(
            collective_id=0, has_side_effects=True, vmem_limit_bytes=62 * 1024 * 1024
        ),
    )(
        kspace.transpose(0, 2, 1, 3),
        cotangent.transpose(0, 2, 1, 3),
        sens.transpose(0, 2, 1, 3),
        mask,
        eta,
        w_first.transpose(2, 3, 4, 1, 0).reshape(27, 2, HID),
        w_last,
        *constants,
    )
    results = pl.pallas_call(
        hand_on,
        out_shape=(rows, rows),
        in_specs=[anywhere] * 2,
        out_specs=(anywhere, anywhere),
        scratch_shapes=[pltpu.VMEM(rows.shape, f32)] * 2 + [pltpu.SemaphoreType.DMA((4,))],
        compiler_params=pltpu.CompilerParams(vmem_limit_bytes=62 * 1024 * 1024),
    )(*results)
    return tuple(result.transpose(0, 2, 1, 3) for result in results)


def solution(mesh):
    part = P("coil", "slab", "row", None)
    return jax.shard_map(
        local,
        mesh=mesh,
        in_specs=(part, part, part, P("slab", "row"), P(), P(), P()),
        out_specs=(part, part),
        check_vma=False,
    )
```

```python
import math

import jax
import jax.numpy as jnp
import ml_dtypes
import numpy as np
from jax import lax
from jax.experimental import pallas as pl
from jax.experimental.pallas import tpu as pltpu
from jax.sharding import PartitionSpec as P

MESH = pl.DeviceIdType.MESH
LEN = 320
HALF = 384
WIDE = 2 * HALF
CELLS = 20
LONG = 16
PEERS = 16
COIL_PEERS = 16
SENT = 8 + CELLS
REACH = 4
OWNERS = 10
HID = 18


def outward(step, middle):
    return middle + (1 - 2 * (step % 2)) * ((step + 1) // 2)


def turned(owner, row):
    return owner + (row % 2) * (OWNERS - 1 - 2 * owner)


def owner_coil(owner, row):
    return (8 * turned(owner, row)) // 5


def coil_owner(coil, row):
    return turned((5 * coil + 7) // 8, row)


def split_table(table):
    high = table.astype(ml_dtypes.bfloat16)
    low = (table - high.astype(np.float64)).astype(ml_dtypes.bfloat16)
    return high, low


def tables():
    at = np.arange(LEN)
    angle = 2.0 * math.pi * ((at[:, None] * at[None, :]) % LEN) / LEN
    cosine, sine = np.cos(angle) / math.sqrt(LEN), np.sin(angle) / math.sqrt(LEN)
    first = np.zeros((PEERS, 24, 2, HALF))
    first[:, :CELLS, 0, :LEN] = cosine.reshape(PEERS, CELLS, LEN)
    first[:, :CELLS, 1, :LEN] = sine.reshape(PEERS, CELLS, LEN)
    line = np.arange(LEN).reshape(PEERS, CELLS)
    long, short = line[:, :LONG].reshape(-1), line[:, LONG:].reshape(-1)
    second = np.zeros((2 * LEN, 2, HALF))
    for part, rows in enumerate(((cosine, sine), (-sine, cosine))):
        for half in range(2):
            second[256 * part : 256 * part + 256, half, :LEN] = rows[half][long]
            second[512 + 64 * part : 576 + 64 * part, half, :LEN] = rows[half][short]
    return split_table(first.reshape(PEERS * 24, WIDE)) + split_table(
        second.reshape(2 * LEN, WIDE)
    )


def selectors():
    repeat = np.zeros((HID * 4, HID), np.float32)
    for unit in range(HID):
        repeat[4 * unit : 4 * unit + 4, unit] = 1.0
    pick = np.zeros((3, 54, 144), np.float32)
    place = np.zeros((3, HID * 4, 144), np.float32)
    for column in range(144):
        e3, channel, e1, row = column // 48, column // 24 % 2, column // 8 % 3, column % 8
        for e2 in range(3):
            pick[e2, 2 * (e1 * 9 + e2 * 3 + e3) + channel, column] = 1.0
            for line in range(HID * 4):
                if row - line % 4 == e2:
                    place[e2, line, column] = 1.0
    pick_back = np.zeros((3, 3, 16, 54), np.float32)
    place_back = np.zeros((3, 3, 16, HID * 4), np.float32)
    for e2 in range(3):
        for plane in range(3):
            for line in range(12):
                e3, channel, row = line // 4, line // 2 % 2, line % 2
                pick_back[e2, plane, line, 2 * ((2 - plane) * 9 + e2 * 3 + e3) + channel] = 1.0
                for column in range(HID * 4):
                    if row + 2 - column % 4 == e2:
                        place_back[e2, plane, line, column] = 1.0
    place_last = np.zeros((8, HID * 4), np.float32)
    pick_last = np.zeros((8, 2), np.float32)
    for line in range(4):
        pick_last[line, line // 2] = 1.0
        for column in range(HID * 4):
            if column % 4 == line % 2 + 1:
                place_last[line, column] = 1.0
    return (
        repeat,
        pick,
        place,
        pick_back.reshape(144, 54),
        place_back.reshape(144, HID * 4),
        place_last,
        pick_last,
    )


def unpack(packed):
    low = lax.broadcasted_iota(jnp.int32, (4, 128), 1) < LEN - 256
    last = packed[16:20]
    upper = jnp.where(low, last, 0.0)
    lower = jnp.where(low, pltpu.roll(last, 64, 1), 0.0)
    return jnp.concatenate(
        [packed[0:8], packed[8:16], jnp.concatenate([upper, lower], axis=0)], axis=1
    )


def split(values):
    high = values.astype(jnp.bfloat16)
    return high, (values - high.astype(jnp.float32)).astype(jnp.bfloat16)


def dot(left, right, dims=((1,), (0,))):
    return lax.dot_general(left, right, (dims, ((), ())), preferred_element_type=jnp.float32)


def pair(left):
    high = left.astype(jnp.bfloat16).astype(jnp.float32)
    both = jnp.concatenate([high, left - high], axis=0)
    return both.astype(jnp.bfloat16), high.astype(jnp.bfloat16)


def dot3(left_pair, right):
    both_left, left_high = left_pair
    rows = left_high.shape[0]
    right_high, right_low = split(right)
    both = dot(both_left, right_high)
    return both[:rows] + both[rows:] + dot(left_high, right_low)


def exchange(blocks, width, lane):
    blocks = list(blocks)
    step = 1
    while step < len(blocks):
        shift = width * step
        low = (lane & shift) == 0
        for first in range(len(blocks)):
            if first & step:
                continue
            upper, lower = blocks[first], blocks[first + step]
            blocks[first] = jnp.where(low, upper, pltpu.roll(lower, shift, 1))
            blocks[first + step] = jnp.where(low, pltpu.roll(upper, 128 - shift, 1), lower)
        step *= 2
    return blocks


def exact_dot(left, right, dims=((1,), (0,))):
    return lax.dot_general(
        left,
        right,
        (dims, ((), ())),
        precision=lax.Precision.HIGHEST,
        preferred_element_type=jnp.float32,
    )


class Halves:
    def __init__(self, source, target, sems, number):
        rows = source.shape[0] // 2
        self.copies = [
            pltpu.make_async_copy(
                source.at[pl.ds(half * rows, rows)],
                target.at[pl.ds(half * rows, rows)],
                sems.at[number, half],
            )
            for half in range(2)
        ]

    def start(self):
        for copy in self.copies:
            copy.start()

    def wait(self):
        for copy in self.copies:
            copy.wait()


def kernel(*refs):
    (
        kspace_hbm,
        cotangent_hbm,
        sens_hbm,
        mask_hbm,
        eta,
        w_first_hbm,
        w_last_hbm,
        *constants_hbm,
    ) = refs[:18]
    grad_kspace_hbm, grad_sens_hbm = refs[18:20]
    (
        kspace,
        cotangent,
        sens,
        mask,
        w_first,
        w_last,
        first_high,
        first_low,
        second_high,
        second_low,
        repeat,
        pick,
        place,
        pick_back,
        place_back,
        place_last,
        pick_last,
        grad_kspace,
        grad_sens,
        lines,
        spread,
        landed,
        wide,
        images,
        maps,
        parts,
        sums,
        near,
        shifted,
        cot_rows,
        acts,
        slopes,
        backs,
        pieces,
        fields,
        load_sem,
        store_sem,
        swap_send,
        swap_recv,
        sum_send,
        sum_recv,
        near_send,
        near_recv,
        field_send,
        field_recv,
        greet_far,
    ) = refs[20:]
    coil, slab, row = lax.axis_index("coil"), lax.axis_index("slab"), lax.axis_index("row")
    owner = coil_owner(coil, row)
    owns = owner_coil(owner, row) == coil

    def neighbour(step):
        other = owner + step
        other_row = row + jnp.where(other < 0, -1, 0) + jnp.where(other >= OWNERS, 1, 0)
        there = jnp.logical_and(other_row >= 0, other_row < PEERS)
        return owner_coil((other + OWNERS) % OWNERS, other_row), other_row, there

    near_by = [(-1, 1), (1, 1), (0, 1), (-1, 0), (1, 0)]

    sources = [kspace_hbm, *constants_hbm[:2], cotangent_hbm, sens_hbm, *constants_hbm[2:4]]
    targets = [kspace, first_high, first_low, cotangent, sens, second_high, second_low]
    sources += [w_first_hbm, w_last_hbm, mask_hbm, *constants_hbm[4:]]
    targets += [w_first, w_last, mask, repeat, pick, place, pick_back, place_back]
    targets += [place_last, pick_last]
    loads = []
    for number, (source, target) in enumerate(zip(sources, targets)):
        if number < 7:
            loads.append(Halves(source, target, load_sem, number))
        else:
            loads.append(pltpu.make_async_copy(source, target, load_sem.at[number, 0]))
    for load in loads[:4]:
        load.start()

    near[...] = jnp.zeros_like(near)

    barrier = pltpu.get_barrier_semaphore()

    @pl.loop(1, PEERS)
    def _(step):
        pl.semaphore_signal(
            barrier, inc=1, device_id={"row": (row + step) % PEERS}, device_id_type=MESH
        )

    @pl.loop(1, REACH + 1)
    def _(step):
        for sign in (1, -1):
            pl.semaphore_signal(
                barrier,
                inc=1,
                device_id={"coil": (coil + sign * step) % COIL_PEERS},
                device_id_type=MESH,
            )

    for step, across in near_by:
        other_coil, other_row, there = neighbour(step)

        @pl.when(jnp.logical_and(owns, there))
        def _():
            pl.semaphore_signal(
                barrier,
                inc=1,
                device_id={
                    "coil": other_coil,
                    "slab": (slab + across) % 2,
                    "row": other_row,
                },
                device_id_type=MESH,
            )

    lane = lax.broadcasted_iota(jnp.int32, (CELLS, 128), 1)

    def put_rows(group, real, imag):
        for part, (first, second) in enumerate(((real, -imag), (imag, real))):
            at = 64 * part + LONG * group
            lines[at : at + LONG, :HALF] = first[:LONG]
            lines[at : at + LONG, HALF:] = second[:LONG]
            at = 128 + 16 * part + 4 * group
            lines[at : at + 4, :HALF] = first[LONG:]
            lines[at : at + 4, HALF:] = second[LONG:]

    def spread_out(which):
        high, low = split(lines[...])
        right = jnp.concatenate([high[:128], low[:128], high[128:192], low[128:192]], axis=0)
        both = dot(first_high[...], right, ((1,), (1,)))
        rest = dot(first_low[...], high, ((1,), (1,)))
        long = both[:, :128] + both[:, 128:256] + rest[:, :128]
        short = both[:, 256:] + pltpu.roll(both[:, 256:], 64, 1) + rest[:, 128:]
        folds = short.reshape(PEERS, 3, 8, 128)
        second = pltpu.roll(folds[:, 1].reshape(PEERS * 8, 128), 32, 1)
        third = pltpu.roll(folds[:, 2].reshape(PEERS * 8, 128), 64, 1)
        at = lax.broadcasted_iota(jnp.int32, (PEERS * 8, 128), 1)
        fold = jnp.where(
            at < 32,
            folds[:, 0].reshape(PEERS * 8, 128),
            jnp.where(at < 64, second, jnp.where(at < 96, third, 0.0)),
        )
        spread[which, :, 0:8, :] = fold.reshape(PEERS, 8, 128)
        spread[which, :, 8:SENT, :] = long.reshape(PEERS, 24, 128)[:, :CELLS]

    def swap(which, peer):
        return pltpu.make_async_remote_copy(
            src_ref=spread.at[which, peer],
            dst_ref=landed.at[which, row],
            send_sem=swap_send.at[which, peer],
            recv_sem=swap_recv.at[which, row],
            device_id={"row": peer},
            device_id_type=MESH,
        )

    def swap_start(which):
        for across, along in ((1, 2), (0, 2), (1, 1), (1, 3), (1, 0), (0, 1), (0, 3), (0, 0)):
            for core in range(2):
                if (across, along, core) != (0, 0, 0):
                    pair = row // 2
                    peer = (
                        (pair // 4 + across) % 2 * 8 + (pair + along) % 4 * 2 + (row + core) % 2
                    )
                    swap(which, peer).start()

        landed[which, row] = spread[which, row]

    def swap_wait(which):
        @pl.loop(1, PEERS)
        def _(step):
            peer = (row + step) % PEERS
            pltpu.make_async_remote_copy(
                src_ref=spread.at[which, peer],
                dst_ref=landed.at[which, peer],
                send_sem=swap_send.at[which, peer],
                recv_sem=swap_recv.at[which, peer],
                device_id={"row": peer},
                device_id_type=MESH,
            ).wait_recv()

    def gather_in(which):
        for half in range(2):
            blocks = [landed[which, 8 * half + peer, 8:SENT, :] for peer in range(8)]
            for unit, block in enumerate(exchange(blocks, LONG, lane)):
                part, group = unit // 4, unit % 4
                start = 256 * part + 128 * half
                wide[24 * group : 24 * group + CELLS, start : start + 128] = block
        blocks = exchange([landed[which, peer, 0:8, :] for peer in range(PEERS)], 4, lane[:8])
        low = lane[:8] < 64
        for group in range(4):
            folds = (
                jnp.where(low, blocks[group], pltpu.roll(blocks[4 + group], 64, 1)),
                jnp.where(low, blocks[8 + group], pltpu.roll(blocks[12 + group], 64, 1)),
                jnp.where(low, pltpu.roll(blocks[group], 64, 1), blocks[4 + group]),
            )
            for number, fold in enumerate(folds):
                at = 24 * group + 8 * number
                wide[at : at + 8, 512:] = fold
        high, low = split(wide[...])
        both = dot(jnp.concatenate([high, low], axis=0), second_high[...])
        return both[:96] + both[96:] + dot(high, second_low[...])

    def halves(ref, group):
        lines_now = ref[group // 2, :, group % 2, :]
        tiles = [lines_now[:, 128 * tile : 128 * tile + 128] for tile in range(5)]
        low = lane < 64
        turned = [pltpu.roll(tile, 64, 1) for tile in tiles[2:]]
        zero = jnp.zeros_like(tiles[0])
        return (
            tiles[:2] + [jnp.where(low, tiles[2], zero)],
            [
                jnp.where(low, turned[0], turned[1]),
                jnp.where(low, turned[1], turned[2]),
                jnp.where(low, turned[2], zero),
            ],
        )

    def whole_lines(real, imag):
        low = lane < 64
        turned = [pltpu.roll(imag[:, 128 * tile : 128 * tile + 128], 64, 1) for tile in range(3)]
        tiles = [
            real[:, :128],
            real[:, 128:256],
            jnp.where(low, real[:, 256:], turned[0]),
            jnp.where(low, turned[0], turned[1]),
            jnp.where(low, turned[1], turned[2]),
        ]
        return jnp.concatenate(tiles, axis=1)

    def put_lines(ref):
        for group in range(4):
            real, imag = halves(ref, group)
            put_rows(group, jnp.concatenate(real, axis=1), jnp.concatenate(imag, axis=1))

    lines[...] = jnp.zeros_like(lines)
    loads[0].wait()
    put_lines(kspace)
    loads[1].wait()
    loads[2].wait()
    for load in loads[4:]:
        load.start()
    spread_out(0)

    near_count = jnp.int32(0)
    for step, across in near_by:
        near_count = near_count + jnp.where(jnp.logical_and(owns, neighbour(step)[2]), 1, 0)
    pl.semaphore_wait(barrier, PEERS - 1 + 2 * REACH + near_count)

    @pl.loop(1, REACH + 1)
    def _(step):
        for sign in (1, -1):
            pl.semaphore_signal(
                greet_far,
                inc=1,
                device_id={"coil": (coil + sign * step) % COIL_PEERS},
                device_id_type=MESH,
            )


    swap_start(0)
    loads[3].wait()
    put_lines(cotangent)
    spread_out(1)
    swap_start(1)

    wide[...] = jnp.zeros_like(wide)
    maps[...] = jnp.zeros_like(maps)
    loads[4].wait()
    for group in range(4):
        for half, tiles in enumerate(halves(sens, group)):
            for number, tile in enumerate(tiles):
                start = half * HALF + 128 * number
                maps[group, :CELLS, start : start + 128] = tile
    for load in loads[5:]:
        load.wait()
    weights = w_first[...].reshape(54, HID)
    weights_rows = exact_dot(repeat[...], weights, ((1,), (1,)))
    forward_matrix = jnp.zeros((HID * 4, 144), jnp.float32)
    for e2 in range(3):
        forward_matrix += place[e2] * exact_dot(weights_rows, pick[e2])
    weights_back = exact_dot(weights, repeat[...], ((1,), (1,)))
    backward_matrix = jnp.sum(
        (exact_dot(pick_back[...], weights_back) * place_back[...]).reshape(3, 48, HID * 4), axis=0
    )
    last_columns = exact_dot(repeat[...], w_last[...], ((1,), (1,)))
    last_matrix = place_last[...] * exact_dot(
        pick_last[...], exact_dot(w_last[...], repeat[...], ((1,), (1,)))
    )
    forward_pair, backward_pair, last_pair = map(
        pair, (forward_matrix, backward_matrix, last_matrix)
    )

    def part_sums(which, total_field):
        for plane in range(2):
            real = imag = None
            for local_coil in range(2):
                group = local_coil * 2 + plane
                map_real, map_imag = maps[group, :, :HALF], maps[group, :, HALF:]
                field = total_field[24 * group : 24 * group + 24]
                field_real, field_imag = field[:, :HALF], field[:, HALF:]
                this_real = map_real * field_real + map_imag * field_imag
                this_imag = map_real * field_imag - map_imag * field_real
                real = this_real if real is None else real + this_real
                imag = this_imag if imag is None else imag + this_imag
            last = real[:, 256:] + pltpu.roll(imag[:, 256:], 64, 1)
            for target in range(OWNERS):
                cut = slice(2 * target, 2 * target + 2)
                for half in range(2):
                    lanes = slice(128 * half, 128 * half + 128)
                    at = 8 * half + 2 * plane
                    parts[which, target, at : at + 2, :] = real[cut, lanes]
                    parts[which, target, at + 4 : at + 6, :] = imag[cut, lanes]
                parts[which, target, 16 + 2 * plane : 18 + 2 * plane, :] = last[cut]

    def part_copy(which, target):
        return pltpu.make_async_remote_copy(
            src_ref=parts.at[which, target],
            dst_ref=sums.at[which, coil],
            send_sem=sum_send.at[which, target],
            recv_sem=sum_recv.at[which, coil],
            device_id={"coil": owner_coil(target, row)},
            device_id_type=MESH,
        )

    def part_start(which):
        @pl.loop(0, OWNERS)
        def _(step):
            target = (owner + outward(step, OWNERS // 2)) % OWNERS

            @pl.when(owner_coil(target, row) != coil)
            def _():
                part_copy(which, target).start()

    def part_total(which):
        @pl.loop(1, COIL_PEERS)
        def _(step):
            peer = (coil + step) % COIL_PEERS
            pltpu.make_async_remote_copy(
                src_ref=parts.at[which, 0],
                dst_ref=sums.at[which, peer],
                send_sem=sum_send.at[which, 0],
                recv_sem=sum_recv.at[which, peer],
                device_id={"coil": peer},
                device_id_type=MESH,
            ).wait_recv()

        sums[which, coil] = parts[which, owner]
        total = sums[which, 0]
        for peer in range(1, COIL_PEERS):
            total = total + sums[which, peer]
        return unpack(total)

    def near_copy(which, step, across):
        other_coil, other_row, there = neighbour(step)
        copy = pltpu.make_async_remote_copy(
            src_ref=near.at[which, 1, slab],
            dst_ref=near.at[which, 1 - step, slab],
            send_sem=near_send.at[which, (step + 1) * 2 + across],
            recv_sem=near_recv.at[which, (1 - step) * 2 + across],
            device_id={"coil": other_coil, "slab": (slab + across) % 2, "row": other_row},
            device_id_type=MESH,
        )
        return copy, there

    def near_start(which):
        for step, across in near_by:
            copy, there = near_copy(which, step, across)
            pl.when(there)(copy.start)

    def near_wait(which):
        for step, across in near_by:
            other_coil, other_row, there = neighbour(step)
            copy = pltpu.make_async_remote_copy(
                src_ref=near.at[which, 1, slab],
                dst_ref=near.at[which, 1 + step, (slab + across) % 2],
                send_sem=near_send.at[which, (step + 1) * 2 + across],
                recv_sem=near_recv.at[which, (1 + step) * 2 + across],
                device_id={"coil": other_coil, "slab": (slab + across) % 2, "row": other_row},
                device_id_type=MESH,
            )
            pl.when(there)(copy.wait_recv)

    def put_piece(which, plane, values):
        for half in range(2):
            lanes = slice(128 * half, 128 * half + 128)
            at = 8 * half + 2 * plane
            pieces[which, owner, at : at + 2, :] = values[0:2, lanes]
            pieces[which, owner, at + 4 : at + 6, :] = values[2:4, lanes]
        low = lax.broadcasted_iota(jnp.int32, (2, 128), 1) < LEN - 256
        pieces[which, owner, 16 + 2 * plane : 18 + 2 * plane, :] = jnp.where(
            low, values[0:2, 256:], pltpu.roll(values[2:4, 256:], 64, 1)
        )

    def field_copy(which, step):
        peer = (coil + step) % COIL_PEERS
        return pltpu.make_async_remote_copy(
            src_ref=pieces.at[which, owner],
            dst_ref=pieces.at[which, owner],
            send_sem=field_send.at[which, peer],
            recv_sem=field_recv.at[which, owner],
            device_id={"coil": peer},
            device_id_type=MESH,
        )

    def field_start(which):
        @pl.loop(0, COIL_PEERS - 1)
        def _(step):
            field_copy(which, outward(step, COIL_PEERS // 2)).start()

    def field_wait(which):
        @pl.loop(0, OWNERS)
        def _(target):
            @pl.when(owner_coil(target, row) != coil)
            def _():
                pltpu.make_async_remote_copy(
                    src_ref=pieces.at[which, target],
                    dst_ref=pieces.at[which, target],
                    send_sem=field_send.at[which, 0],
                    recv_sem=field_recv.at[which, target],
                    device_id={"coil": owner_coil(target, row)},
                    device_id_type=MESH,
                ).wait_recv()

        for target in range(OWNERS):
            cut = slice(2 * target, 2 * target + 2)
            for plane in range(2):
                for part in range(2):
                    for half in range(2):
                        at = 8 * half + 4 * part + 2 * plane
                        fields[which, part, plane, cut, 128 * half : 128 * half + 128] = pieces[
                            which, target, at : at + 2, :
                        ]
                last = pieces[which, target, 16 + 2 * plane : 18 + 2 * plane, :]
                fields[which, 0, plane, cut, 256:] = last
                fields[which, 1, plane, cut, 256:] = pltpu.roll(last, 64, 1)

    swap_wait(0)
    total_field = gather_in(0)
    images[0] = total_field
    part_sums(0, total_field)
    pl.semaphore_wait(greet_far, 2 * REACH)
    part_start(0)
    swap_wait(1)
    total_field = gather_in(1)
    images[1] = total_field
    part_sums(1, total_field)
    part_start(1)

    @pl.when(owns)
    def _():
        shifted[...] = jnp.zeros_like(shifted)
        near[0, 1, slab] = part_total(0)
        near_start(0)
        near[1, 1, slab] = part_total(1)
        near_start(1)
        backs[0] = jnp.zeros((48, HALF), jnp.float32)
        backs[4] = jnp.zeros((48, HALF), jnp.float32)
        near_wait(0)
        for part in range(2):
            for side in range(2):
                for plane in range(2):
                    line = part * 4 + plane * 2
                    for step in range(3):
                        shifted[1, part, 1 + 2 * side + plane, 2 * step : 2 * step + 2, :] = near[
                            0, step, side, line : line + 2, :
                        ]
        middle = shifted[1].reshape(2 * 6 * 8, HALF)
        shifted[0] = pltpu.roll(middle, 1, 1).reshape(2, 6, 8, HALF)
        shifted[2] = pltpu.roll(middle, HALF - 1, 1).reshape(2, 6, 8, HALF)
        for plane in range(3):
            pre = dot3(
                forward_pair,
                shifted[:, :, pl.ds(slab + plane, 3)].reshape(144, HALF),
            )
            sigmoid = 1.0 / (1.0 + jnp.exp(-pre))
            acts[plane] = pre * sigmoid
            slopes[plane] = sigmoid * (1.0 + pre * (1.0 - sigmoid))
        for plane in range(2):
            put_piece(0, plane, dot3(last_pair, acts[slab + plane]))
        near_wait(1)
        for part in range(2):
            for side in range(2):
                for plane in range(2):
                    line = part * 4 + plane * 2
                    for again in (0, 4):
                        cot_rows[part, 2 * side + plane, again : again + 1, :] = near[
                            1, 0, side, line + 1 : line + 2, :
                        ]
                        cot_rows[part, 2 * side + plane, again + 1 : again + 3, :] = near[
                            1, 1, side, line : line + 2, :
                        ]
                        cot_rows[part, 2 * side + plane, again + 3 : again + 4, :] = near[
                            1, 2, side, line : line + 1, :
                        ]
        for plane in range(3):
            real = jnp.broadcast_to(cot_rows[0, slab + plane][None], (9, 8, HALF))
            imag = jnp.broadcast_to(cot_rows[1, slab + plane][None], (9, 8, HALF))
            spread_cot = last_columns[:, 0:1] * real.reshape(HID * 4, HALF) + last_columns[
                :, 1:2
            ] * imag.reshape(HID * 4, HALF)
            backs[plane + 1] = dot3(backward_pair, slopes[plane] * spread_cot)
        for plane in range(2):
            back = (
                backs[slab + plane, 0:16]
                + backs[slab + plane + 1, 16:32]
                + backs[slab + plane + 2, 32:48]
            )
            back = (
                pltpu.roll(back[0:4], HALF - 1, 1) + back[4:8] + pltpu.roll(back[8:12], 1, 1)
            )
            put_piece(1, plane, back)
        field_start(1)
        field_start(0)

    field_wait(1)
    for group in range(4):
        plane = group % 2
        other_real, other_imag = fields[1, 0, plane, :CELLS], fields[1, 1, plane, :CELLS]
        real, imag = maps[group, :CELLS, :HALF], maps[group, :CELLS, HALF:]
        put_rows(
            group,
            real * other_real - imag * other_imag,
            -(real * other_imag + imag * other_real),
        )
    spread_out(2)
    swap_start(2)
    stores = [
        Halves(grad_sens, grad_sens_hbm, store_sem, 0),
        Halves(grad_kspace, grad_kspace_hbm, store_sem, 1),
    ]
    field_wait(0)
    for group in range(4):
        plane = group % 2
        at = slice(24 * group, 24 * group + CELLS)
        out_real = out_imag = None
        for which in range(2):
            other_real, other_imag = fields[which, 0, plane, :CELLS], fields[which, 1, plane, :CELLS]
            real, imag = images[1 - which, at, :HALF], images[1 - which, at, HALF:]
            this_real = -(real * other_real + imag * other_imag)
            this_imag = real * other_imag - imag * other_real
            out_real = this_real if out_real is None else out_real + this_real
            out_imag = this_imag if out_imag is None else out_imag + this_imag
        grad_sens[group // 2, :, plane, :] = whole_lines(out_real, out_imag)
    stores[0].start()
    square_row = lax.broadcasted_iota(jnp.int32, (CELLS, CELLS), 0)
    square_column = lax.broadcasted_iota(jnp.int32, (CELLS, CELLS), 1)
    factors = []
    for plane in range(2):
        sampled = jnp.broadcast_to(mask[plane : plane + 1, :].astype(jnp.float32), (CELLS, CELLS))
        column = jnp.sum(
            jnp.where(square_row == square_column, sampled, 0.0), axis=1, keepdims=True
        )
        factors.append(1.0 - eta[0] * column)
    swap_wait(2)
    model = gather_in(2)
    for group in range(4):
        plane = group % 2
        mine = model[24 * group : 24 * group + CELLS]
        grad_kspace[group // 2, :, plane, :] = factors[plane] * cotangent[
            group // 2, :, plane, :
        ] - whole_lines(mine[:, :HALF], -mine[:, HALF:])
    stores[1].start()

    for which in range(3):

        @pl.loop(1, PEERS)
        def _(step):
            swap(which, (row + step) % PEERS).wait_send()

    for which in range(2):

        @pl.loop(0, OWNERS)
        def _(target):
            @pl.when(owner_coil(target, row) != coil)
            def _():
                part_copy(which, target).wait_send()

        @pl.when(owns)
        def _():
            for step, across in near_by:
                copy, there = near_copy(which, step, across)
                pl.when(there)(copy.wait_send)

            @pl.loop(1, COIL_PEERS)
            def _(step):
                field_copy(which, step).wait_send()
    stores[0].wait()
    stores[1].wait()


def hand_on(first, second, first_out, second_out, first_held, second_held, load_sem, store_sem):
    loads = [
        pltpu.make_async_copy(source.at[half], held.at[half], load_sem.at[number, half])
        for number, (source, held) in enumerate(((first, first_held), (second, second_held)))
        for half in range(2)
    ]
    stores = [
        pltpu.make_async_copy(held.at[half], target.at[half], store_sem.at[number, half])
        for number, (held, target) in enumerate(((first_held, first_out), (second_held, second_out)))
        for half in range(2)
    ]
    for load in loads:
        load.start()
    for load, store in zip(loads, stores):
        load.wait()
        store.start()
    for store in stores:
        store.wait()


def local(kspace, cotangent, sens, mask, eta, w_first, w_last):
    constants = [jnp.asarray(array) for array in tables() + selectors()]
    smem = pl.BlockSpec(memory_space=pltpu.SMEM)
    anywhere = pl.BlockSpec(memory_space=pl.ANY)
    f32, b16 = jnp.float32, jnp.bfloat16
    rows = jax.ShapeDtypeStruct((2, CELLS, 2, 2 * LEN), f32)
    results = pl.pallas_call(
        kernel,
        out_shape=(rows, rows),
        in_specs=[anywhere] * 4 + [smem] + [anywhere] * 13,
        out_specs=(anywhere, anywhere),
        scratch_shapes=[
            pltpu.VMEM(rows.shape, f32),
            pltpu.VMEM(rows.shape, f32),
            pltpu.VMEM(rows.shape, f32),
            pltpu.VMEM(mask.shape, jnp.int32),
            pltpu.VMEM((27, 2, HID), f32),
            pltpu.VMEM(w_last.shape, f32),
            *[pltpu.VMEM(array.shape, array.dtype) for array in constants],
            pltpu.VMEM(rows.shape, f32),
            pltpu.VMEM(rows.shape, f32),
            pltpu.VMEM((256, WIDE), f32),
            pltpu.VMEM((3, PEERS, SENT, 128), f32),
            pltpu.VMEM((3, PEERS, SENT, 128), f32),
            pltpu.VMEM((96, 2 * LEN), f32),
            pltpu.VMEM((2, 96, WIDE), f32),
            pltpu.VMEM((4, 24, WIDE), f32),
            pltpu.VMEM((2, OWNERS, 20, 128), f32),
            pltpu.VMEM((2, COIL_PEERS, 20, 128), f32),
            pltpu.VMEM((2, 3, 2, 8, HALF), f32),
            pltpu.VMEM((3, 2, 6, 8, HALF), f32),
            pltpu.VMEM((2, 4, 8, HALF), f32),
            pltpu.VMEM((3, HID * 4, HALF), f32),
            pltpu.VMEM((3, HID * 4, HALF), f32),
            pltpu.VMEM((5, 48, HALF), f32),
            pltpu.VMEM((2, OWNERS, 20, 128), f32),
            pltpu.VMEM((2, 2, 2, 24, HALF), f32),
            pltpu.SemaphoreType.DMA((17, 2)),
            pltpu.SemaphoreType.DMA((2, 2)),
            pltpu.SemaphoreType.DMA((3, PEERS)),
            pltpu.SemaphoreType.DMA((3, PEERS)),
            pltpu.SemaphoreType.DMA((2, OWNERS)),
            pltpu.SemaphoreType.DMA((2, COIL_PEERS)),
            pltpu.SemaphoreType.DMA((2, 6)),
            pltpu.SemaphoreType.DMA((2, 6)),
            pltpu.SemaphoreType.DMA((2, COIL_PEERS)),
            pltpu.SemaphoreType.DMA((2, OWNERS)),
            pltpu.SemaphoreType.REGULAR,
        ],
        compiler_params=pltpu.CompilerParams(
            collective_id=0, has_side_effects=True, vmem_limit_bytes=62 * 1024 * 1024
        ),
    )(
        kspace.transpose(0, 2, 1, 3),
        cotangent.transpose(0, 2, 1, 3),
        sens.transpose(0, 2, 1, 3),
        mask,
        eta,
        w_first.transpose(2, 3, 4, 1, 0).reshape(27, 2, HID),
        w_last,
        *constants,
    )
    results = pl.pallas_call(
        hand_on,
        out_shape=(rows, rows),
        in_specs=[anywhere] * 2,
        out_specs=(anywhere, anywhere),
        scratch_shapes=[pltpu.VMEM(rows.shape, f32)] * 2 + [pltpu.SemaphoreType.DMA((2, 2))] * 2,
        compiler_params=pltpu.CompilerParams(vmem_limit_bytes=62 * 1024 * 1024),
    )(*results)
    return tuple(result.transpose(0, 2, 1, 3) for result in results)


def solution(mesh):
    part = P("coil", "slab", "row", None)
    return jax.shard_map(
        local,
        mesh=mesh,
        in_specs=(part, part, part, P("slab", "row"), P(), P(), P()),
        out_specs=(part, part),
        check_vma=False,
    )
```

```python
import math

import jax
import jax.numpy as jnp
import ml_dtypes
import numpy as np
from jax import lax
from jax.experimental import pallas as pl
from jax.experimental.pallas import tpu as pltpu
from jax.sharding import PartitionSpec as P

MESH = pl.DeviceIdType.MESH
LEN = 320
HALF = 384
WIDE = 2 * HALF
CELLS = 20
LONG = 16
PEERS = 16
COIL_PEERS = 16
SENT = 8 + CELLS
REACH = 4
OWNERS = 10
SHARED = OWNERS // 2
HID = 18


def outward(step, middle):
    return middle + (1 - 2 * (step % 2)) * ((step + 1) // 2)


def turned(owner, row):
    return owner + (row % 2) * (OWNERS - 1 - 2 * owner)


def owner_coil(owner, row):
    return (8 * turned(owner, row)) // 5


def coil_owner(coil, row):
    return turned((5 * coil + 7) // 8, row)


def split_table(table):
    high = table.astype(ml_dtypes.bfloat16)
    low = (table - high.astype(np.float64)).astype(ml_dtypes.bfloat16)
    return high, low


def tables():
    at = np.arange(LEN)
    angle = 2.0 * math.pi * ((at[:, None] * at[None, :]) % LEN) / LEN
    cosine, sine = np.cos(angle) / math.sqrt(LEN), np.sin(angle) / math.sqrt(LEN)
    first = np.zeros((PEERS, 24, 2, HALF))
    first[:, :CELLS, 0, :LEN] = cosine.reshape(PEERS, CELLS, LEN)
    first[:, :CELLS, 1, :LEN] = sine.reshape(PEERS, CELLS, LEN)
    line = np.arange(LEN).reshape(PEERS, CELLS)
    long, short = line[:, :LONG].reshape(-1), line[:, LONG:].reshape(-1)
    second = np.zeros((2 * LEN, 2, HALF))
    for part, rows in enumerate(((cosine, sine), (-sine, cosine))):
        for half in range(2):
            second[256 * part : 256 * part + 256, half, :LEN] = rows[half][long]
            second[512 + 64 * part : 576 + 64 * part, half, :LEN] = rows[half][short]
    return split_table(first.reshape(PEERS * 24, WIDE)) + split_table(
        second.reshape(2 * LEN, WIDE)
    )


def selectors():
    repeat = np.zeros((HID * 4, HID), np.float32)
    for unit in range(HID):
        repeat[4 * unit : 4 * unit + 4, unit] = 1.0
    pick = np.zeros((3, 54, 144), np.float32)
    place = np.zeros((3, HID * 4, 144), np.float32)
    for column in range(144):
        e3, channel, e1, row = column // 48, column // 24 % 2, column // 8 % 3, column % 8
        for e2 in range(3):
            pick[e2, 2 * (e1 * 9 + e2 * 3 + e3) + channel, column] = 1.0
            for line in range(HID * 4):
                if row - line % 4 == e2:
                    place[e2, line, column] = 1.0
    pick_back = np.zeros((3, 3, 16, 54), np.float32)
    place_back = np.zeros((3, 3, 16, HID * 4), np.float32)
    for e2 in range(3):
        for plane in range(3):
            for line in range(12):
                e3, channel, row = line // 4, line // 2 % 2, line % 2
                pick_back[e2, plane, line, 2 * ((2 - plane) * 9 + e2 * 3 + e3) + channel] = 1.0
                for column in range(HID * 4):
                    if row + 2 - column % 4 == e2:
                        place_back[e2, plane, line, column] = 1.0
    place_last = np.zeros((8, HID * 4), np.float32)
    pick_last = np.zeros((8, 2), np.float32)
    for line in range(4):
        pick_last[line, line // 2] = 1.0
        for column in range(HID * 4):
            if column % 4 == line % 2 + 1:
                place_last[line, column] = 1.0
    return (
        repeat,
        pick,
        place,
        pick_back.reshape(144, 54),
        place_back.reshape(144, HID * 4),
        place_last,
        pick_last,
    )


def unpack(packed):
    low = lax.broadcasted_iota(jnp.int32, (4, 128), 1) < LEN - 256
    last = packed[16:20]
    upper = jnp.where(low, last, 0.0)
    lower = jnp.where(low, pltpu.roll(last, 64, 1), 0.0)
    return jnp.concatenate(
        [packed[0:8], packed[8:16], jnp.concatenate([upper, lower], axis=0)], axis=1
    )


def split(values):
    high = values.astype(jnp.bfloat16)
    return high, (values - high.astype(jnp.float32)).astype(jnp.bfloat16)


def dot(left, right, dims=((1,), (0,))):
    return lax.dot_general(left, right, (dims, ((), ())), preferred_element_type=jnp.float32)


def pair(left):
    high = left.astype(jnp.bfloat16).astype(jnp.float32)
    both = jnp.concatenate([high, left - high], axis=0)
    return both.astype(jnp.bfloat16), high.astype(jnp.bfloat16)


def dot3(left_pair, right):
    both_left, left_high = left_pair
    rows = left_high.shape[0]
    right_high, right_low = split(right)
    both = dot(both_left, right_high)
    return both[:rows] + both[rows:] + dot(left_high, right_low)


def exchange(blocks, width, lane):
    blocks = list(blocks)
    step = 1
    while step < len(blocks):
        shift = width * step
        low = (lane & shift) == 0
        for first in range(len(blocks)):
            if first & step:
                continue
            upper, lower = blocks[first], blocks[first + step]
            blocks[first] = jnp.where(low, upper, pltpu.roll(lower, shift, 1))
            blocks[first + step] = jnp.where(low, pltpu.roll(upper, 128 - shift, 1), lower)
        step *= 2
    return blocks


def exact_dot(left, right, dims=((1,), (0,))):
    return lax.dot_general(
        left,
        right,
        (dims, ((), ())),
        precision=lax.Precision.HIGHEST,
        preferred_element_type=jnp.float32,
    )


class Halves:
    def __init__(self, source, target, sems, number):
        rows = source.shape[0] // 2
        self.copies = [
            pltpu.make_async_copy(
                source.at[pl.ds(half * rows, rows)],
                target.at[pl.ds(half * rows, rows)],
                sems.at[number, half],
            )
            for half in range(2)
        ]

    def start(self):
        for copy in self.copies:
            copy.start()

    def wait(self):
        for copy in self.copies:
            copy.wait()


def kernel(*refs):
    (
        kspace_hbm,
        cotangent_hbm,
        sens_hbm,
        mask_hbm,
        eta,
        w_first_hbm,
        w_last_hbm,
        *constants_hbm,
    ) = refs[:18]
    grad_kspace_hbm, grad_sens_hbm = refs[18:20]
    (
        kspace,
        cotangent,
        sens,
        mask,
        w_first,
        w_last,
        first_high,
        first_low,
        second_high,
        second_low,
        repeat,
        pick,
        place,
        pick_back,
        place_back,
        place_last,
        pick_last,
        grad_kspace,
        grad_sens,
        lines,
        spread,
        landed,
        wide,
        images,
        maps,
        parts,
        paired,
        sums,
        near,
        shifted,
        cot_rows,
        acts,
        slopes,
        backs,
        pieces,
        fields,
        load_sem,
        store_sem,
        swap_send,
        swap_recv,
        pair_send,
        pair_recv,
        sum_send,
        sum_recv,
        near_send,
        near_recv,
        field_send,
        field_recv,
        greet_far,
    ) = refs[20:]
    coil, slab, row = lax.axis_index("coil"), lax.axis_index("slab"), lax.axis_index("row")
    owner = coil_owner(coil, row)
    owns = owner_coil(owner, row) == coil

    def neighbour(step):
        other = owner + step
        other_row = row + jnp.where(other < 0, -1, 0) + jnp.where(other >= OWNERS, 1, 0)
        there = jnp.logical_and(other_row >= 0, other_row < PEERS)
        return owner_coil((other + OWNERS) % OWNERS, other_row), other_row, there

    near_by = [(-1, 1), (1, 1), (0, 1), (-1, 0), (1, 0)]

    sources = [kspace_hbm, *constants_hbm[:2], cotangent_hbm, sens_hbm, *constants_hbm[2:4]]
    targets = [kspace, first_high, first_low, cotangent, sens, second_high, second_low]
    sources += [w_first_hbm, w_last_hbm, mask_hbm, *constants_hbm[4:]]
    targets += [w_first, w_last, mask, repeat, pick, place, pick_back, place_back]
    targets += [place_last, pick_last]
    loads = []
    for number, (source, target) in enumerate(zip(sources, targets)):
        if number < 7:
            loads.append(Halves(source, target, load_sem, number))
        else:
            loads.append(pltpu.make_async_copy(source, target, load_sem.at[number, 0]))
    for load in loads[:4]:
        load.start()

    near[...] = jnp.zeros_like(near)

    barrier = pltpu.get_barrier_semaphore()

    @pl.loop(1, PEERS)
    def _(step):
        pl.semaphore_signal(
            barrier, inc=1, device_id={"row": (row + step) % PEERS}, device_id_type=MESH
        )

    @pl.loop(1, REACH + 1)
    def _(step):
        for sign in (1, -1):
            pl.semaphore_signal(
                barrier,
                inc=1,
                device_id={"coil": (coil + sign * step) % COIL_PEERS},
                device_id_type=MESH,
            )

    for step, across in near_by:
        other_coil, other_row, there = neighbour(step)

        @pl.when(jnp.logical_and(owns, there))
        def _():
            pl.semaphore_signal(
                barrier,
                inc=1,
                device_id={
                    "coil": other_coil,
                    "slab": (slab + across) % 2,
                    "row": other_row,
                },
                device_id_type=MESH,
            )

    lane = lax.broadcasted_iota(jnp.int32, (CELLS, 128), 1)

    def put_rows(group, real, imag):
        for part, (first, second) in enumerate(((real, -imag), (imag, real))):
            at = 64 * part + LONG * group
            lines[at : at + LONG, :HALF] = first[:LONG]
            lines[at : at + LONG, HALF:] = second[:LONG]
            at = 128 + 16 * part + 4 * group
            lines[at : at + 4, :HALF] = first[LONG:]
            lines[at : at + 4, HALF:] = second[LONG:]

    def spread_out(which):
        high, low = split(lines[...])
        right = jnp.concatenate([high[:128], low[:128], high[128:192], low[128:192]], axis=0)
        both = dot(first_high[...], right, ((1,), (1,)))
        rest = dot(first_low[...], high, ((1,), (1,)))
        long = both[:, :128] + both[:, 128:256] + rest[:, :128]
        short = both[:, 256:] + pltpu.roll(both[:, 256:], 64, 1) + rest[:, 128:]
        folds = short.reshape(PEERS, 3, 8, 128)
        second = pltpu.roll(folds[:, 1].reshape(PEERS * 8, 128), 32, 1)
        third = pltpu.roll(folds[:, 2].reshape(PEERS * 8, 128), 64, 1)
        at = lax.broadcasted_iota(jnp.int32, (PEERS * 8, 128), 1)
        fold = jnp.where(
            at < 32,
            folds[:, 0].reshape(PEERS * 8, 128),
            jnp.where(at < 64, second, jnp.where(at < 96, third, 0.0)),
        )
        spread[which, :, 0:8, :] = fold.reshape(PEERS, 8, 128)
        spread[which, :, 8:SENT, :] = long.reshape(PEERS, 24, 128)[:, :CELLS]

    def swap(which, peer):
        return pltpu.make_async_remote_copy(
            src_ref=spread.at[which, peer],
            dst_ref=landed.at[which, row],
            send_sem=swap_send.at[which, peer],
            recv_sem=swap_recv.at[which, row],
            device_id={"row": peer},
            device_id_type=MESH,
        )

    def swap_start(which):
        for across, along in ((1, 2), (0, 2), (1, 1), (1, 3), (1, 0), (0, 1), (0, 3), (0, 0)):
            for core in range(2):
                if (across, along, core) != (0, 0, 0):
                    pair = row // 2
                    peer = (
                        (pair // 4 + across) % 2 * 8 + (pair + along) % 4 * 2 + (row + core) % 2
                    )
                    swap(which, peer).start()

        landed[which, row] = spread[which, row]

    def swap_wait(which):
        @pl.loop(1, PEERS)
        def _(step):
            peer = (row + step) % PEERS
            pltpu.make_async_remote_copy(
                src_ref=spread.at[which, peer],
                dst_ref=landed.at[which, peer],
                send_sem=swap_send.at[which, peer],
                recv_sem=swap_recv.at[which, peer],
                device_id={"row": peer},
                device_id_type=MESH,
            ).wait_recv()

    def gather_in(which):
        for half in range(2):
            blocks = [landed[which, 8 * half + peer, 8:SENT, :] for peer in range(8)]
            for unit, block in enumerate(exchange(blocks, LONG, lane)):
                part, group = unit // 4, unit % 4
                start = 256 * part + 128 * half
                wide[24 * group : 24 * group + CELLS, start : start + 128] = block
        blocks = exchange([landed[which, peer, 0:8, :] for peer in range(PEERS)], 4, lane[:8])
        low = lane[:8] < 64
        for group in range(4):
            folds = (
                jnp.where(low, blocks[group], pltpu.roll(blocks[4 + group], 64, 1)),
                jnp.where(low, blocks[8 + group], pltpu.roll(blocks[12 + group], 64, 1)),
                jnp.where(low, pltpu.roll(blocks[group], 64, 1), blocks[4 + group]),
            )
            for number, fold in enumerate(folds):
                at = 24 * group + 8 * number
                wide[at : at + 8, 512:] = fold
        high, low = split(wide[...])
        both = dot(jnp.concatenate([high, low], axis=0), second_high[...])
        return both[:96] + both[96:] + dot(high, second_low[...])

    def halves(ref, group):
        lines_now = ref[group // 2, :, group % 2, :]
        tiles = [lines_now[:, 128 * tile : 128 * tile + 128] for tile in range(5)]
        low = lane < 64
        turned = [pltpu.roll(tile, 64, 1) for tile in tiles[2:]]
        zero = jnp.zeros_like(tiles[0])
        return (
            tiles[:2] + [jnp.where(low, tiles[2], zero)],
            [
                jnp.where(low, turned[0], turned[1]),
                jnp.where(low, turned[1], turned[2]),
                jnp.where(low, turned[2], zero),
            ],
        )

    def whole_lines(real, imag):
        low = lane < 64
        turned = [pltpu.roll(imag[:, 128 * tile : 128 * tile + 128], 64, 1) for tile in range(3)]
        tiles = [
            real[:, :128],
            real[:, 128:256],
            jnp.where(low, real[:, 256:], turned[0]),
            jnp.where(low, turned[0], turned[1]),
            jnp.where(low, turned[1], turned[2]),
        ]
        return jnp.concatenate(tiles, axis=1)

    def put_lines(ref):
        for group in range(4):
            real, imag = halves(ref, group)
            put_rows(group, jnp.concatenate(real, axis=1), jnp.concatenate(imag, axis=1))

    lines[...] = jnp.zeros_like(lines)
    loads[0].wait()
    put_lines(kspace)
    loads[1].wait()
    loads[2].wait()
    for load in loads[4:]:
        load.start()
    spread_out(0)

    near_count = jnp.int32(0)
    for step, across in near_by:
        near_count = near_count + jnp.where(jnp.logical_and(owns, neighbour(step)[2]), 1, 0)
    pl.semaphore_wait(barrier, PEERS - 1 + 2 * REACH + near_count)

    @pl.loop(1, REACH + 1)
    def _(step):
        for sign in (1, -1):
            pl.semaphore_signal(
                greet_far,
                inc=1,
                device_id={"coil": (coil + sign * step) % COIL_PEERS},
                device_id_type=MESH,
            )


    swap_start(0)
    loads[3].wait()
    put_lines(cotangent)
    spread_out(1)
    swap_start(1)

    wide[...] = jnp.zeros_like(wide)
    maps[...] = jnp.zeros_like(maps)
    loads[4].wait()
    for group in range(4):
        for half, tiles in enumerate(halves(sens, group)):
            for number, tile in enumerate(tiles):
                start = half * HALF + 128 * number
                maps[group, :CELLS, start : start + 128] = tile
    for load in loads[5:]:
        load.wait()
    weights = w_first[...].reshape(54, HID)
    weights_rows = exact_dot(repeat[...], weights, ((1,), (1,)))
    forward_matrix = jnp.zeros((HID * 4, 144), jnp.float32)
    for e2 in range(3):
        forward_matrix += place[e2] * exact_dot(weights_rows, pick[e2])
    weights_back = exact_dot(weights, repeat[...], ((1,), (1,)))
    backward_matrix = jnp.sum(
        (exact_dot(pick_back[...], weights_back) * place_back[...]).reshape(3, 48, HID * 4), axis=0
    )
    last_columns = exact_dot(repeat[...], w_last[...], ((1,), (1,)))
    last_matrix = place_last[...] * exact_dot(
        pick_last[...], exact_dot(w_last[...], repeat[...], ((1,), (1,)))
    )
    forward_pair, backward_pair, last_pair = map(
        pair, (forward_matrix, backward_matrix, last_matrix)
    )

    def part_sums(which, total_field):
        for plane in range(2):
            real = imag = None
            for local_coil in range(2):
                group = local_coil * 2 + plane
                map_real, map_imag = maps[group, :, :HALF], maps[group, :, HALF:]
                field = total_field[24 * group : 24 * group + 24]
                field_real, field_imag = field[:, :HALF], field[:, HALF:]
                this_real = map_real * field_real + map_imag * field_imag
                this_imag = map_real * field_imag - map_imag * field_real
                real = this_real if real is None else real + this_real
                imag = this_imag if imag is None else imag + this_imag
            last = real[:, 256:] + pltpu.roll(imag[:, 256:], 64, 1)
            for target in range(OWNERS):
                cut = slice(2 * target, 2 * target + 2)
                at_piece = target % 2 * SHARED + target // 2
                for half in range(2):
                    lanes = slice(128 * half, 128 * half + 128)
                    at = 8 * half + 2 * plane
                    parts[which, at_piece, at : at + 2, :] = real[cut, lanes]
                    parts[which, at_piece, at + 4 : at + 6, :] = imag[cut, lanes]
                parts[which, at_piece, 16 + 2 * plane : 18 + 2 * plane, :] = last[cut]

    parity = coil % 2

    def piece_of(target):
        return target % 2 * SHARED + target // 2

    def pair_copy(which):
        return pltpu.make_async_remote_copy(
            src_ref=parts.at[which, pl.ds((1 - parity) * SHARED, SHARED)],
            dst_ref=paired.at[which],
            send_sem=pair_send.at[which],
            recv_sem=pair_recv.at[which],
            device_id={"coil": coil + 1 - 2 * parity},
            device_id_type=MESH,
        )

    def part_copy(which, number):
        return pltpu.make_async_remote_copy(
            src_ref=parts.at[which, parity * SHARED + number],
            dst_ref=sums.at[which, coil // 2],
            send_sem=sum_send.at[which, number],
            recv_sem=sum_recv.at[which, coil // 2],
            device_id={"coil": owner_coil(2 * number + parity, row)},
            device_id_type=MESH,
        )

    def part_start(which):
        pair_copy(which).wait_recv()
        mine = pl.ds(parity * SHARED, SHARED)
        parts[which, mine] = parts[which, mine] + paired[which]

        @pl.loop(0, SHARED)
        def _(step):
            number = (owner // 2 + outward(step, SHARED // 2)) % SHARED

            @pl.when(owner_coil(2 * number + parity, row) != coil)
            def _():
                part_copy(which, number).start()

    def part_total(which):
        @pl.loop(0, COIL_PEERS // 2)
        def _(number):
            peer = 2 * number + owner % 2

            @pl.when(peer != coil)
            def _():
                pltpu.make_async_remote_copy(
                    src_ref=parts.at[which, 0],
                    dst_ref=sums.at[which, number],
                    send_sem=sum_send.at[which, 0],
                    recv_sem=sum_recv.at[which, number],
                    device_id={"coil": peer},
                    device_id_type=MESH,
                ).wait_recv()

        @pl.when(owner % 2 == parity)
        def _():
            sums[which, coil // 2] = parts[which, piece_of(owner)]

        total = sums[which, 0]
        for number in range(1, COIL_PEERS // 2):
            total = total + sums[which, number]
        return unpack(total)

    def near_copy(which, step, across):
        other_coil, other_row, there = neighbour(step)
        copy = pltpu.make_async_remote_copy(
            src_ref=near.at[which, 1, slab],
            dst_ref=near.at[which, 1 - step, slab],
            send_sem=near_send.at[which, (step + 1) * 2 + across],
            recv_sem=near_recv.at[which, (1 - step) * 2 + across],
            device_id={"coil": other_coil, "slab": (slab + across) % 2, "row": other_row},
            device_id_type=MESH,
        )
        return copy, there

    def near_start(which):
        for step, across in near_by:
            copy, there = near_copy(which, step, across)
            pl.when(there)(copy.start)

    def near_wait(which):
        for step, across in near_by:
            other_coil, other_row, there = neighbour(step)
            copy = pltpu.make_async_remote_copy(
                src_ref=near.at[which, 1, slab],
                dst_ref=near.at[which, 1 + step, (slab + across) % 2],
                send_sem=near_send.at[which, (step + 1) * 2 + across],
                recv_sem=near_recv.at[which, (1 + step) * 2 + across],
                device_id={"coil": other_coil, "slab": (slab + across) % 2, "row": other_row},
                device_id_type=MESH,
            )
            pl.when(there)(copy.wait_recv)

    def put_piece(which, plane, values):
        for half in range(2):
            lanes = slice(128 * half, 128 * half + 128)
            at = 8 * half + 2 * plane
            pieces[which, owner, at : at + 2, :] = values[0:2, lanes]
            pieces[which, owner, at + 4 : at + 6, :] = values[2:4, lanes]
        low = lax.broadcasted_iota(jnp.int32, (2, 128), 1) < LEN - 256
        pieces[which, owner, 16 + 2 * plane : 18 + 2 * plane, :] = jnp.where(
            low, values[0:2, 256:], pltpu.roll(values[2:4, 256:], 64, 1)
        )

    def field_copy(which, step):
        peer = (coil + step) % COIL_PEERS
        return pltpu.make_async_remote_copy(
            src_ref=pieces.at[which, owner],
            dst_ref=pieces.at[which, owner],
            send_sem=field_send.at[which, peer],
            recv_sem=field_recv.at[which, owner],
            device_id={"coil": peer},
            device_id_type=MESH,
        )

    def field_start(which):
        @pl.loop(0, COIL_PEERS - 1)
        def _(step):
            field_copy(which, outward(step, COIL_PEERS // 2)).start()

    def field_wait(which):
        @pl.loop(0, OWNERS)
        def _(target):
            @pl.when(owner_coil(target, row) != coil)
            def _():
                pltpu.make_async_remote_copy(
                    src_ref=pieces.at[which, target],
                    dst_ref=pieces.at[which, target],
                    send_sem=field_send.at[which, 0],
                    recv_sem=field_recv.at[which, target],
                    device_id={"coil": owner_coil(target, row)},
                    device_id_type=MESH,
                ).wait_recv()

        for target in range(OWNERS):
            cut = slice(2 * target, 2 * target + 2)
            for plane in range(2):
                for part in range(2):
                    for half in range(2):
                        at = 8 * half + 4 * part + 2 * plane
                        fields[which, part, plane, cut, 128 * half : 128 * half + 128] = pieces[
                            which, target, at : at + 2, :
                        ]
                last = pieces[which, target, 16 + 2 * plane : 18 + 2 * plane, :]
                fields[which, 0, plane, cut, 256:] = last
                fields[which, 1, plane, cut, 256:] = pltpu.roll(last, 64, 1)

    swap_wait(0)
    total_field = gather_in(0)
    images[0] = total_field
    part_sums(0, total_field)
    pair_copy(0).start()
    swap_wait(1)
    total_field = gather_in(1)
    images[1] = total_field
    part_sums(1, total_field)
    pair_copy(1).start()
    pl.semaphore_wait(greet_far, 2 * REACH)
    part_start(0)
    part_start(1)

    @pl.when(owns)
    def _():
        shifted[...] = jnp.zeros_like(shifted)
        near[0, 1, slab] = part_total(0)
        near_start(0)
        near[1, 1, slab] = part_total(1)
        near_start(1)
        backs[0] = jnp.zeros((48, HALF), jnp.float32)
        backs[4] = jnp.zeros((48, HALF), jnp.float32)
        near_wait(0)
        for part in range(2):
            for side in range(2):
                for plane in range(2):
                    line = part * 4 + plane * 2
                    for step in range(3):
                        shifted[1, part, 1 + 2 * side + plane, 2 * step : 2 * step + 2, :] = near[
                            0, step, side, line : line + 2, :
                        ]
        middle = shifted[1].reshape(2 * 6 * 8, HALF)
        shifted[0] = pltpu.roll(middle, 1, 1).reshape(2, 6, 8, HALF)
        shifted[2] = pltpu.roll(middle, HALF - 1, 1).reshape(2, 6, 8, HALF)
        for plane in range(3):
            pre = dot3(
                forward_pair,
                shifted[:, :, pl.ds(slab + plane, 3)].reshape(144, HALF),
            )
            sigmoid = 1.0 / (1.0 + jnp.exp(-pre))
            acts[plane] = pre * sigmoid
            slopes[plane] = sigmoid * (1.0 + pre * (1.0 - sigmoid))
        for plane in range(2):
            put_piece(0, plane, dot3(last_pair, acts[slab + plane]))
        near_wait(1)
        for part in range(2):
            for side in range(2):
                for plane in range(2):
                    line = part * 4 + plane * 2
                    for again in (0, 4):
                        cot_rows[part, 2 * side + plane, again : again + 1, :] = near[
                            1, 0, side, line + 1 : line + 2, :
                        ]
                        cot_rows[part, 2 * side + plane, again + 1 : again + 3, :] = near[
                            1, 1, side, line : line + 2, :
                        ]
                        cot_rows[part, 2 * side + plane, again + 3 : again + 4, :] = near[
                            1, 2, side, line : line + 1, :
                        ]
        for plane in range(3):
            real = jnp.broadcast_to(cot_rows[0, slab + plane][None], (9, 8, HALF))
            imag = jnp.broadcast_to(cot_rows[1, slab + plane][None], (9, 8, HALF))
            spread_cot = last_columns[:, 0:1] * real.reshape(HID * 4, HALF) + last_columns[
                :, 1:2
            ] * imag.reshape(HID * 4, HALF)
            backs[plane + 1] = dot3(backward_pair, slopes[plane] * spread_cot)
        for plane in range(2):
            back = (
                backs[slab + plane, 0:16]
                + backs[slab + plane + 1, 16:32]
                + backs[slab + plane + 2, 32:48]
            )
            back = (
                pltpu.roll(back[0:4], HALF - 1, 1) + back[4:8] + pltpu.roll(back[8:12], 1, 1)
            )
            put_piece(1, plane, back)
        field_start(1)
        field_start(0)

    field_wait(1)
    for group in range(4):
        plane = group % 2
        other_real, other_imag = fields[1, 0, plane, :CELLS], fields[1, 1, plane, :CELLS]
        real, imag = maps[group, :CELLS, :HALF], maps[group, :CELLS, HALF:]
        put_rows(
            group,
            real * other_real - imag * other_imag,
            -(real * other_imag + imag * other_real),
        )
    spread_out(2)
    swap_start(2)
    stores = [
        Halves(grad_sens, grad_sens_hbm, store_sem, 0),
        Halves(grad_kspace, grad_kspace_hbm, store_sem, 1),
    ]
    field_wait(0)
    for group in range(4):
        plane = group % 2
        at = slice(24 * group, 24 * group + CELLS)
        out_real = out_imag = None
        for which in range(2):
            other_real, other_imag = fields[which, 0, plane, :CELLS], fields[which, 1, plane, :CELLS]
            real, imag = images[1 - which, at, :HALF], images[1 - which, at, HALF:]
            this_real = -(real * other_real + imag * other_imag)
            this_imag = real * other_imag - imag * other_real
            out_real = this_real if out_real is None else out_real + this_real
            out_imag = this_imag if out_imag is None else out_imag + this_imag
        grad_sens[group // 2, :, plane, :] = whole_lines(out_real, out_imag)
    stores[0].start()
    square_row = lax.broadcasted_iota(jnp.int32, (CELLS, CELLS), 0)
    square_column = lax.broadcasted_iota(jnp.int32, (CELLS, CELLS), 1)
    factors = []
    for plane in range(2):
        sampled = jnp.broadcast_to(mask[plane : plane + 1, :].astype(jnp.float32), (CELLS, CELLS))
        column = jnp.sum(
            jnp.where(square_row == square_column, sampled, 0.0), axis=1, keepdims=True
        )
        factors.append(1.0 - eta[0] * column)
    swap_wait(2)
    model = gather_in(2)
    for group in range(4):
        plane = group % 2
        mine = model[24 * group : 24 * group + CELLS]
        grad_kspace[group // 2, :, plane, :] = factors[plane] * cotangent[
            group // 2, :, plane, :
        ] - whole_lines(mine[:, :HALF], -mine[:, HALF:])
    stores[1].start()

    for which in range(3):

        @pl.loop(1, PEERS)
        def _(step):
            swap(which, (row + step) % PEERS).wait_send()

    for which in range(2):

        pair_copy(which).wait_send()

        @pl.loop(0, SHARED)
        def _(number):
            @pl.when(owner_coil(2 * number + parity, row) != coil)
            def _():
                part_copy(which, number).wait_send()

        @pl.when(owns)
        def _():
            for step, across in near_by:
                copy, there = near_copy(which, step, across)
                pl.when(there)(copy.wait_send)

            @pl.loop(1, COIL_PEERS)
            def _(step):
                field_copy(which, step).wait_send()
    stores[0].wait()
    stores[1].wait()


def hand_on(first, second, first_out, second_out, first_held, second_held, load_sem, store_sem):
    loads = [
        pltpu.make_async_copy(source.at[half], held.at[half], load_sem.at[number, half])
        for number, (source, held) in enumerate(((first, first_held), (second, second_held)))
        for half in range(2)
    ]
    stores = [
        pltpu.make_async_copy(held.at[half], target.at[half], store_sem.at[number, half])
        for number, (held, target) in enumerate(((first_held, first_out), (second_held, second_out)))
        for half in range(2)
    ]
    for load in loads:
        load.start()
    for load, store in zip(loads, stores):
        load.wait()
        store.start()
    for store in stores:
        store.wait()


def local(kspace, cotangent, sens, mask, eta, w_first, w_last):
    constants = [jnp.asarray(array) for array in tables() + selectors()]
    smem = pl.BlockSpec(memory_space=pltpu.SMEM)
    anywhere = pl.BlockSpec(memory_space=pl.ANY)
    f32, b16 = jnp.float32, jnp.bfloat16
    rows = jax.ShapeDtypeStruct((2, CELLS, 2, 2 * LEN), f32)
    results = pl.pallas_call(
        kernel,
        out_shape=(rows, rows),
        in_specs=[anywhere] * 4 + [smem] + [anywhere] * 13,
        out_specs=(anywhere, anywhere),
        scratch_shapes=[
            pltpu.VMEM(rows.shape, f32),
            pltpu.VMEM(rows.shape, f32),
            pltpu.VMEM(rows.shape, f32),
            pltpu.VMEM(mask.shape, jnp.int32),
            pltpu.VMEM((27, 2, HID), f32),
            pltpu.VMEM(w_last.shape, f32),
            *[pltpu.VMEM(array.shape, array.dtype) for array in constants],
            pltpu.VMEM(rows.shape, f32),
            pltpu.VMEM(rows.shape, f32),
            pltpu.VMEM((256, WIDE), f32),
            pltpu.VMEM((3, PEERS, SENT, 128), f32),
            pltpu.VMEM((3, PEERS, SENT, 128), f32),
            pltpu.VMEM((96, 2 * LEN), f32),
            pltpu.VMEM((2, 96, WIDE), f32),
            pltpu.VMEM((4, 24, WIDE), f32),
            pltpu.VMEM((2, OWNERS, 20, 128), f32),
            pltpu.VMEM((2, SHARED, 20, 128), f32),
            pltpu.VMEM((2, COIL_PEERS // 2, 20, 128), f32),
            pltpu.VMEM((2, 3, 2, 8, HALF), f32),
            pltpu.VMEM((3, 2, 6, 8, HALF), f32),
            pltpu.VMEM((2, 4, 8, HALF), f32),
            pltpu.VMEM((3, HID * 4, HALF), f32),
            pltpu.VMEM((3, HID * 4, HALF), f32),
            pltpu.VMEM((5, 48, HALF), f32),
            pltpu.VMEM((2, OWNERS, 20, 128), f32),
            pltpu.VMEM((2, 2, 2, 24, HALF), f32),
            pltpu.SemaphoreType.DMA((17, 2)),
            pltpu.SemaphoreType.DMA((2, 2)),
            pltpu.SemaphoreType.DMA((3, PEERS)),
            pltpu.SemaphoreType.DMA((3, PEERS)),
            pltpu.SemaphoreType.DMA((2,)),
            pltpu.SemaphoreType.DMA((2,)),
            pltpu.SemaphoreType.DMA((2, SHARED)),
            pltpu.SemaphoreType.DMA((2, COIL_PEERS // 2)),
            pltpu.SemaphoreType.DMA((2, 6)),
            pltpu.SemaphoreType.DMA((2, 6)),
            pltpu.SemaphoreType.DMA((2, COIL_PEERS)),
            pltpu.SemaphoreType.DMA((2, OWNERS)),
            pltpu.SemaphoreType.REGULAR,
        ],
        compiler_params=pltpu.CompilerParams(
            collective_id=0, has_side_effects=True, vmem_limit_bytes=62 * 1024 * 1024
        ),
    )(
        kspace.transpose(0, 2, 1, 3),
        cotangent.transpose(0, 2, 1, 3),
        sens.transpose(0, 2, 1, 3),
        mask,
        eta,
        w_first.transpose(2, 3, 4, 1, 0).reshape(27, 2, HID),
        w_last,
        *constants,
    )
    results = pl.pallas_call(
        hand_on,
        out_shape=(rows, rows),
        in_specs=[anywhere] * 2,
        out_specs=(anywhere, anywhere),
        scratch_shapes=[pltpu.VMEM(rows.shape, f32)] * 2 + [pltpu.SemaphoreType.DMA((2, 2))] * 2,
        compiler_params=pltpu.CompilerParams(vmem_limit_bytes=62 * 1024 * 1024),
    )(*results)
    return tuple(result.transpose(0, 2, 1, 3) for result in results)


def solution(mesh):
    part = P("coil", "slab", "row", None)
    return jax.shard_map(
        local,
        mesh=mesh,
        in_specs=(part, part, part, P("slab", "row"), P(), P(), P()),
        out_specs=(part, part),
        check_vma=False,
    )
```

```python
import math

import jax
import jax.numpy as jnp
import ml_dtypes
import numpy as np
from jax import lax
from jax.experimental import pallas as pl
from jax.experimental.pallas import tpu as pltpu
from jax.sharding import PartitionSpec as P

MESH = pl.DeviceIdType.MESH
LEN = 320
HALF = 384
WIDE = 2 * HALF
CELLS = 20
LONG = 16
PEERS = 16
COIL_PEERS = 16
SENT = 8 + CELLS
REACH = 3
OWNERS = 10
SHARED = OWNERS // 2
HID = 18


def outward(step, middle):
    return middle + (1 - 2 * (step % 2)) * ((step + 1) // 2)


def turned(owner, row):
    return owner + (row % 2) * (OWNERS - 1 - 2 * owner)


def owner_coil(owner, row):
    return (8 * turned(owner, row)) // 5


def coil_owner(coil, row):
    return turned((5 * coil + 7) // 8, row)


def split_table(table):
    high = table.astype(ml_dtypes.bfloat16)
    low = (table - high.astype(np.float64)).astype(ml_dtypes.bfloat16)
    return high, low


def tables():
    at = np.arange(LEN)
    angle = 2.0 * math.pi * ((at[:, None] * at[None, :]) % LEN) / LEN
    cosine, sine = np.cos(angle) / math.sqrt(LEN), np.sin(angle) / math.sqrt(LEN)
    first = np.zeros((PEERS, 24, 2, HALF))
    first[:, :CELLS, 0, :LEN] = cosine.reshape(PEERS, CELLS, LEN)
    first[:, :CELLS, 1, :LEN] = sine.reshape(PEERS, CELLS, LEN)
    line = np.arange(LEN).reshape(PEERS, CELLS)
    long, short = line[:, :LONG].reshape(-1), line[:, LONG:].reshape(-1)
    second = np.zeros((2 * LEN, 2, HALF))
    for part, rows in enumerate(((cosine, sine), (-sine, cosine))):
        for half in range(2):
            second[256 * part : 256 * part + 256, half, :LEN] = rows[half][long]
            second[512 + 64 * part : 576 + 64 * part, half, :LEN] = rows[half][short]
    return split_table(first.reshape(PEERS * 24, WIDE)) + split_table(
        second.reshape(2 * LEN, WIDE)
    )


def selectors():
    repeat = np.zeros((HID * 4, HID), np.float32)
    for unit in range(HID):
        repeat[4 * unit : 4 * unit + 4, unit] = 1.0
    pick = np.zeros((3, 54, 144), np.float32)
    place = np.zeros((3, HID * 4, 144), np.float32)
    for column in range(144):
        e3, channel, e1, row = column // 48, column // 24 % 2, column // 8 % 3, column % 8
        for e2 in range(3):
            pick[e2, 2 * (e1 * 9 + e2 * 3 + e3) + channel, column] = 1.0
            for line in range(HID * 4):
                if row - line % 4 == e2:
                    place[e2, line, column] = 1.0
    pick_back = np.zeros((3, 3, 16, 54), np.float32)
    place_back = np.zeros((3, 3, 16, HID * 4), np.float32)
    for e2 in range(3):
        for plane in range(3):
            for line in range(12):
                e3, channel, row = line // 4, line // 2 % 2, line % 2
                pick_back[e2, plane, line, 2 * ((2 - plane) * 9 + e2 * 3 + e3) + channel] = 1.0
                for column in range(HID * 4):
                    if row + 2 - column % 4 == e2:
                        place_back[e2, plane, line, column] = 1.0
    place_last = np.zeros((8, HID * 4), np.float32)
    pick_last = np.zeros((8, 2), np.float32)
    for line in range(4):
        pick_last[line, line // 2] = 1.0
        for column in range(HID * 4):
            if column % 4 == line % 2 + 1:
                place_last[line, column] = 1.0
    return (
        repeat,
        pick,
        place,
        pick_back.reshape(144, 54),
        place_back.reshape(144, HID * 4),
        place_last,
        pick_last,
    )


def unpack(packed):
    low = lax.broadcasted_iota(jnp.int32, (4, 128), 1) < LEN - 256
    last = packed[16:20]
    upper = jnp.where(low, last, 0.0)
    lower = jnp.where(low, pltpu.roll(last, 64, 1), 0.0)
    return jnp.concatenate(
        [packed[0:8], packed[8:16], jnp.concatenate([upper, lower], axis=0)], axis=1
    )


def split(values):
    high = values.astype(jnp.bfloat16)
    return high, (values - high.astype(jnp.float32)).astype(jnp.bfloat16)


def dot(left, right, dims=((1,), (0,))):
    return lax.dot_general(left, right, (dims, ((), ())), preferred_element_type=jnp.float32)


def pair(left):
    high = left.astype(jnp.bfloat16).astype(jnp.float32)
    both = jnp.concatenate([high, left - high], axis=0)
    return both.astype(jnp.bfloat16), high.astype(jnp.bfloat16)


def dot3(left_pair, right):
    both_left, left_high = left_pair
    rows = left_high.shape[0]
    right_high, right_low = split(right)
    both = dot(both_left, right_high)
    return both[:rows] + both[rows:] + dot(left_high, right_low)


def exchange(blocks, width, lane):
    blocks = list(blocks)
    step = 1
    while step < len(blocks):
        shift = width * step
        low = (lane & shift) == 0
        for first in range(len(blocks)):
            if first & step:
                continue
            upper, lower = blocks[first], blocks[first + step]
            blocks[first] = jnp.where(low, upper, pltpu.roll(lower, shift, 1))
            blocks[first + step] = jnp.where(low, pltpu.roll(upper, 128 - shift, 1), lower)
        step *= 2
    return blocks


def exact_dot(left, right, dims=((1,), (0,))):
    return lax.dot_general(
        left,
        right,
        (dims, ((), ())),
        precision=lax.Precision.HIGHEST,
        preferred_element_type=jnp.float32,
    )


class Halves:
    def __init__(self, source, target, sems, number):
        rows = source.shape[0] // 2
        self.copies = [
            pltpu.make_async_copy(
                source.at[pl.ds(half * rows, rows)],
                target.at[pl.ds(half * rows, rows)],
                sems.at[number, half],
            )
            for half in range(2)
        ]

    def start(self):
        for copy in self.copies:
            copy.start()

    def wait(self):
        for copy in self.copies:
            copy.wait()


def kernel(*refs):
    (
        kspace_hbm,
        cotangent_hbm,
        sens_hbm,
        mask_hbm,
        eta,
        w_first_hbm,
        w_last_hbm,
        *constants_hbm,
    ) = refs[:18]
    grad_kspace_hbm, grad_sens_hbm = refs[18:20]
    (
        kspace,
        cotangent,
        sens,
        mask,
        w_first,
        w_last,
        first_high,
        first_low,
        second_high,
        second_low,
        repeat,
        pick,
        place,
        pick_back,
        place_back,
        place_last,
        pick_last,
        grad_kspace,
        grad_sens,
        lines,
        spread,
        landed,
        wide,
        images,
        maps,
        parts,
        paired,
        sums,
        near,
        shifted,
        cot_rows,
        acts,
        slopes,
        backs,
        pieces,
        fields,
        load_sem,
        store_sem,
        swap_send,
        swap_recv,
        pair_send,
        pair_recv,
        sum_send,
        sum_recv,
        near_send,
        near_recv,
        field_send,
        field_recv,
        greet_far,
    ) = refs[20:]
    coil, slab, row = lax.axis_index("coil"), lax.axis_index("slab"), lax.axis_index("row")
    owner = coil_owner(coil, row)
    owns = owner_coil(owner, row) == coil

    def neighbour(step):
        other = owner + step
        other_row = row + jnp.where(other < 0, -1, 0) + jnp.where(other >= OWNERS, 1, 0)
        there = jnp.logical_and(other_row >= 0, other_row < PEERS)
        return owner_coil((other + OWNERS) % OWNERS, other_row), other_row, there

    near_by = [(-1, 1), (1, 1), (0, 1), (-1, 0), (1, 0)]

    sources = [kspace_hbm, *constants_hbm[:2], cotangent_hbm, sens_hbm, *constants_hbm[2:4]]
    targets = [kspace, first_high, first_low, cotangent, sens, second_high, second_low]
    sources += [w_first_hbm, w_last_hbm, mask_hbm, *constants_hbm[4:]]
    targets += [w_first, w_last, mask, repeat, pick, place, pick_back, place_back]
    targets += [place_last, pick_last]
    loads = []
    for number, (source, target) in enumerate(zip(sources, targets)):
        if number < 7:
            loads.append(Halves(source, target, load_sem, number))
        else:
            loads.append(pltpu.make_async_copy(source, target, load_sem.at[number, 0]))
    near[...] = jnp.zeros_like(near)

    barrier = pltpu.get_barrier_semaphore()

    def greet_coil(sem):
        for step in range(REACH, 0, -1):
            for sign in (1, -1):
                pl.semaphore_signal(
                    sem,
                    inc=1,
                    device_id={"coil": (coil + sign * step) % COIL_PEERS},
                    device_id_type=MESH,
                )

    def greet_slab(sem):
        pl.semaphore_signal(sem, inc=1, device_id={"slab": 1 - slab}, device_id_type=MESH)

    @pl.loop(1, PEERS)
    def _(step):
        pl.semaphore_signal(
            barrier, inc=1, device_id={"row": (row + step) % PEERS}, device_id_type=MESH
        )

    greet_coil(barrier)
    greet_slab(barrier)

    for load in loads[:4]:
        load.start()

    lane = lax.broadcasted_iota(jnp.int32, (CELLS, 128), 1)

    def put_rows(group, real, imag):
        for part, (first, second) in enumerate(((real, -imag), (imag, real))):
            at = 64 * part + LONG * group
            lines[at : at + LONG, :HALF] = first[:LONG]
            lines[at : at + LONG, HALF:] = second[:LONG]
            at = 128 + 16 * part + 4 * group
            lines[at : at + 4, :HALF] = first[LONG:]
            lines[at : at + 4, HALF:] = second[LONG:]

    def spread_out(which):
        high, low = split(lines[...])
        right = jnp.concatenate([high[:128], low[:128], high[128:192], low[128:192]], axis=0)
        both = dot(first_high[...], right, ((1,), (1,)))
        rest = dot(first_low[...], high, ((1,), (1,)))
        long = both[:, :128] + both[:, 128:256] + rest[:, :128]
        short = both[:, 256:] + pltpu.roll(both[:, 256:], 64, 1) + rest[:, 128:]
        folds = short.reshape(PEERS, 3, 8, 128)
        second = pltpu.roll(folds[:, 1].reshape(PEERS * 8, 128), 32, 1)
        third = pltpu.roll(folds[:, 2].reshape(PEERS * 8, 128), 64, 1)
        at = lax.broadcasted_iota(jnp.int32, (PEERS * 8, 128), 1)
        fold = jnp.where(
            at < 32,
            folds[:, 0].reshape(PEERS * 8, 128),
            jnp.where(at < 64, second, jnp.where(at < 96, third, 0.0)),
        )
        spread[which, :, 0:8, :] = fold.reshape(PEERS, 8, 128)
        spread[which, :, 8:SENT, :] = long.reshape(PEERS, 24, 128)[:, :CELLS]

    def swap(which, peer):
        return pltpu.make_async_remote_copy(
            src_ref=spread.at[which, peer],
            dst_ref=landed.at[which, row],
            send_sem=swap_send.at[which, peer],
            recv_sem=swap_recv.at[which, row],
            device_id={"row": peer},
            device_id_type=MESH,
        )

    def swap_start(which):
        for across, along in ((1, 2), (0, 2), (1, 1), (1, 3), (1, 0), (0, 1), (0, 3), (0, 0)):
            for core in range(2):
                if (across, along, core) != (0, 0, 0):
                    pair = row // 2
                    peer = (
                        (pair // 4 + across) % 2 * 8 + (pair + along) % 4 * 2 + (row + core) % 2
                    )
                    swap(which, peer).start()

        landed[which, row] = spread[which, row]

    def swap_wait(which):
        @pl.loop(1, PEERS)
        def _(step):
            peer = (row + step) % PEERS
            pltpu.make_async_remote_copy(
                src_ref=spread.at[which, peer],
                dst_ref=landed.at[which, peer],
                send_sem=swap_send.at[which, peer],
                recv_sem=swap_recv.at[which, peer],
                device_id={"row": peer},
                device_id_type=MESH,
            ).wait_recv()

    def swap_settle(which):
        @pl.loop(1, PEERS)
        def _(step):
            swap(which, (row + step) % PEERS).wait_send()

    def gather_in(which):
        for half in range(2):
            blocks = [landed[which, 8 * half + peer, 8:SENT, :] for peer in range(8)]
            for unit, block in enumerate(exchange(blocks, LONG, lane)):
                part, group = unit // 4, unit % 4
                start = 256 * part + 128 * half
                wide[24 * group : 24 * group + CELLS, start : start + 128] = block
        blocks = exchange([landed[which, peer, 0:8, :] for peer in range(PEERS)], 4, lane[:8])
        low = lane[:8] < 64
        for group in range(4):
            folds = (
                jnp.where(low, blocks[group], pltpu.roll(blocks[4 + group], 64, 1)),
                jnp.where(low, blocks[8 + group], pltpu.roll(blocks[12 + group], 64, 1)),
                jnp.where(low, pltpu.roll(blocks[group], 64, 1), blocks[4 + group]),
            )
            for number, fold in enumerate(folds):
                at = 24 * group + 8 * number
                wide[at : at + 8, 512:] = fold
        high, low = split(wide[...])
        both = dot(jnp.concatenate([high, low], axis=0), second_high[...])
        return both[:96] + both[96:] + dot(high, second_low[...])

    def halves(ref, group):
        lines_now = ref[group // 2, :, group % 2, :]
        tiles = [lines_now[:, 128 * tile : 128 * tile + 128] for tile in range(5)]
        low = lane < 64
        turned = [pltpu.roll(tile, 64, 1) for tile in tiles[2:]]
        zero = jnp.zeros_like(tiles[0])
        return (
            tiles[:2] + [jnp.where(low, tiles[2], zero)],
            [
                jnp.where(low, turned[0], turned[1]),
                jnp.where(low, turned[1], turned[2]),
                jnp.where(low, turned[2], zero),
            ],
        )

    def whole_lines(real, imag):
        low = lane < 64
        turned = [pltpu.roll(imag[:, 128 * tile : 128 * tile + 128], 64, 1) for tile in range(3)]
        tiles = [
            real[:, :128],
            real[:, 128:256],
            jnp.where(low, real[:, 256:], turned[0]),
            jnp.where(low, turned[0], turned[1]),
            jnp.where(low, turned[1], turned[2]),
        ]
        return jnp.concatenate(tiles, axis=1)

    def put_lines(ref):
        for group in range(4):
            real, imag = halves(ref, group)
            put_rows(group, jnp.concatenate(real, axis=1), jnp.concatenate(imag, axis=1))

    lines[...] = jnp.zeros_like(lines)
    loads[0].wait()
    put_lines(kspace)
    loads[1].wait()
    loads[2].wait()
    for load in loads[4:]:
        load.start()
    spread_out(0)

    pl.semaphore_wait(barrier, PEERS - 1 + 2 * REACH + 1)
    swap_start(0)
    greet_coil(greet_far.at[0])
    greet_slab(greet_far.at[0])
    loads[3].wait()
    put_lines(cotangent)
    spread_out(1)
    swap_start(1)

    wide[...] = jnp.zeros_like(wide)
    maps[...] = jnp.zeros_like(maps)
    loads[4].wait()
    for group in range(4):
        for half, tiles in enumerate(halves(sens, group)):
            for number, tile in enumerate(tiles):
                start = half * HALF + 128 * number
                maps[group, :CELLS, start : start + 128] = tile
    for load in loads[5:]:
        load.wait()
    weights = w_first[...].reshape(54, HID)
    weights_rows = exact_dot(repeat[...], weights, ((1,), (1,)))
    forward_matrix = jnp.zeros((HID * 4, 144), jnp.float32)
    for e2 in range(3):
        forward_matrix += place[e2] * exact_dot(weights_rows, pick[e2])
    weights_back = exact_dot(weights, repeat[...], ((1,), (1,)))
    backward_matrix = jnp.sum(
        (exact_dot(pick_back[...], weights_back) * place_back[...]).reshape(3, 48, HID * 4), axis=0
    )
    last_columns = exact_dot(repeat[...], w_last[...], ((1,), (1,)))
    last_matrix = place_last[...] * exact_dot(
        pick_last[...], exact_dot(w_last[...], repeat[...], ((1,), (1,)))
    )
    forward_pair, backward_pair, last_pair = map(
        pair, (forward_matrix, backward_matrix, last_matrix)
    )

    def part_sums(which, total_field):
        for plane in range(2):
            real = imag = None
            for local_coil in range(2):
                group = local_coil * 2 + plane
                map_real, map_imag = maps[group, :, :HALF], maps[group, :, HALF:]
                field = total_field[24 * group : 24 * group + 24]
                field_real, field_imag = field[:, :HALF], field[:, HALF:]
                this_real = map_real * field_real + map_imag * field_imag
                this_imag = map_real * field_imag - map_imag * field_real
                real = this_real if real is None else real + this_real
                imag = this_imag if imag is None else imag + this_imag
            last = real[:, 256:] + pltpu.roll(imag[:, 256:], 64, 1)
            for target in range(OWNERS):
                cut = slice(2 * target, 2 * target + 2)
                at_piece = target % 2 * SHARED + target // 2
                for half in range(2):
                    lanes = slice(128 * half, 128 * half + 128)
                    at = 8 * half + 2 * plane
                    parts[which, at_piece, at : at + 2, :] = real[cut, lanes]
                    parts[which, at_piece, at + 4 : at + 6, :] = imag[cut, lanes]
                parts[which, at_piece, 16 + 2 * plane : 18 + 2 * plane, :] = last[cut]

    parity = coil % 2

    def piece_of(target):
        return target % 2 * SHARED + target // 2

    def pair_copy(which):
        return pltpu.make_async_remote_copy(
            src_ref=parts.at[which, pl.ds((1 - parity) * SHARED, SHARED)],
            dst_ref=paired.at[which],
            send_sem=pair_send.at[which],
            recv_sem=pair_recv.at[which],
            device_id={"coil": coil + 1 - 2 * parity},
            device_id_type=MESH,
        )

    def part_copy(which, number):
        return pltpu.make_async_remote_copy(
            src_ref=parts.at[which, parity * SHARED + number],
            dst_ref=sums.at[which, coil // 2],
            send_sem=sum_send.at[which, number],
            recv_sem=sum_recv.at[which, coil // 2],
            device_id={"coil": owner_coil(2 * number + parity, row)},
            device_id_type=MESH,
        )

    def part_start(which):
        pair_copy(which).wait_recv()
        mine = pl.ds(parity * SHARED, SHARED)
        parts[which, mine] = parts[which, mine] + paired[which]

        @pl.loop(0, SHARED)
        def _(step):
            number = (owner // 2 + outward(step, SHARED // 2)) % SHARED

            @pl.when(owner_coil(2 * number + parity, row) != coil)
            def _():
                part_copy(which, number).start()

    def part_total(which):
        @pl.loop(0, COIL_PEERS // 2)
        def _(number):
            peer = 2 * number + owner % 2

            @pl.when(peer != coil)
            def _():
                pltpu.make_async_remote_copy(
                    src_ref=parts.at[which, 0],
                    dst_ref=sums.at[which, number],
                    send_sem=sum_send.at[which, 0],
                    recv_sem=sum_recv.at[which, number],
                    device_id={"coil": peer},
                    device_id_type=MESH,
                ).wait_recv()

        @pl.when(owner % 2 == parity)
        def _():
            sums[which, coil // 2] = parts[which, piece_of(owner)]

        total = sums[which, 0]
        for number in range(1, COIL_PEERS // 2):
            total = total + sums[which, number]
        return unpack(total)

    def near_copy(which, step, across):
        other_coil, other_row, there = neighbour(step)
        copy = pltpu.make_async_remote_copy(
            src_ref=near.at[which, 1, slab],
            dst_ref=near.at[which, 1 - step, slab],
            send_sem=near_send.at[which, (step + 1) * 2 + across],
            recv_sem=near_recv.at[which, (1 - step) * 2 + across],
            device_id={"coil": other_coil, "slab": (slab + across) % 2, "row": other_row},
            device_id_type=MESH,
        )
        return copy, there

    def near_start(which):
        for step, across in near_by:
            copy, there = near_copy(which, step, across)
            pl.when(there)(copy.start)

    def near_wait(which):
        for step, across in near_by:
            other_coil, other_row, there = neighbour(step)
            copy = pltpu.make_async_remote_copy(
                src_ref=near.at[which, 1, slab],
                dst_ref=near.at[which, 1 + step, (slab + across) % 2],
                send_sem=near_send.at[which, (step + 1) * 2 + across],
                recv_sem=near_recv.at[which, (1 + step) * 2 + across],
                device_id={"coil": other_coil, "slab": (slab + across) % 2, "row": other_row},
                device_id_type=MESH,
            )
            pl.when(there)(copy.wait_recv)

    def put_piece(which, plane, values):
        for half in range(2):
            lanes = slice(128 * half, 128 * half + 128)
            at = 8 * half + 2 * plane
            pieces[which, owner, at : at + 2, :] = values[0:2, lanes]
            pieces[which, owner, at + 4 : at + 6, :] = values[2:4, lanes]
        low = lax.broadcasted_iota(jnp.int32, (2, 128), 1) < LEN - 256
        pieces[which, owner, 16 + 2 * plane : 18 + 2 * plane, :] = jnp.where(
            low, values[0:2, 256:], pltpu.roll(values[2:4, 256:], 64, 1)
        )

    def field_copy(which, step):
        peer = (coil + step) % COIL_PEERS
        return pltpu.make_async_remote_copy(
            src_ref=pieces.at[which, owner],
            dst_ref=pieces.at[which, owner],
            send_sem=field_send.at[which, peer],
            recv_sem=field_recv.at[which, owner],
            device_id={"coil": peer},
            device_id_type=MESH,
        )

    def field_start(which):
        @pl.loop(0, COIL_PEERS - 1)
        def _(step):
            field_copy(which, outward(step, COIL_PEERS // 2)).start()

    def field_wait(which):
        @pl.loop(0, OWNERS)
        def _(target):
            @pl.when(owner_coil(target, row) != coil)
            def _():
                pltpu.make_async_remote_copy(
                    src_ref=pieces.at[which, target],
                    dst_ref=pieces.at[which, target],
                    send_sem=field_send.at[which, 0],
                    recv_sem=field_recv.at[which, target],
                    device_id={"coil": owner_coil(target, row)},
                    device_id_type=MESH,
                ).wait_recv()

        for target in range(OWNERS):
            cut = slice(2 * target, 2 * target + 2)
            for plane in range(2):
                for part in range(2):
                    for half in range(2):
                        at = 8 * half + 4 * part + 2 * plane
                        fields[which, part, plane, cut, 128 * half : 128 * half + 128] = pieces[
                            which, target, at : at + 2, :
                        ]
                last = pieces[which, target, 16 + 2 * plane : 18 + 2 * plane, :]
                fields[which, 0, plane, cut, 256:] = last
                fields[which, 1, plane, cut, 256:] = pltpu.roll(last, 64, 1)

    pl.semaphore_wait(greet_far.at[0], 2 * REACH + 1)
    greet_coil(greet_far.at[1])
    swap_wait(0)
    total_field = gather_in(0)
    images[0] = total_field
    part_sums(0, total_field)
    pair_copy(0).start()
    swap_wait(1)
    total_field = gather_in(1)
    images[1] = total_field
    part_sums(1, total_field)
    pair_copy(1).start()
    pl.semaphore_wait(greet_far.at[1], 2 * REACH)
    part_start(0)
    part_start(1)

    @pl.when(owns)
    def _():
        shifted[...] = jnp.zeros_like(shifted)
        near[0, 1, slab] = part_total(0)
        near_start(0)
        near[1, 1, slab] = part_total(1)
        near_start(1)
        backs[0] = jnp.zeros((48, HALF), jnp.float32)
        backs[4] = jnp.zeros((48, HALF), jnp.float32)
        near_wait(0)
        for part in range(2):
            for side in range(2):
                for plane in range(2):
                    line = part * 4 + plane * 2
                    for step in range(3):
                        shifted[1, part, 1 + 2 * side + plane, 2 * step : 2 * step + 2, :] = near[
                            0, step, side, line : line + 2, :
                        ]
        middle = shifted[1].reshape(2 * 6 * 8, HALF)
        shifted[0] = pltpu.roll(middle, 1, 1).reshape(2, 6, 8, HALF)
        shifted[2] = pltpu.roll(middle, HALF - 1, 1).reshape(2, 6, 8, HALF)
        for plane in range(3):
            pre = dot3(
                forward_pair,
                shifted[:, :, pl.ds(slab + plane, 3)].reshape(144, HALF),
            )
            sigmoid = 1.0 / (1.0 + jnp.exp(-pre))
            acts[plane] = pre * sigmoid
            slopes[plane] = sigmoid * (1.0 + pre * (1.0 - sigmoid))
        for plane in range(2):
            put_piece(0, plane, dot3(last_pair, acts[slab + plane]))
        near_wait(1)
        for part in range(2):
            for side in range(2):
                for plane in range(2):
                    line = part * 4 + plane * 2
                    for again in (0, 4):
                        cot_rows[part, 2 * side + plane, again : again + 1, :] = near[
                            1, 0, side, line + 1 : line + 2, :
                        ]
                        cot_rows[part, 2 * side + plane, again + 1 : again + 3, :] = near[
                            1, 1, side, line : line + 2, :
                        ]
                        cot_rows[part, 2 * side + plane, again + 3 : again + 4, :] = near[
                            1, 2, side, line : line + 1, :
                        ]
        for plane in range(3):
            real = jnp.broadcast_to(cot_rows[0, slab + plane][None], (9, 8, HALF))
            imag = jnp.broadcast_to(cot_rows[1, slab + plane][None], (9, 8, HALF))
            spread_cot = last_columns[:, 0:1] * real.reshape(HID * 4, HALF) + last_columns[
                :, 1:2
            ] * imag.reshape(HID * 4, HALF)
            backs[plane + 1] = dot3(backward_pair, slopes[plane] * spread_cot)
        for plane in range(2):
            back = (
                backs[slab + plane, 0:16]
                + backs[slab + plane + 1, 16:32]
                + backs[slab + plane + 2, 32:48]
            )
            back = (
                pltpu.roll(back[0:4], HALF - 1, 1) + back[4:8] + pltpu.roll(back[8:12], 1, 1)
            )
            put_piece(1, plane, back)
        field_start(1)
        field_start(0)

    field_wait(1)
    for group in range(4):
        plane = group % 2
        other_real, other_imag = fields[1, 0, plane, :CELLS], fields[1, 1, plane, :CELLS]
        real, imag = maps[group, :CELLS, :HALF], maps[group, :CELLS, HALF:]
        put_rows(
            group,
            real * other_real - imag * other_imag,
            -(real * other_imag + imag * other_real),
        )
    spread_out(2)
    swap_start(2)
    stores = [
        Halves(grad_sens, grad_sens_hbm, store_sem, 0),
        Halves(grad_kspace, grad_kspace_hbm, store_sem, 1),
    ]
    field_wait(0)
    for group in range(4):
        plane = group % 2
        at = slice(24 * group, 24 * group + CELLS)
        out_real = out_imag = None
        for which in range(2):
            other_real, other_imag = fields[which, 0, plane, :CELLS], fields[which, 1, plane, :CELLS]
            real, imag = images[1 - which, at, :HALF], images[1 - which, at, HALF:]
            this_real = -(real * other_real + imag * other_imag)
            this_imag = real * other_imag - imag * other_real
            out_real = this_real if out_real is None else out_real + this_real
            out_imag = this_imag if out_imag is None else out_imag + this_imag
        grad_sens[group // 2, :, plane, :] = whole_lines(out_real, out_imag)
    stores[0].start()
    square_row = lax.broadcasted_iota(jnp.int32, (CELLS, CELLS), 0)
    square_column = lax.broadcasted_iota(jnp.int32, (CELLS, CELLS), 1)
    factors = []
    for plane in range(2):
        sampled = jnp.broadcast_to(mask[plane : plane + 1, :].astype(jnp.float32), (CELLS, CELLS))
        column = jnp.sum(
            jnp.where(square_row == square_column, sampled, 0.0), axis=1, keepdims=True
        )
        factors.append(1.0 - eta[0] * column)
    for which in range(2):
        swap_settle(which)
        pair_copy(which).wait_send()

        @pl.loop(0, SHARED)
        def _(number):
            @pl.when(owner_coil(2 * number + parity, row) != coil)
            def _():
                part_copy(which, number).wait_send()

        @pl.when(owns)
        def _():
            for step, across in near_by:
                copy, there = near_copy(which, step, across)
                pl.when(there)(copy.wait_send)

            @pl.loop(1, COIL_PEERS)
            def _(step):
                field_copy(which, step).wait_send()
    swap_wait(2)
    model = gather_in(2)
    for group in range(4):
        plane = group % 2
        mine = model[24 * group : 24 * group + CELLS]
        grad_kspace[group // 2, :, plane, :] = factors[plane] * cotangent[
            group // 2, :, plane, :
        ] - whole_lines(mine[:, :HALF], -mine[:, HALF:])
        if plane == 1:
            stores[1].copies[group // 2].start()

    swap_settle(2)
    stores[0].wait()
    stores[1].wait()


def hand_on(first, second, first_out, second_out, first_held, second_held, load_sem, store_sem):
    loads = [
        pltpu.make_async_copy(source.at[half], held.at[half], load_sem.at[number, half])
        for number, (source, held) in enumerate(((first, first_held), (second, second_held)))
        for half in range(2)
    ]
    stores = [
        pltpu.make_async_copy(held.at[half], target.at[half], store_sem.at[number, half])
        for number, (held, target) in enumerate(((first_held, first_out), (second_held, second_out)))
        for half in range(2)
    ]
    for load in loads:
        load.start()
    for load, store in zip(loads, stores):
        load.wait()
        store.start()
    for store in stores:
        store.wait()


def local(kspace, cotangent, sens, mask, eta, w_first, w_last):
    constants = [jnp.asarray(array) for array in tables() + selectors()]
    smem = pl.BlockSpec(memory_space=pltpu.SMEM)
    anywhere = pl.BlockSpec(memory_space=pl.ANY)
    f32, b16 = jnp.float32, jnp.bfloat16
    rows = jax.ShapeDtypeStruct((2, CELLS, 2, 2 * LEN), f32)
    results = pl.pallas_call(
        kernel,
        out_shape=(rows, rows),
        in_specs=[anywhere] * 4 + [smem] + [anywhere] * 13,
        out_specs=(anywhere, anywhere),
        scratch_shapes=[
            pltpu.VMEM(rows.shape, f32),
            pltpu.VMEM(rows.shape, f32),
            pltpu.VMEM(rows.shape, f32),
            pltpu.VMEM(mask.shape, jnp.int32),
            pltpu.VMEM((27, 2, HID), f32),
            pltpu.VMEM(w_last.shape, f32),
            *[pltpu.VMEM(array.shape, array.dtype) for array in constants],
            pltpu.VMEM(rows.shape, f32),
            pltpu.VMEM(rows.shape, f32),
            pltpu.VMEM((256, WIDE), f32),
            pltpu.VMEM((3, PEERS, SENT, 128), f32),
            pltpu.VMEM((3, PEERS, SENT, 128), f32),
            pltpu.VMEM((96, 2 * LEN), f32),
            pltpu.VMEM((2, 96, WIDE), f32),
            pltpu.VMEM((4, 24, WIDE), f32),
            pltpu.VMEM((2, OWNERS, 20, 128), f32),
            pltpu.VMEM((2, SHARED, 20, 128), f32),
            pltpu.VMEM((2, COIL_PEERS // 2, 20, 128), f32),
            pltpu.VMEM((2, 3, 2, 8, HALF), f32),
            pltpu.VMEM((3, 2, 6, 8, HALF), f32),
            pltpu.VMEM((2, 4, 8, HALF), f32),
            pltpu.VMEM((3, HID * 4, HALF), f32),
            pltpu.VMEM((3, HID * 4, HALF), f32),
            pltpu.VMEM((5, 48, HALF), f32),
            pltpu.VMEM((2, OWNERS, 20, 128), f32),
            pltpu.VMEM((2, 2, 2, 24, HALF), f32),
            pltpu.SemaphoreType.DMA((17, 2)),
            pltpu.SemaphoreType.DMA((2, 2)),
            pltpu.SemaphoreType.DMA((3, PEERS)),
            pltpu.SemaphoreType.DMA((3, PEERS)),
            pltpu.SemaphoreType.DMA((2,)),
            pltpu.SemaphoreType.DMA((2,)),
            pltpu.SemaphoreType.DMA((2, SHARED)),
            pltpu.SemaphoreType.DMA((2, COIL_PEERS // 2)),
            pltpu.SemaphoreType.DMA((2, 6)),
            pltpu.SemaphoreType.DMA((2, 6)),
            pltpu.SemaphoreType.DMA((2, COIL_PEERS)),
            pltpu.SemaphoreType.DMA((2, OWNERS)),
            pltpu.SemaphoreType.REGULAR((2,)),
        ],
        compiler_params=pltpu.CompilerParams(
            collective_id=0, has_side_effects=True, vmem_limit_bytes=62 * 1024 * 1024
        ),
    )(
        kspace.transpose(0, 2, 1, 3),
        cotangent.transpose(0, 2, 1, 3),
        sens.transpose(0, 2, 1, 3),
        mask,
        eta,
        w_first.transpose(2, 3, 4, 1, 0).reshape(27, 2, HID),
        w_last,
        *constants,
    )
    results = pl.pallas_call(
        hand_on,
        out_shape=(rows, rows),
        in_specs=[anywhere] * 2,
        out_specs=(anywhere, anywhere),
        scratch_shapes=[pltpu.VMEM(rows.shape, f32)] * 2 + [pltpu.SemaphoreType.DMA((2, 2))] * 2,
        compiler_params=pltpu.CompilerParams(vmem_limit_bytes=62 * 1024 * 1024),
    )(*results)
    return tuple(result.transpose(0, 2, 1, 3) for result in results)


def solution(mesh):
    part = P("coil", "slab", "row", None)
    return jax.shard_map(
        local,
        mesh=mesh,
        in_specs=(part, part, part, P("slab", "row"), P(), P(), P()),
        out_specs=(part, part),
        check_vma=False,
    )
```

```python
import math

import jax
import jax.numpy as jnp
import ml_dtypes
import numpy as np
from jax import lax
from jax.experimental import pallas as pl
from jax.experimental.pallas import tpu as pltpu
from jax.sharding import PartitionSpec as P

MESH = pl.DeviceIdType.MESH
LEN = 320
HALF = 384
WIDE = 2 * HALF
CELLS = 20
LONG = 16
PEERS = 16
COIL_PEERS = 16
SENT = 8 + CELLS
REACH = 3
OWNERS = 10
SHARED = OWNERS // 2
HID = 18


def outward(step, middle):
    return middle + (1 - 2 * (step % 2)) * ((step + 1) // 2)


def turned(owner, row):
    return owner + (row % 2) * (OWNERS - 1 - 2 * owner)


def owner_coil(owner, row):
    return (8 * turned(owner, row)) // 5


def coil_owner(coil, row):
    return turned((5 * coil + 7) // 8, row)


def split_table(table):
    high = table.astype(ml_dtypes.bfloat16)
    low = (table - high.astype(np.float64)).astype(ml_dtypes.bfloat16)
    return high, low


def tables():
    at = np.arange(LEN)
    angle = 2.0 * math.pi * ((at[:, None] * at[None, :]) % LEN) / LEN
    cosine, sine = np.cos(angle) / math.sqrt(LEN), np.sin(angle) / math.sqrt(LEN)
    first = np.zeros((PEERS, 24, 2, HALF))
    first[:, :CELLS, 0, :LEN] = cosine.reshape(PEERS, CELLS, LEN)
    first[:, :CELLS, 1, :LEN] = sine.reshape(PEERS, CELLS, LEN)
    line = np.arange(LEN).reshape(PEERS, CELLS)
    long, short = line[:, :LONG].reshape(-1), line[:, LONG:].reshape(-1)
    second = np.zeros((2 * LEN, 2, HALF))
    for part, rows in enumerate(((cosine, sine), (-sine, cosine))):
        for half in range(2):
            second[256 * part : 256 * part + 256, half, :LEN] = rows[half][long]
            second[512 + 64 * part : 576 + 64 * part, half, :LEN] = rows[half][short]
    return split_table(first.reshape(PEERS * 24, WIDE)) + split_table(
        second.reshape(2 * LEN, WIDE)
    )


def selectors():
    repeat = np.zeros((HID * 4, HID), np.float32)
    for unit in range(HID):
        repeat[4 * unit : 4 * unit + 4, unit] = 1.0
    pick = np.zeros((3, 54, 144), np.float32)
    place = np.zeros((3, HID * 4, 144), np.float32)
    for column in range(144):
        e3, channel, e1, row = column // 48, column // 24 % 2, column // 8 % 3, column % 8
        for e2 in range(3):
            pick[e2, 2 * (e1 * 9 + e2 * 3 + e3) + channel, column] = 1.0
            for line in range(HID * 4):
                if row - line % 4 == e2:
                    place[e2, line, column] = 1.0
    pick_back = np.zeros((3, 3, 16, 54), np.float32)
    place_back = np.zeros((3, 3, 16, HID * 4), np.float32)
    for e2 in range(3):
        for plane in range(3):
            for line in range(12):
                e3, channel, row = line // 4, line // 2 % 2, line % 2
                pick_back[e2, plane, line, 2 * ((2 - plane) * 9 + e2 * 3 + e3) + channel] = 1.0
                for column in range(HID * 4):
                    if row + 2 - column % 4 == e2:
                        place_back[e2, plane, line, column] = 1.0
    place_last = np.zeros((8, HID * 4), np.float32)
    pick_last = np.zeros((8, 2), np.float32)
    for line in range(4):
        pick_last[line, line // 2] = 1.0
        for column in range(HID * 4):
            if column % 4 == line % 2 + 1:
                place_last[line, column] = 1.0
    return (
        repeat,
        pick,
        place,
        pick_back.reshape(144, 54),
        place_back.reshape(144, HID * 4),
        place_last,
        pick_last,
    )


def unpack(packed):
    low = lax.broadcasted_iota(jnp.int32, (4, 128), 1) < LEN - 256
    last = packed[16:20]
    upper = jnp.where(low, last, 0.0)
    lower = jnp.where(low, pltpu.roll(last, 64, 1), 0.0)
    return jnp.concatenate(
        [packed[0:8], packed[8:16], jnp.concatenate([upper, lower], axis=0)], axis=1
    )


def split(values):
    high = values.astype(jnp.bfloat16)
    return high, (values - high.astype(jnp.float32)).astype(jnp.bfloat16)


def dot(left, right, dims=((1,), (0,))):
    return lax.dot_general(left, right, (dims, ((), ())), preferred_element_type=jnp.float32)


def pair(left):
    high = left.astype(jnp.bfloat16).astype(jnp.float32)
    both = jnp.concatenate([high, left - high], axis=0)
    return both.astype(jnp.bfloat16), high.astype(jnp.bfloat16)


def dot3(left_pair, right):
    both_left, left_high = left_pair
    rows = left_high.shape[0]
    right_high, right_low = split(right)
    both = dot(both_left, right_high)
    return both[:rows] + both[rows:] + dot(left_high, right_low)


def exchange(blocks, width, lane):
    blocks = list(blocks)
    step = 1
    while step < len(blocks):
        shift = width * step
        low = (lane & shift) == 0
        for first in range(len(blocks)):
            if first & step:
                continue
            upper, lower = blocks[first], blocks[first + step]
            blocks[first] = jnp.where(low, upper, pltpu.roll(lower, shift, 1))
            blocks[first + step] = jnp.where(low, pltpu.roll(upper, 128 - shift, 1), lower)
        step *= 2
    return blocks


def exact_dot(left, right, dims=((1,), (0,))):
    return lax.dot_general(
        left,
        right,
        (dims, ((), ())),
        precision=lax.Precision.HIGHEST,
        preferred_element_type=jnp.float32,
    )


class Halves:
    def __init__(self, source, target, sems, number):
        rows = source.shape[0] // 2
        self.copies = [
            pltpu.make_async_copy(
                source.at[pl.ds(half * rows, rows)],
                target.at[pl.ds(half * rows, rows)],
                sems.at[number, half],
            )
            for half in range(2)
        ]

    def start(self):
        for copy in self.copies:
            copy.start()

    def wait(self):
        for copy in self.copies:
            copy.wait()


def kernel(*refs):
    (
        kspace_hbm,
        cotangent_hbm,
        sens_hbm,
        mask_hbm,
        eta,
        w_first_hbm,
        w_last_hbm,
        *constants_hbm,
    ) = refs[:18]
    grad_kspace_hbm, grad_sens_hbm = refs[18:20]
    (
        kspace,
        cotangent,
        sens,
        mask,
        w_first,
        w_last,
        first_high,
        first_low,
        second_high,
        second_low,
        repeat,
        pick,
        place,
        pick_back,
        place_back,
        place_last,
        pick_last,
        grad_kspace,
        grad_sens,
        lines,
        spread,
        landed,
        wide,
        images,
        maps,
        parts,
        paired,
        sums,
        near,
        shifted,
        cot_rows,
        acts,
        slopes,
        backs,
        pieces,
        fields,
        load_sem,
        store_sem,
        swap_send,
        swap_recv,
        pair_send,
        pair_recv,
        sum_send,
        sum_recv,
        near_send,
        near_recv,
        field_send,
        field_recv,
        greet_far,
    ) = refs[20:]
    coil, slab, row = lax.axis_index("coil"), lax.axis_index("slab"), lax.axis_index("row")
    owner = coil_owner(coil, row)
    owns = owner_coil(owner, row) == coil

    def neighbour(step):
        other = owner + step
        other_row = row + jnp.where(other < 0, -1, 0) + jnp.where(other >= OWNERS, 1, 0)
        there = jnp.logical_and(other_row >= 0, other_row < PEERS)
        return owner_coil((other + OWNERS) % OWNERS, other_row), other_row, there

    near_by = [(-1, 1), (1, 1), (0, 1), (-1, 0), (1, 0)]

    sources = [kspace_hbm, *constants_hbm[:2], cotangent_hbm, sens_hbm, *constants_hbm[2:4]]
    targets = [kspace, first_high, first_low, cotangent, sens, second_high, second_low]
    sources += [w_first_hbm, w_last_hbm, mask_hbm, *constants_hbm[4:]]
    targets += [w_first, w_last, mask, repeat, pick, place, pick_back, place_back]
    targets += [place_last, pick_last]
    loads = []
    for number, (source, target) in enumerate(zip(sources, targets)):
        if number < 7:
            loads.append(Halves(source, target, load_sem, number))
        else:
            loads.append(pltpu.make_async_copy(source, target, load_sem.at[number, 0]))
    near[...] = jnp.zeros_like(near)

    barrier = pltpu.get_barrier_semaphore()

    def greet_coil(sem):
        for step in range(REACH, 0, -1):
            for sign in (1, -1):
                pl.semaphore_signal(
                    sem,
                    inc=1,
                    device_id={"coil": (coil + sign * step) % COIL_PEERS},
                    device_id_type=MESH,
                )

    def greet_slab(sem):
        pl.semaphore_signal(sem, inc=1, device_id={"slab": 1 - slab}, device_id_type=MESH)

    @pl.loop(1, PEERS)
    def _(step):
        pl.semaphore_signal(
            barrier, inc=1, device_id={"row": (row + step) % PEERS}, device_id_type=MESH
        )

    greet_coil(barrier)
    greet_slab(barrier)

    for load in loads[:4]:
        load.start()

    lane = lax.broadcasted_iota(jnp.int32, (CELLS, 128), 1)

    def put_rows(group, real, imag):
        for part, (first, second) in enumerate(((real, -imag), (imag, real))):
            at = 64 * part + LONG * group
            lines[at : at + LONG, :HALF] = first[:LONG]
            lines[at : at + LONG, HALF:] = second[:LONG]
            at = 128 + 16 * part + 4 * group
            lines[at : at + 4, :HALF] = first[LONG:]
            lines[at : at + 4, HALF:] = second[LONG:]

    def spread_out(which):
        high, low = split(lines[...])
        right = jnp.concatenate([high[:128], low[:128], high[128:192], low[128:192]], axis=0)
        both = dot(first_high[...], right, ((1,), (1,)))
        rest = dot(first_low[...], high, ((1,), (1,)))
        long = both[:, :128] + both[:, 128:256] + rest[:, :128]
        short = both[:, 256:] + pltpu.roll(both[:, 256:], 64, 1) + rest[:, 128:]
        folds = short.reshape(PEERS, 3, 8, 128)
        second = pltpu.roll(folds[:, 1].reshape(PEERS * 8, 128), 32, 1)
        third = pltpu.roll(folds[:, 2].reshape(PEERS * 8, 128), 64, 1)
        at = lax.broadcasted_iota(jnp.int32, (PEERS * 8, 128), 1)
        fold = jnp.where(
            at < 32,
            folds[:, 0].reshape(PEERS * 8, 128),
            jnp.where(at < 64, second, jnp.where(at < 96, third, 0.0)),
        )
        spread[which, :, 0:8, :] = fold.reshape(PEERS, 8, 128)
        spread[which, :, 8:SENT, :] = long.reshape(PEERS, 24, 128)[:, :CELLS]

    def swap(which, peer):
        return pltpu.make_async_remote_copy(
            src_ref=spread.at[which, peer],
            dst_ref=landed.at[which, row],
            send_sem=swap_send.at[which, peer],
            recv_sem=swap_recv.at[which, row],
            device_id={"row": peer},
            device_id_type=MESH,
        )

    def swap_start(which):
        for across, along in ((1, 2), (0, 2), (1, 1), (1, 3), (1, 0), (0, 1), (0, 3), (0, 0)):
            for core in range(2):
                if (across, along, core) != (0, 0, 0):
                    pair = row // 2
                    peer = (
                        (pair // 4 + across) % 2 * 8 + (pair + along) % 4 * 2 + (row + core) % 2
                    )
                    swap(which, peer).start()

        landed[which, row] = spread[which, row]

    def swap_wait(which):
        @pl.loop(1, PEERS)
        def _(step):
            peer = (row + step) % PEERS
            pltpu.make_async_remote_copy(
                src_ref=spread.at[which, peer],
                dst_ref=landed.at[which, peer],
                send_sem=swap_send.at[which, peer],
                recv_sem=swap_recv.at[which, peer],
                device_id={"row": peer},
                device_id_type=MESH,
            ).wait_recv()

    def swap_settle(which):
        @pl.loop(1, PEERS)
        def _(step):
            swap(which, (row + step) % PEERS).wait_send()

    def gather_in(which):
        for half in range(2):
            blocks = [landed[which, 8 * half + peer, 8:SENT, :] for peer in range(8)]
            for unit, block in enumerate(exchange(blocks, LONG, lane)):
                part, group = unit // 4, unit % 4
                start = 256 * part + 128 * half
                wide[24 * group : 24 * group + CELLS, start : start + 128] = block
        blocks = exchange([landed[which, peer, 0:8, :] for peer in range(PEERS)], 4, lane[:8])
        low = lane[:8] < 64
        for group in range(4):
            folds = (
                jnp.where(low, blocks[group], pltpu.roll(blocks[4 + group], 64, 1)),
                jnp.where(low, blocks[8 + group], pltpu.roll(blocks[12 + group], 64, 1)),
                jnp.where(low, pltpu.roll(blocks[group], 64, 1), blocks[4 + group]),
            )
            for number, fold in enumerate(folds):
                at = 24 * group + 8 * number
                wide[at : at + 8, 512:] = fold
        high, low = split(wide[...])
        both = dot(jnp.concatenate([high, low], axis=0), second_high[...])
        return both[:96] + both[96:] + dot(high, second_low[...])

    def halves(ref, group):
        lines_now = ref[group // 2, :, group % 2, :]
        tiles = [lines_now[:, 128 * tile : 128 * tile + 128] for tile in range(5)]
        low = lane < 64
        turned = [pltpu.roll(tile, 64, 1) for tile in tiles[2:]]
        zero = jnp.zeros_like(tiles[0])
        return (
            tiles[:2] + [jnp.where(low, tiles[2], zero)],
            [
                jnp.where(low, turned[0], turned[1]),
                jnp.where(low, turned[1], turned[2]),
                jnp.where(low, turned[2], zero),
            ],
        )

    def whole_lines(real, imag):
        low = lane < 64
        turned = [pltpu.roll(imag[:, 128 * tile : 128 * tile + 128], 64, 1) for tile in range(3)]
        tiles = [
            real[:, :128],
            real[:, 128:256],
            jnp.where(low, real[:, 256:], turned[0]),
            jnp.where(low, turned[0], turned[1]),
            jnp.where(low, turned[1], turned[2]),
        ]
        return jnp.concatenate(tiles, axis=1)

    def put_lines(ref):
        for group in range(4):
            real, imag = halves(ref, group)
            put_rows(group, jnp.concatenate(real, axis=1), jnp.concatenate(imag, axis=1))

    lines[...] = jnp.zeros_like(lines)
    loads[0].wait()
    put_lines(kspace)
    loads[1].wait()
    loads[2].wait()
    for load in loads[4:]:
        load.start()
    spread_out(0)

    pl.semaphore_wait(barrier, PEERS - 1 + 2 * REACH + 1)
    swap_start(0)
    greet_coil(greet_far.at[0])
    greet_slab(greet_far.at[0])
    loads[3].wait()
    put_lines(cotangent)
    spread_out(1)
    swap_start(1)

    wide[...] = jnp.zeros_like(wide)
    maps[...] = jnp.zeros_like(maps)
    loads[4].wait()
    for group in range(4):
        for half, tiles in enumerate(halves(sens, group)):
            for number, tile in enumerate(tiles):
                start = half * HALF + 128 * number
                maps[group, :CELLS, start : start + 128] = tile
    for load in loads[5:]:
        load.wait()
    weights = w_first[...].reshape(54, HID)
    weights_rows = exact_dot(repeat[...], weights, ((1,), (1,)))
    forward_matrix = jnp.zeros((HID * 4, 144), jnp.float32)
    for e2 in range(3):
        forward_matrix += place[e2] * exact_dot(weights_rows, pick[e2])
    weights_back = exact_dot(weights, repeat[...], ((1,), (1,)))
    backward_matrix = jnp.sum(
        (exact_dot(pick_back[...], weights_back) * place_back[...]).reshape(3, 48, HID * 4), axis=0
    )
    last_columns = exact_dot(repeat[...], w_last[...], ((1,), (1,)))
    last_matrix = place_last[...] * exact_dot(
        pick_last[...], exact_dot(w_last[...], repeat[...], ((1,), (1,)))
    )
    forward_pair, backward_pair, last_pair = map(
        pair, (forward_matrix, backward_matrix, last_matrix)
    )

    def part_sums(which, total_field):
        for plane in range(2):
            real = imag = None
            for local_coil in range(2):
                group = local_coil * 2 + plane
                map_real, map_imag = maps[group, :, :HALF], maps[group, :, HALF:]
                field = total_field[24 * group : 24 * group + 24]
                field_real, field_imag = field[:, :HALF], field[:, HALF:]
                this_real = map_real * field_real + map_imag * field_imag
                this_imag = map_real * field_imag - map_imag * field_real
                real = this_real if real is None else real + this_real
                imag = this_imag if imag is None else imag + this_imag
            last = real[:, 256:] + pltpu.roll(imag[:, 256:], 64, 1)
            for target in range(OWNERS):
                cut = slice(2 * target, 2 * target + 2)
                at_piece = target % 2 * SHARED + target // 2
                for half in range(2):
                    lanes = slice(128 * half, 128 * half + 128)
                    at = 8 * half + 2 * plane
                    parts[which, at_piece, at : at + 2, :] = real[cut, lanes]
                    parts[which, at_piece, at + 4 : at + 6, :] = imag[cut, lanes]
                parts[which, at_piece, 16 + 2 * plane : 18 + 2 * plane, :] = last[cut]

    place_now = (coil + row % 2) % COIL_PEERS
    parity = place_now % 2

    def piece_of(target):
        return target % 2 * SHARED + target // 2

    def pair_copy(which):
        return pltpu.make_async_remote_copy(
            src_ref=parts.at[which, pl.ds((1 - parity) * SHARED, SHARED)],
            dst_ref=paired.at[which],
            send_sem=pair_send.at[which],
            recv_sem=pair_recv.at[which],
            device_id={"coil": (coil + 1 - 2 * parity) % COIL_PEERS},
            device_id_type=MESH,
        )

    def part_copy(which, number):
        return pltpu.make_async_remote_copy(
            src_ref=parts.at[which, parity * SHARED + number],
            dst_ref=sums.at[which, place_now // 2],
            send_sem=sum_send.at[which, number],
            recv_sem=sum_recv.at[which, place_now // 2],
            device_id={"coil": owner_coil(2 * number + parity, row)},
            device_id_type=MESH,
        )

    def part_start(which):
        pair_copy(which).wait_recv()
        mine = pl.ds(parity * SHARED, SHARED)
        parts[which, mine] = parts[which, mine] + paired[which]

        @pl.loop(0, SHARED)
        def _(step):
            number = (owner // 2 + outward(step, SHARED // 2)) % SHARED

            @pl.when(owner_coil(2 * number + parity, row) != coil)
            def _():
                part_copy(which, number).start()

    def part_total(which):
        @pl.loop(0, COIL_PEERS // 2)
        def _(number):
            peer = (2 * number + owner % 2 + COIL_PEERS - row % 2) % COIL_PEERS

            @pl.when(peer != coil)
            def _():
                pltpu.make_async_remote_copy(
                    src_ref=parts.at[which, 0],
                    dst_ref=sums.at[which, number],
                    send_sem=sum_send.at[which, 0],
                    recv_sem=sum_recv.at[which, number],
                    device_id={"coil": peer},
                    device_id_type=MESH,
                ).wait_recv()

        @pl.when(owner % 2 == parity)
        def _():
            sums[which, place_now // 2] = parts[which, piece_of(owner)]

        total = sums[which, 0]
        for number in range(1, COIL_PEERS // 2):
            total = total + sums[which, number]
        return unpack(total)

    def near_copy(which, step, across):
        other_coil, other_row, there = neighbour(step)
        copy = pltpu.make_async_remote_copy(
            src_ref=near.at[which, 1, slab],
            dst_ref=near.at[which, 1 - step, slab],
            send_sem=near_send.at[which, (step + 1) * 2 + across],
            recv_sem=near_recv.at[which, (1 - step) * 2 + across],
            device_id={"coil": other_coil, "slab": (slab + across) % 2, "row": other_row},
            device_id_type=MESH,
        )
        return copy, there

    def near_start(which):
        for step, across in near_by:
            copy, there = near_copy(which, step, across)
            pl.when(there)(copy.start)

    def near_wait(which):
        for step, across in near_by:
            other_coil, other_row, there = neighbour(step)
            copy = pltpu.make_async_remote_copy(
                src_ref=near.at[which, 1, slab],
                dst_ref=near.at[which, 1 + step, (slab + across) % 2],
                send_sem=near_send.at[which, (step + 1) * 2 + across],
                recv_sem=near_recv.at[which, (1 + step) * 2 + across],
                device_id={"coil": other_coil, "slab": (slab + across) % 2, "row": other_row},
                device_id_type=MESH,
            )
            pl.when(there)(copy.wait_recv)

    def put_piece(which, plane, values):
        for half in range(2):
            lanes = slice(128 * half, 128 * half + 128)
            at = 8 * half + 2 * plane
            pieces[which, owner, at : at + 2, :] = values[0:2, lanes]
            pieces[which, owner, at + 4 : at + 6, :] = values[2:4, lanes]
        low = lax.broadcasted_iota(jnp.int32, (2, 128), 1) < LEN - 256
        pieces[which, owner, 16 + 2 * plane : 18 + 2 * plane, :] = jnp.where(
            low, values[0:2, 256:], pltpu.roll(values[2:4, 256:], 64, 1)
        )

    def field_copy(which, step):
        peer = (coil + step) % COIL_PEERS
        return pltpu.make_async_remote_copy(
            src_ref=pieces.at[which, owner],
            dst_ref=pieces.at[which, owner],
            send_sem=field_send.at[which, peer],
            recv_sem=field_recv.at[which, owner],
            device_id={"coil": peer},
            device_id_type=MESH,
        )

    def field_start(which):
        @pl.loop(0, COIL_PEERS - 1)
        def _(step):
            field_copy(which, outward(step, COIL_PEERS // 2)).start()

    def field_wait(which):
        @pl.loop(0, OWNERS)
        def _(target):
            @pl.when(owner_coil(target, row) != coil)
            def _():
                pltpu.make_async_remote_copy(
                    src_ref=pieces.at[which, target],
                    dst_ref=pieces.at[which, target],
                    send_sem=field_send.at[which, 0],
                    recv_sem=field_recv.at[which, target],
                    device_id={"coil": owner_coil(target, row)},
                    device_id_type=MESH,
                ).wait_recv()

        for target in range(OWNERS):
            cut = slice(2 * target, 2 * target + 2)
            for plane in range(2):
                for part in range(2):
                    for half in range(2):
                        at = 8 * half + 4 * part + 2 * plane
                        fields[which, part, plane, cut, 128 * half : 128 * half + 128] = pieces[
                            which, target, at : at + 2, :
                        ]
                last = pieces[which, target, 16 + 2 * plane : 18 + 2 * plane, :]
                fields[which, 0, plane, cut, 256:] = last
                fields[which, 1, plane, cut, 256:] = pltpu.roll(last, 64, 1)

    pl.semaphore_wait(greet_far.at[0], 2 * REACH + 1)
    greet_coil(greet_far.at[1])
    swap_wait(0)
    total_field = gather_in(0)
    images[0] = total_field
    part_sums(0, total_field)
    pair_copy(0).start()
    swap_wait(1)
    total_field = gather_in(1)
    images[1] = total_field
    part_sums(1, total_field)
    pair_copy(1).start()
    pl.semaphore_wait(greet_far.at[1], 2 * REACH)
    part_start(0)
    part_start(1)

    @pl.when(owns)
    def _():
        shifted[...] = jnp.zeros_like(shifted)
        near[0, 1, slab] = part_total(0)
        near_start(0)
        near[1, 1, slab] = part_total(1)
        near_start(1)
        backs[0] = jnp.zeros((48, HALF), jnp.float32)
        backs[4] = jnp.zeros((48, HALF), jnp.float32)
        near_wait(0)
        for part in range(2):
            for side in range(2):
                for plane in range(2):
                    line = part * 4 + plane * 2
                    for step in range(3):
                        shifted[1, part, 1 + 2 * side + plane, 2 * step : 2 * step + 2, :] = near[
                            0, step, side, line : line + 2, :
                        ]
        middle = shifted[1].reshape(2 * 6 * 8, HALF)
        shifted[0] = pltpu.roll(middle, 1, 1).reshape(2, 6, 8, HALF)
        shifted[2] = pltpu.roll(middle, HALF - 1, 1).reshape(2, 6, 8, HALF)
        for plane in range(3):
            pre = dot3(
                forward_pair,
                shifted[:, :, pl.ds(slab + plane, 3)].reshape(144, HALF),
            )
            sigmoid = 1.0 / (1.0 + jnp.exp(-pre))
            acts[plane] = pre * sigmoid
            slopes[plane] = sigmoid * (1.0 + pre * (1.0 - sigmoid))
        for plane in range(2):
            put_piece(0, plane, dot3(last_pair, acts[slab + plane]))
        near_wait(1)
        for part in range(2):
            for side in range(2):
                for plane in range(2):
                    line = part * 4 + plane * 2
                    for again in (0, 4):
                        cot_rows[part, 2 * side + plane, again : again + 1, :] = near[
                            1, 0, side, line + 1 : line + 2, :
                        ]
                        cot_rows[part, 2 * side + plane, again + 1 : again + 3, :] = near[
                            1, 1, side, line : line + 2, :
                        ]
                        cot_rows[part, 2 * side + plane, again + 3 : again + 4, :] = near[
                            1, 2, side, line : line + 1, :
                        ]
        gradients = []
        for plane in range(3):
            real = jnp.broadcast_to(cot_rows[0, slab + plane][None], (9, 8, HALF))
            imag = jnp.broadcast_to(cot_rows[1, slab + plane][None], (9, 8, HALF))
            spread_cot = last_columns[:, 0:1] * real.reshape(HID * 4, HALF) + last_columns[
                :, 1:2
            ] * imag.reshape(HID * 4, HALF)
            gradients.append(slopes[plane] * spread_cot)
        spread_back = dot3(backward_pair, jnp.concatenate(gradients, axis=1))
        for plane in range(3):
            backs[plane + 1] = spread_back[:, HALF * plane : HALF * plane + HALF]
        for plane in range(2):
            back = (
                backs[slab + plane, 0:16]
                + backs[slab + plane + 1, 16:32]
                + backs[slab + plane + 2, 32:48]
            )
            back = (
                pltpu.roll(back[0:4], HALF - 1, 1) + back[4:8] + pltpu.roll(back[8:12], 1, 1)
            )
            put_piece(1, plane, back)
        field_start(1)
        field_start(0)

    field_wait(1)
    for group in range(4):
        plane = group % 2
        other_real, other_imag = fields[1, 0, plane, :CELLS], fields[1, 1, plane, :CELLS]
        real, imag = maps[group, :CELLS, :HALF], maps[group, :CELLS, HALF:]
        put_rows(
            group,
            real * other_real - imag * other_imag,
            -(real * other_imag + imag * other_real),
        )
    spread_out(2)
    swap_start(2)
    stores = [
        Halves(grad_sens, grad_sens_hbm, store_sem, 0),
        Halves(grad_kspace, grad_kspace_hbm, store_sem, 1),
    ]
    field_wait(0)
    for group in range(4):
        plane = group % 2
        at = slice(24 * group, 24 * group + CELLS)
        out_real = out_imag = None
        for which in range(2):
            other_real, other_imag = fields[which, 0, plane, :CELLS], fields[which, 1, plane, :CELLS]
            real, imag = images[1 - which, at, :HALF], images[1 - which, at, HALF:]
            this_real = -(real * other_real + imag * other_imag)
            this_imag = real * other_imag - imag * other_real
            out_real = this_real if out_real is None else out_real + this_real
            out_imag = this_imag if out_imag is None else out_imag + this_imag
        grad_sens[group // 2, :, plane, :] = whole_lines(out_real, out_imag)
    stores[0].start()
    square_row = lax.broadcasted_iota(jnp.int32, (CELLS, CELLS), 0)
    square_column = lax.broadcasted_iota(jnp.int32, (CELLS, CELLS), 1)
    factors = []
    for plane in range(2):
        sampled = jnp.broadcast_to(mask[plane : plane + 1, :].astype(jnp.float32), (CELLS, CELLS))
        column = jnp.sum(
            jnp.where(square_row == square_column, sampled, 0.0), axis=1, keepdims=True
        )
        factors.append(1.0 - eta[0] * column)
    for which in range(2):
        swap_settle(which)
        pair_copy(which).wait_send()

        @pl.loop(0, SHARED)
        def _(number):
            @pl.when(owner_coil(2 * number + parity, row) != coil)
            def _():
                part_copy(which, number).wait_send()

        @pl.when(owns)
        def _():
            for step, across in near_by:
                copy, there = near_copy(which, step, across)
                pl.when(there)(copy.wait_send)

            @pl.loop(1, COIL_PEERS)
            def _(step):
                field_copy(which, step).wait_send()
    swap_wait(2)
    model = gather_in(2)
    for group in range(4):
        plane = group % 2
        mine = model[24 * group : 24 * group + CELLS]
        grad_kspace[group // 2, :, plane, :] = factors[plane] * cotangent[
            group // 2, :, plane, :
        ] - whole_lines(mine[:, :HALF], -mine[:, HALF:])
        if plane == 1:
            stores[1].copies[group // 2].start()

    swap_settle(2)
    stores[0].wait()
    stores[1].wait()


def hand_on(first, second, first_out, second_out, first_held, second_held, load_sem, store_sem):
    loads = [
        pltpu.make_async_copy(source.at[half], held.at[half], load_sem.at[number, half])
        for number, (source, held) in enumerate(((first, first_held), (second, second_held)))
        for half in range(2)
    ]
    stores = [
        pltpu.make_async_copy(held.at[half], target.at[half], store_sem.at[number, half])
        for number, (held, target) in enumerate(((first_held, first_out), (second_held, second_out)))
        for half in range(2)
    ]
    for load in loads:
        load.start()
    for load, store in zip(loads, stores):
        load.wait()
        store.start()
    for store in stores:
        store.wait()


def local(kspace, cotangent, sens, mask, eta, w_first, w_last):
    constants = [jnp.asarray(array) for array in tables() + selectors()]
    smem = pl.BlockSpec(memory_space=pltpu.SMEM)
    anywhere = pl.BlockSpec(memory_space=pl.ANY)
    f32, b16 = jnp.float32, jnp.bfloat16
    rows = jax.ShapeDtypeStruct((2, CELLS, 2, 2 * LEN), f32)
    results = pl.pallas_call(
        kernel,
        out_shape=(rows, rows),
        in_specs=[anywhere] * 4 + [smem] + [anywhere] * 13,
        out_specs=(anywhere, anywhere),
        scratch_shapes=[
            pltpu.VMEM(rows.shape, f32),
            pltpu.VMEM(rows.shape, f32),
            pltpu.VMEM(rows.shape, f32),
            pltpu.VMEM(mask.shape, jnp.int32),
            pltpu.VMEM((27, 2, HID), f32),
            pltpu.VMEM(w_last.shape, f32),
            *[pltpu.VMEM(array.shape, array.dtype) for array in constants],
            pltpu.VMEM(rows.shape, f32),
            pltpu.VMEM(rows.shape, f32),
            pltpu.VMEM((256, WIDE), f32),
            pltpu.VMEM((3, PEERS, SENT, 128), f32),
            pltpu.VMEM((3, PEERS, SENT, 128), f32),
            pltpu.VMEM((96, 2 * LEN), f32),
            pltpu.VMEM((2, 96, WIDE), f32),
            pltpu.VMEM((4, 24, WIDE), f32),
            pltpu.VMEM((2, OWNERS, 20, 128), f32),
            pltpu.VMEM((2, SHARED, 20, 128), f32),
            pltpu.VMEM((2, COIL_PEERS // 2, 20, 128), f32),
            pltpu.VMEM((2, 3, 2, 8, HALF), f32),
            pltpu.VMEM((3, 2, 6, 8, HALF), f32),
            pltpu.VMEM((2, 4, 8, HALF), f32),
            pltpu.VMEM((3, HID * 4, HALF), f32),
            pltpu.VMEM((3, HID * 4, HALF), f32),
            pltpu.VMEM((5, 48, HALF), f32),
            pltpu.VMEM((2, OWNERS, 20, 128), f32),
            pltpu.VMEM((2, 2, 2, 24, HALF), f32),
            pltpu.SemaphoreType.DMA((17, 2)),
            pltpu.SemaphoreType.DMA((2, 2)),
            pltpu.SemaphoreType.DMA((3, PEERS)),
            pltpu.SemaphoreType.DMA((3, PEERS)),
            pltpu.SemaphoreType.DMA((2,)),
            pltpu.SemaphoreType.DMA((2,)),
            pltpu.SemaphoreType.DMA((2, SHARED)),
            pltpu.SemaphoreType.DMA((2, COIL_PEERS // 2)),
            pltpu.SemaphoreType.DMA((2, 6)),
            pltpu.SemaphoreType.DMA((2, 6)),
            pltpu.SemaphoreType.DMA((2, COIL_PEERS)),
            pltpu.SemaphoreType.DMA((2, OWNERS)),
            pltpu.SemaphoreType.REGULAR((2,)),
        ],
        compiler_params=pltpu.CompilerParams(
            collective_id=0, has_side_effects=True, vmem_limit_bytes=62 * 1024 * 1024
        ),
    )(
        kspace.transpose(0, 2, 1, 3),
        cotangent.transpose(0, 2, 1, 3),
        sens.transpose(0, 2, 1, 3),
        mask,
        eta,
        w_first.transpose(2, 3, 4, 1, 0).reshape(27, 2, HID),
        w_last,
        *constants,
    )
    results = pl.pallas_call(
        hand_on,
        out_shape=(rows, rows),
        in_specs=[anywhere] * 2,
        out_specs=(anywhere, anywhere),
        scratch_shapes=[pltpu.VMEM(rows.shape, f32)] * 2 + [pltpu.SemaphoreType.DMA((2, 2))] * 2,
        compiler_params=pltpu.CompilerParams(vmem_limit_bytes=62 * 1024 * 1024),
    )(*results)
    return tuple(result.transpose(0, 2, 1, 3) for result in results)


def solution(mesh):
    part = P("coil", "slab", "row", None)
    return jax.shard_map(
        local,
        mesh=mesh,
        in_specs=(part, part, part, P("slab", "row"), P(), P(), P()),
        out_specs=(part, part),
        check_vma=False,
    )
```
